256 devices in a mesh: dp: 8 (over y, core), table: 32 (over x, z).
Axes of the slice: x: 4, y: 4, z: 8, core: 2. Of those that a mesh axis runs over, the one named last changes fastest.
Arguments:
- embed_table: bfloat16 [65536, 512], P('table'), may hold values from -6 to 6
- owner_shard: int32 [2048, 64, 2, 1], P(('dp', 'table')), may hold values from 0 to 31; in each aligned block of 128 rows (0 to 127, 128 to 255, ..., all dimensions but the last counted through in order) at most 8 rows name the same one
- slot_row: int32 [2048, 64, 2], P(('dp', 'table')), may hold values from 0 to 2047
- lengths: int32 [2048], P(('dp', 'table')), may hold values from 1 to 64, as said below
- send_order: int32 [256, 8], P(('dp', 'table')), may hold values from 0 to 7, each once within a row
- proj_weight: bfloat16 [1024, 3072], replicated, may hold values from -0.1875 to 0.1875
- out_weight: bfloat16 [1024, 1024], replicated, may hold values from -0.1875 to 0.1875
- upstream: bfloat16 [2048, 64, 1024], P(('dp', 'table')), may hold values from -6 to 6
Outputs:
- table_grad: bfloat16 [65536, 512], P('table', 'dp')
- proj_grad: bfloat16 [1024, 3072], P('table', 'dp')
- out_grad: bfloat16 [1024, 1024], P('table', 'dp')
The draws below stay inside these ranges and needn't reach their ends.
Inputs may be any that keep to these rules, and one draw needn't show every extreme that they name: `owner_shard`: within the 128 lookups of one history no owner shard is named more than 8 times. `lengths`: every device has at least one history of all 64 positions. `send_order`: each row is a permutation.
All inputs are finite; a program needn't handle non-finite values.
Results may differ from the reference program's by a relative error of at most 0.029.
Values may be sent and summed in bfloat16 or wider, within the bound.
A program may use at most 128 MiB of HBM per device.

```python
import math
import jax
import jax.numpy as jnp
import numpy as np
from jax import lax

D = 1024
EMB = 512
HEADS = 8
QK = 64
PROJ = 3072
SEQ = 64
HIST_DEV = 8
ROWS_DEV = 2048
MOST = 8
HISTS = 2048
ROWS = 65536
N_DP = 8
N_TABLE = 32


def draw_lengths(key, part):
    key = jax.random.fold_in(key, 11)
    first_key, second_key = jax.random.split(key)
    device_count = HISTS // HIST_DEV
    base = jax.random.randint(first_key, (device_count, HIST_DEV), 1, SEQ + 1)
    full_slot = jax.random.randint(second_key, (device_count, 1), 0, HIST_DEV)
    chosen = jnp.arange(HIST_DEV)[None, :] == full_slot
    return jnp.where(chosen, SEQ, base).reshape(HISTS).astype(jnp.int32)


def set_ends(result, own_key, least, largest):
    place = [jax.random.randint(jax.random.fold_in(own_key, axis), (), 0, length) for axis, length in enumerate(result.shape)]
    longest = result.shape.index(max(result.shape))
    beside = place[:longest] + [(place[longest] + 1) % result.shape[longest]] + place[longest + 1:]
    return result.at[tuple(place)].set(least).at[tuple(beside)].set(largest)


def shard_levels(own_key, shape, cuts, smallest, high):
    loudness = 1.0
    for axis_at, shards_of in cuts:
        steps = jax.random.uniform(jax.random.fold_in(jax.random.fold_in(own_key, 6), axis_at), (shards_of,), jnp.float32, smallest / len(cuts), high / len(cuts))
        loudness = loudness * jnp.repeat(jnp.exp(steps), shape[axis_at] // shards_of).reshape((-1,) + (1,) * (len(shape) - 1 - axis_at))
    return loudness


def routed_block(own_key, own, number, rows, number_of, top, bound, skew):
    sequence = jax.random.permutation(own_key, number_of)
    heavy_load, ordinary = portions_of(number_of, rows * top, bound, skew, True), portions_of(number_of, rows * top, bound, skew, False)
    places = jnp.arange(number_of)

    def named(sizes, offset_by):
        used = int((sizes > 0).sum())
        fixed = max(1, used // 4)
        passed = fixed + (places - fixed + offset_by * (used - fixed)) % max(1, number_of - fixed)
        return jnp.zeros((number_of,), jnp.int32).at[sequence[jnp.where(places < fixed, places, passed)]].set(jnp.asarray(sizes, jnp.int32))

    sizes = jnp.where(number % 4 == 0, named(heavy_load, number // 4), named(ordinary, number - number // 4 - 1))
    mixed = jax.random.permutation(jax.random.fold_in(own, 3), number_of)
    donor, taker = mixed[0:number_of // 2 * 2:2], mixed[1:number_of // 2 * 2:2]
    margin = jnp.minimum(sizes[donor] - 1, bound - sizes[taker]) // 2
    margin = jnp.where((donor == sequence[0]) | (taker == sequence[0]) | (sizes[taker] == 0), 0, jnp.maximum(margin, 0))
    passed = jax.random.randint(jax.random.fold_in(own, 4), (number_of // 2,), 0, 1 << 20) % (margin + 1)
    sizes = sizes.at[donor].add(-passed).at[taker].add(passed)
    members = jnp.searchsorted(jnp.cumsum(sizes), jnp.arange(rows * top), side="right").astype(jnp.int32)
    listing = members.reshape(top, rows).T
    listing = listing[jax.random.permutation(jax.random.fold_in(own, 1), rows)]
    offset_by = jax.random.randint(jax.random.fold_in(own, 2), (rows, 1), 0, top)
    return jnp.take_along_axis(listing, (jnp.arange(top)[None, :] + offset_by) % top, axis=1)


def portions_of(count, total, most, skew, full):
    weights = [(1 << 20) // math.isqrt(standing ** skew) + 1 for standing in range(1, count + 1)]
    largest = most if full else min(most, max(-(-total // count), total * weights[0] // sum(weights)))
    least = 1 if total - largest >= count - 1 else 0
    counts, spare = [largest] + [least] * (count - 1), total - largest - least * (count - 1)
    while spare > 0:
        candidates = [i for i in range(1, count) if counts[i] < largest] or [i for i in range(1, count) if counts[i] < most]
        whole, left = sum([weights[i] for i in candidates]), spare
        for i in candidates:
            addition = min(most - counts[i], max(1, left * weights[i] // whole), spare)
            counts[i] = counts[i] + addition
            spare = spare - addition
    return np.array(counts)


def noise(key, extent, scale, most, shards=(), dtype=jnp.bfloat16):
    level = shard_levels(key, extent, shards, -0.22, 0.18) if shards else 1.0
    result = jax.random.normal(key, extent, jnp.float32) * scale * level
    return jnp.minimum(jnp.maximum(result, -most), most).astype(dtype)


def setup_inputs(seed: int = 0) -> dict:
    seeds = jax.random.split(jax.random.key(seed), 9)
    embed_table = noise(seeds[0], (ROWS, EMB), 1.0, 6.0, ((0, 32),))
    owner_shard_keys = jax.random.split(jax.random.fold_in(seeds[1], 1), HISTS * SEQ * 2 // (2 * SEQ))
    owner_shard_turns = jax.random.permutation(jax.random.fold_in(seeds[1], 3), HISTS * SEQ * 2 // (2 * SEQ))
    owner_shard = jax.vmap(lambda own, number: routed_block(jax.random.fold_in(seeds[1], 2), own, number, 2 * SEQ, N_TABLE, 1, MOST, 2))(owner_shard_keys, owner_shard_turns).reshape((HISTS, SEQ, 2, 1))
    slot_row = set_ends(jax.random.randint(seeds[2], (HISTS, SEQ, 2), 0, ROWS_DEV), jax.random.fold_in(seeds[2], 1), 0, ROWS_DEV - 1).astype(jnp.int32)
    lengths = draw_lengths(jax.random.fold_in(seeds[8], 71), 0)
    send_order = jax.vmap(lambda own: jax.random.permutation(own, HIST_DEV))(jax.random.split(seeds[4], (N_DP * N_TABLE))).reshape((N_DP * N_TABLE, HIST_DEV)).astype(jnp.int32)
    proj_weight = noise(seeds[5], (D, PROJ), D ** -0.5, 0.1875)
    out_weight = noise(seeds[6], (D, D), D ** -0.5, 0.1875)
    upstream = noise(seeds[7], (HISTS, SEQ, D), 1.0, 6.0, ((0, 256),))
    return dict(embed_table=embed_table, owner_shard=owner_shard, slot_row=slot_row, lengths=lengths, send_order=send_order, proj_weight=proj_weight, out_weight=out_weight, upstream=upstream)


EPSILON = 1e-06

def norm_rows(values):
    average = lax.optimization_barrier(jnp.mean(values, axis=-1, keepdims=True))
    centred = values - average
    spread = lax.optimization_barrier(jnp.mean(centred * centred, axis=-1, keepdims=True))
    return centred * lax.rsqrt(spread + EPSILON)

def attend(projected, lengths):
    blocks, positions, _ = projected.shape
    value_width = D
    query_width = HEADS * QK
    gate_part = projected[:, :, :value_width].astype(jnp.float32)
    values = projected[:, :, value_width:2 * value_width].reshape(blocks, positions, HEADS, value_width // HEADS)
    queries = projected[:, :, 2 * value_width:2 * value_width + query_width].reshape(blocks, positions, HEADS, QK)
    key_part = projected[:, :, 2 * value_width + query_width:].reshape(blocks, positions, HEADS, QK)
    scores = jnp.einsum('bqhd,bkhd->bhqk', queries, key_part, preferred_element_type=jnp.float32)
    places = jnp.arange(positions)
    causal = places[:, None] >= places[None, :]
    weights = jnp.where(causal[None, None], jax.nn.silu(scores), 0.0) / lengths.astype(jnp.float32)[:, None, None, None]
    weights = weights.astype(jnp.bfloat16)
    attended = jnp.einsum('bhqk,bkhd->bqhd', weights, values, preferred_element_type=jnp.float32)
    return norm_rows(attended.reshape(blocks, positions, value_width)) * gate_part

def local_layer(fetched, lengths, upstream, proj_weight, out_weight):
    blocks, positions, feature_count = fetched.shape
    is_valid = jnp.arange(positions)[None, :] < lengths[:, None]
    grad_top = jnp.where(is_valid[:, :, None], upstream, jnp.zeros_like(upstream))
    flat_rows = fetched.reshape(blocks * positions, feature_count).astype(jnp.float32)
    normed_full, norm_back = jax.vjp(norm_rows, flat_rows)
    normed = normed_full.astype(jnp.bfloat16)
    before = jnp.dot(normed, proj_weight, preferred_element_type=jnp.float32)
    projected = jax.nn.silu(before).astype(jnp.bfloat16).reshape(blocks, positions, -1)
    mixed_full, attend_back = jax.vjp(lambda inner: attend(inner, lengths), projected)
    mixed = mixed_full.astype(jnp.bfloat16).reshape(blocks * positions, -1)
    flat_top = grad_top.reshape(blocks * positions, -1)
    grad_mixed = lax.dot_general(flat_top, out_weight, (((1,), (1,)), ((), ())), preferred_element_type=jnp.float32).astype(jnp.bfloat16)
    grad_projected = attend_back(grad_mixed.reshape(blocks, positions, -1).astype(jnp.float32))[0]
    sigmoid_before = jax.nn.sigmoid(before)
    slope = sigmoid_before * (1.0 + before * (1.0 - sigmoid_before))
    grad_before = (grad_projected.reshape(blocks * positions, -1).astype(jnp.float32) * slope).astype(jnp.bfloat16)
    grad_normed = lax.dot_general(grad_before, proj_weight, (((1,), (1,)), ((), ())), preferred_element_type=jnp.float32)
    grad_rows = (norm_back(grad_normed)[0] + flat_top.astype(jnp.float32)).astype(jnp.bfloat16)
    return (normed, mixed, flat_top, grad_before, grad_rows.reshape(blocks, positions, feature_count))

def reference(embed_table, owner_shard, slot_row, lengths, send_order, proj_weight, out_weight, upstream):
    group_count = N_DP
    shard_count = N_TABLE
    per_peer = HIST_DEV // group_count
    hand_order = send_order.reshape(group_count, shard_count, group_count, per_peer)
    source = (jnp.arange(group_count)[:, None, None, None] * shard_count + jnp.arange(shard_count)[None, :, None, None]) * HIST_DEV
    placed = jnp.transpose(source + hand_order, (2, 1, 0, 3)).reshape(-1).astype(jnp.int32)
    owners = owner_shard[:, :, :, 0][placed]
    table_rows = (owners * ROWS_DEV + slot_row[placed]).reshape(-1).astype(jnp.int32)
    fetched = embed_table[table_rows].reshape(group_count, shard_count, HIST_DEV, SEQ, D)
    arranged = lengths[placed].reshape(group_count, shard_count, HIST_DEV)
    upstream_blocks = upstream.reshape(group_count, shard_count, HIST_DEV, SEQ, D)
    grad_scale = float(HISTS * SEQ) ** (-0.5)
    zero = (jnp.zeros((D, PROJ), jnp.float32), jnp.zeros((D, D), jnp.float32))

    def device_step(totals, inputs):
        rows_block, length_block, upstream_block = inputs
        normed, mixed, flat_top, grad_before, grad_rows = local_layer(rows_block, length_block, upstream_block, proj_weight, out_weight)
        first = lax.dot_general(normed, grad_before, (((0,), (0,)), ((), ())), preferred_element_type=jnp.float32) * grad_scale
        second = lax.dot_general(mixed, flat_top, (((0,), (0,)), ((), ())), preferred_element_type=jnp.float32) * grad_scale
        first = lax.optimization_barrier(first.astype(jnp.bfloat16)).astype(jnp.float32)
        second = lax.optimization_barrier(second.astype(jnp.bfloat16)).astype(jnp.float32)
        return ((totals[0] + first, totals[1] + second), grad_rows)

    def group_step(totals, inputs):
        partial_sums, grads = lax.scan(device_step, zero, inputs)
        return ((totals[0] + partial_sums[0], totals[1] + partial_sums[1]), grads)
    totals, grads = lax.scan(group_step, zero, (fetched, arranged, upstream_blocks))
    grad_flat = grads.reshape(-1, EMB).astype(jnp.float32)
    table_grad = jnp.zeros((ROWS, EMB), jnp.float32).at[table_rows].add(grad_flat)
    return (table_grad.astype(jnp.bfloat16), totals[0].astype(jnp.bfloat16), totals[1].astype(jnp.bfloat16))
```

```python
import functools

import jax
import jax.numpy as jnp
from jax import lax
from jax.experimental import pallas as pl
from jax.experimental.pallas import tpu as pltpu
from jax.sharding import PartitionSpec as P

D = 1024
EMB = 512
HEADS = 8
QK = 64
PROJ = 3072
SEQ = 64
HIST = 8
ROWS_DEV = 2048
MOST = 8
N_DP = 8
N_TABLE = 32
PAIRS = HIST // 2
TOK = 2 * SEQ
SLOTS = 2 * N_TABLE * MOST
EPSILON = 1e-06
SCALE = float(2048 * 64) ** (-0.5)
MESH = pl.DeviceIdType.MESH
VMEM_LIMIT = 60 * 1024 * 1024
F32 = jnp.float32
BF16 = jnp.bfloat16


def mm(a, b):
    return lax.dot_general(a, b, (((1,), (0,)), ((), ())), preferred_element_type=F32)


def mm_nt(a, b):
    return lax.dot_general(a, b, (((1,), (1,)), ((), ())), preferred_element_type=F32)


def mm_tn(a, b):
    return lax.dot_general(a, b, (((0,), (0,)), ((), ())), preferred_element_type=F32)


def sigmoid(x):
    return 0.5 * jnp.tanh(0.5 * x) + 0.5


def gather_kernel(req_ref, table_ref, out_ref):
    places = lax.broadcasted_iota(jnp.int32, (256, ROWS_DEV), 1)
    chosen = (places == req_ref[...]).astype(BF16)
    out_ref[...] = mm(chosen, table_ref[...]).astype(BF16)


def gather_rows(requested, table):
    count = requested.shape[0]
    return pl.pallas_call(
        gather_kernel,
        grid=(count // 256,),
        out_shape=jax.ShapeDtypeStruct((count, EMB), BF16),
        in_specs=[
            pl.BlockSpec((256, 1), lambda i: (i, 0)),
            pl.BlockSpec((ROWS_DEV, EMB), lambda i: (0, 0)),
        ],
        out_specs=pl.BlockSpec((256, EMB), lambda i: (i, 0)),
        compiler_params=pltpu.CompilerParams(vmem_limit_bytes=VMEM_LIMIT),
        name="gather_rows",
    )(requested, table)


def layer_kernel(
    rep_ref, cols_ref, rows_ref, up_ref, wp_ref, wo_ref, out_ref, g_ref,
    normed_t, mixed_t, tops, gbs,
):
    def pair(p, carry):
        start = pl.multiple_of(p * TOK, TOK)
        tokens = pl.ds(start, TOK)
        info = cols_ref[tokens, :]
        item_at, action_at = info[:, 0:1], info[:, 1:2]
        length = info[:, 2:3]
        replies = rep_ref[:, p].reshape(SLOTS, EMB)
        places = lax.broadcasted_iota(jnp.int32, (TOK, SLOTS), 1)
        left = mm((places == item_at).astype(BF16), replies)
        right = mm((places == action_at).astype(BF16), replies)
        fetched = jnp.concatenate([left, right], axis=1)
        average = jnp.mean(fetched, axis=1, keepdims=True)
        centred = fetched - average
        rstd = lax.rsqrt(jnp.mean(centred * centred, axis=1, keepdims=True) + EPSILON)
        normed_full = centred * rstd
        normed = normed_full.astype(BF16)
        normed_t[:, tokens] = normed_full.T.astype(BF16)

        before = mm(normed, wp_ref[...])
        gate = sigmoid(before)
        slope = gate * (1.0 + before * (1.0 - gate))
        projected = (before * gate).astype(BF16)
        u = projected[:, :D].astype(F32)
        values = projected[:, D : 2 * D]
        queries = projected[:, 2 * D : 2 * D + HEADS * QK]
        keys = projected[:, 2 * D + HEADS * QK :]

        at = lax.broadcasted_iota(jnp.int32, (TOK, TOK), 0)
        source = lax.broadcasted_iota(jnp.int32, (TOK, TOK), 1)
        seen = (source <= at) & ((at // SEQ) == (source // SEQ))
        share = jnp.where(seen, 1.0 / length.astype(F32), 0.0)
        lane = lax.broadcasted_iota(jnp.int32, (TOK, TOK), 1)
        parts = (lane < QK, lane >= QK)
        zero = jnp.zeros((TOK, TOK), BF16)

        weights, factors, attended = [], [], []
        for h in range(HEADS):
            two = slice((h // 2) * TOK, (h // 2 + 1) * TOK)
            key = jnp.where(parts[h % 2], keys[:, two], zero)
            score = mm_nt(queries[:, two], key)
            open_ = sigmoid(score)
            weight = (score * open_ * share).astype(BF16)
            weights.append(weight)
            factors.append(open_ * (1.0 + score * (1.0 - open_)) * share)
            attended.append(mm(weight, values[:, h * TOK : (h + 1) * TOK]))
        attended = jnp.concatenate(attended, axis=1)
        average = jnp.mean(attended, axis=1, keepdims=True)
        centred = attended - average
        spread = lax.rsqrt(jnp.mean(centred * centred, axis=1, keepdims=True) + EPSILON)
        inner = centred * spread
        mixed_t[:, tokens] = (inner * u).T.astype(BF16)

        place = lax.broadcasted_iota(jnp.int32, (TOK, D), 0) % SEQ
        top = jnp.where(place < length, up_ref[tokens, :].astype(F32), 0.0)
        top_low = top.astype(BF16)
        tops[tokens, :] = top_low
        grad_mixed = mm_nt(top_low, wo_ref[...]).astype(BF16).astype(F32)
        grad_u = (grad_mixed * inner).astype(BF16)
        grad_inner = grad_mixed * u
        first = jnp.mean(grad_inner, axis=1, keepdims=True)
        second = jnp.mean(grad_inner * inner, axis=1, keepdims=True)
        grad_att = (spread * (grad_inner - first - inner * second)).astype(BF16)

        grad_v, grad_q, grad_k = [], [], []
        for h in range(HEADS):
            own = slice(h * TOK, (h + 1) * TOK)
            two = slice((h // 2) * TOK, (h // 2 + 1) * TOK)
            grad_weight = mm_nt(grad_att[:, own], values[:, own]).astype(BF16).astype(F32)
            grad_v.append(mm_tn(weights[h], grad_att[:, own]).astype(BF16))
            grad_score = (grad_weight * factors[h]).astype(BF16)
            key = jnp.where(parts[h % 2], keys[:, two], zero)
            query = jnp.where(parts[h % 2], queries[:, two], zero)
            gq = mm(grad_score, key)
            gk = mm_tn(grad_score, query)
            if h % 2:
                grad_q[-1] = (grad_q[-1] + gq).astype(BF16)
                grad_k[-1] = (grad_k[-1] + gk).astype(BF16)
            else:
                grad_q.append(gq)
                grad_k.append(gk)
        grad_projected = jnp.concatenate([grad_u] + grad_v + grad_q + grad_k, axis=1)
        grad_before = (grad_projected.astype(F32) * slope).astype(BF16)
        gbs[tokens, :] = grad_before
        grad_normed = mm_nt(grad_before, wp_ref[...])
        first = jnp.mean(grad_normed, axis=1, keepdims=True)
        second = jnp.mean(grad_normed * normed_full, axis=1, keepdims=True)
        grad_rows = (top + rstd * (grad_normed - first - normed_full * second)).astype(BF16)

        slots = lax.broadcasted_iota(jnp.int32, (SLOTS, TOK), 0)
        item_row = rows_ref[p, 0:1, :]
        action_row = rows_ref[p, 1:2, :]
        back = mm((slots == item_row).astype(BF16), grad_rows[:, :EMB])
        back = back + mm((slots == action_row).astype(BF16), grad_rows[:, EMB:])
        out_ref[:, p] = back.astype(BF16).reshape(N_TABLE, 16, EMB)
        return carry

    lax.fori_loop(0, PAIRS, pair, 0)

    for y in range(N_DP // 2):
        wide = mm(normed_t[...], gbs[:, y * 768 : (y + 1) * 768]) * SCALE
        narrow = mm(mixed_t[...], tops[:, y * 256 : (y + 1) * 256]) * SCALE
        for c in range(2):
            g_ref[2 * y + c, :, 0:384] = wide[:, c * 384 : (c + 1) * 384].astype(BF16)
            g_ref[2 * y + c, :, 384:512] = narrow[:, c * 128 : (c + 1) * 128].astype(BF16)


def layer(replies, cols, rows, upstream, proj_weight, out_weight):
    whole = pl.BlockSpec(memory_space=pltpu.VMEM)
    return pl.pallas_call(
        layer_kernel,
        out_shape=(
            jax.ShapeDtypeStruct((N_TABLE, PAIRS, 16, EMB), BF16),
            jax.ShapeDtypeStruct((N_DP, D, 512), BF16),
        ),
        in_specs=[whole] * 6,
        out_specs=(whole, whole),
        scratch_shapes=[
            pltpu.VMEM((D, HIST * SEQ), BF16),
            pltpu.VMEM((D, HIST * SEQ), BF16),
            pltpu.VMEM((HIST * SEQ, D), BF16),
            pltpu.VMEM((HIST * SEQ, PROJ), BF16),
        ],
        compiler_params=pltpu.CompilerParams(vmem_limit_bytes=VMEM_LIMIT),
        name="layer",
    )(replies, cols, rows, upstream, proj_weight, out_weight)


class Ring:
    def __init__(self, place, to_right, to_left, chunk, half, far, near, send, recv):
        self.place, self.right, self.left = place, to_right, to_left
        self.chunk, self.half, self.far, self.near = chunk, half, far, near
        self.send, self.recv = send, recv

    def copy(self, number, src, dst, device):
        return pltpu.make_async_remote_copy(
            src_ref=src, dst_ref=dst, send_sem=self.send.at[number], recv_sem=self.recv.at[number],
            device_id=device, device_id_type=MESH,
        )

    def begin(self):
        across, after, ahead = (lax.rem(self.place + k, 4) for k in (2, 1, 3))
        self.after, self.ahead = after, ahead
        part, half, far, near = self.chunk, self.half, self.far, self.near
        self.copies = [
            self.copy(0, half(part(across), 0), far.at[0], self.right),
            self.copy(1, half(part(across), 1), far.at[1], self.left),
            self.copy(2, half(part(after), 1), half(near.at[0], 1), self.right),
            self.copy(3, half(part(ahead), 0), half(near.at[1], 0), self.left),
            self.copy(4, half(part(after), 0), half(near.at[0], 0), self.right),
            self.copy(5, half(part(ahead), 1), half(near.at[1], 1), self.left),
        ]
        for k in range(4):
            self.copies[k].start()

    def forward(self, add):
        self.copies[0].wait_recv()
        add(self.half(self.chunk(self.after), 0), self.far.at[0])
        self.copies[4].start()
        self.copies[1].wait_recv()
        add(self.half(self.chunk(self.ahead), 1), self.far.at[1])
        self.copies[5].start()

    def arrive(self):
        for k in range(2, 6):
            self.copies[k].wait_recv()

    def end(self):
        for k in range(6):
            self.copies[k].wait_send()


def add_into(target, other):
    for n in range(target.shape[0]):
        target[n] = (target[n].astype(F32) + other[n].astype(F32)).astype(BF16)


def finish_kernel(
    g_ref, slots_ref, req_ref, dense_ref, table_ref,
    core_buf, s1, far_a, far_b, near_a, near_b, sum_a, sum_b,
    far_a2, far_b2, near_a2, near_b2, s4, zbuf, incoming, t2, t_core, t_far, t_near,
    core_send, core_recv, ring_send, ring_recv, z_send, z_recv, a_send, a_recv, own_sem,
):
    dp = lax.axis_index("dp")
    tab = lax.axis_index("table")
    y, c = dp // 2, dp % 2
    x, z = tab // 8, tab % 8
    other = (2 * y + 1 - c, tab)
    y_right = (2 * lax.rem(y + 1, 4) + c, tab)
    y_left = (2 * lax.rem(y + 3, 4) + c, tab)
    x_right = (dp, lax.rem(tab + 8, 32))
    x_left = (dp, lax.rem(tab + 24, 32))

    barrier = pltpu.get_barrier_semaphore()
    for device in (other, y_right, y_left):
        pl.semaphore_signal(barrier, inc=1, device_id=device, device_id_type=MESH)

    def greet(k, carry):
        pl.semaphore_signal(
            barrier, inc=1, device_id=(dp, lax.rem(tab + k, 32)), device_id_type=MESH
        )
        return carry

    lax.fori_loop(1, 32, greet, 0)
    pl.semaphore_wait(barrier, 34)

    def core_copy(k):
        return pltpu.make_async_remote_copy(
            src_ref=g_ref.at[2 * k + 1 - c], dst_ref=core_buf.at[k],
            send_sem=core_send.at[k], recv_sem=core_recv.at[k],
            device_id=other, device_id_type=MESH,
        )

    for k in range(4):
        core_copy(k).start()

    def give_copy(k):
        peer = lax.rem(tab + k, 32)
        return pltpu.make_async_remote_copy(
            src_ref=slots_ref.at[peer], dst_ref=incoming.at[tab],
            send_sem=a_send.at[k], recv_sem=a_recv.at[k],
            device_id=(dp, peer), device_id_type=MESH,
        )

    def give(k, carry):
        give_copy(k).start()
        return carry

    lax.fori_loop(1, 32, give, 0)
    own = pltpu.make_async_copy(slots_ref.at[tab], incoming.at[tab], own_sem)
    own.start()

    def merge(k):
        def step(n, carry):
            rows = pl.ds(pl.multiple_of(n * 256, 256), 256)
            mine = g_ref[2 * k + c, rows, :].astype(F32)
            s1[k, n] = (mine + core_buf[k, rows, :].astype(F32)).astype(BF16)
            return carry

        lax.fori_loop(0, 4, step, 0)

    for k in range(4):
        core_copy(k).wait_recv()
        merge(k)

    def two(ref, n):
        return ref.at[pl.ds(2 * n, 2)]

    ring_a = Ring(y, y_right, y_left, lambda k: s1.at[k, :, pl.ds(0, 128), :], two, far_a, near_a,
                  ring_send.at[0], ring_recv.at[0])
    ring_b = Ring(x, x_right, x_left, lambda k: s1.at[:, k, pl.ds(128, 128), :], two, far_b, near_b,
                  ring_send.at[1], ring_recv.at[1])
    ring_a.begin()
    ring_b.begin()
    ring_a.forward(add_into)
    ring_b.forward(add_into)
    ring_a.arrive()
    for n in range(4):
        sum_a[n] = (
            s1[y, n, 0:128, :].astype(F32) + near_a[0, n].astype(F32) + near_a[1, n].astype(F32)
        ).astype(BF16)

    def rows64(ref, n):
        return ref.at[pl.ds(64 * n, 64), :]

    def add_flat(target, other_ref):
        target[...] = (target[...].astype(F32) + other_ref[...].astype(F32)).astype(BF16)

    ring_a2 = Ring(x, x_right, x_left, lambda k: sum_a.at[k], rows64, far_a2, near_a2,
                   ring_send.at[2], ring_recv.at[2])
    ring_a2.begin()
    ring_b.arrive()
    for n in range(4):
        sum_b[n] = (
            s1[n, x, 128:256, :].astype(F32) + near_b[0, n].astype(F32) + near_b[1, n].astype(F32)
        ).astype(BF16)
    ring_b2 = Ring(y, y_right, y_left, lambda k: sum_b.at[k], rows64, far_b2, near_b2,
                   ring_send.at[3], ring_recv.at[3])
    ring_b2.begin()
    ring_a2.forward(add_flat)
    ring_b2.forward(add_flat)
    ring_a2.arrive()
    low = sum_a[x].astype(F32) + near_a2[0].astype(F32) + near_a2[1].astype(F32)
    s4[0:4] = low.astype(BF16).reshape(4, 32, 512)
    ring_b2.arrive()
    high = sum_b[y].astype(F32) + near_b2[0].astype(F32) + near_b2[1].astype(F32)
    s4[4:8] = high.astype(BF16).reshape(4, 32, 512)

    def z_copy(k):
        peer = lax.rem(z + k, 8)
        return pltpu.make_async_remote_copy(
            src_ref=s4.at[peer], dst_ref=zbuf.at[k],
            send_sem=z_send.at[k], recv_sem=z_recv.at[k],
            device_id=(dp, 8 * x + peer), device_id_type=MESH,
        )

    for k in range(1, 8):
        z_copy(k).start()

    def taken(k, carry):
        give_copy(k).wait_recv()
        return carry

    own.wait()
    lax.fori_loop(1, 32, taken, 0)

    def rows_of(first):
        places = lax.broadcasted_iota(jnp.int32, (256, ROWS_DEV), 0) + first
        chosen = (places == req_ref[...]).astype(BF16)
        return mm(chosen, incoming[...].reshape(N_TABLE * 64, EMB)).astype(BF16).astype(F32)

    def table_block(b, carry):
        upper = rows_of(b * 256)
        lower = rows_of(b * 256 + 1024)
        rows = pl.ds(pl.multiple_of(b * 256, 256), 256)
        is_left = lax.broadcasted_iota(jnp.int32, (256, 128), 1) < 64
        for k in range(4):
            up, low = upper[:, k * 128 : (k + 1) * 128], lower[:, k * 128 : (k + 1) * 128]
            t2[0, k, rows, :] = jnp.where(is_left, up, pltpu.roll(low, 64, 1)).astype(BF16)
            t2[1, k, rows, :] = jnp.where(is_left, pltpu.roll(up, 64, 1), low).astype(BF16)
        return carry

    lax.fori_loop(0, 4, table_block, 0)
    t_copy = pltpu.make_async_remote_copy(
        src_ref=t2.at[1 - c], dst_ref=t_core, send_sem=core_send.at[4], recv_sem=core_recv.at[4],
        device_id=other, device_id_type=MESH,
    )
    t_copy.start()

    total = s4[z].astype(F32)
    for k in range(1, 8):
        z_copy(k).wait_recv()
        total = total + zbuf[k].astype(F32)
    dense_ref[...] = total.astype(BF16)

    t_copy.wait_recv()
    for k in range(4):
        add_flat(t2.at[c, k], t_core.at[k])

    def rows512(ref, n):
        return ref.at[pl.ds(512 * n, 512), :]

    ring_t = Ring(y, y_right, y_left, lambda k: t2.at[c, k], rows512, t_far, t_near,
                  ring_send.at[4], ring_recv.at[4])
    ring_t.begin()
    ring_t.forward(add_flat)
    ring_t.arrive()
    table_ref[...] = (
        t2[c, y].astype(F32) + t_near[0].astype(F32) + t_near[1].astype(F32)
    ).astype(BF16)

    def sent(k, carry):
        give_copy(k).wait_send()
        return carry

    lax.fori_loop(1, 32, sent, 0)
    for k in range(4):
        core_copy(k).wait_send()
    for k in range(1, 8):
        z_copy(k).wait_send()
    t_copy.wait_send()
    for ring in (ring_a, ring_b, ring_a2, ring_b2, ring_t):
        ring.end()


def finish(dense_terms, outgoing, requested):
    whole = pl.BlockSpec(memory_space=pltpu.VMEM)
    dma = pltpu.SemaphoreType.DMA
    return pl.pallas_call(
        finish_kernel,
        out_shape=(
            jax.ShapeDtypeStruct((32, 512), BF16),
            jax.ShapeDtypeStruct((1024, 128), BF16),
        ),
        in_specs=[whole] * 3,
        out_specs=(whole, whole),
        scratch_shapes=[
            pltpu.VMEM((4, D, 512), BF16),
            pltpu.VMEM((4, 4, 256, 512), BF16),
            pltpu.VMEM((2, 2, 128, 512), BF16),
            pltpu.VMEM((2, 2, 128, 512), BF16),
            pltpu.VMEM((2, 4, 128, 512), BF16),
            pltpu.VMEM((2, 4, 128, 512), BF16),
            pltpu.VMEM((4, 128, 512), BF16),
            pltpu.VMEM((4, 128, 512), BF16),
            pltpu.VMEM((2, 64, 512), BF16),
            pltpu.VMEM((2, 64, 512), BF16),
            pltpu.VMEM((2, 128, 512), BF16),
            pltpu.VMEM((2, 128, 512), BF16),
            pltpu.VMEM((8, 32, 512), BF16),
            pltpu.VMEM((8, 32, 512), BF16),
            pltpu.VMEM((N_TABLE, 64, EMB), BF16),
            pltpu.VMEM((2, 4, 1024, 128), BF16),
            pltpu.VMEM((4, 1024, 128), BF16),
            pltpu.VMEM((2, 512, 128), BF16),
            pltpu.VMEM((2, 1024, 128), BF16),
            dma((5,)), dma((5,)), dma((5, 6)), dma((5, 6)), dma((8,)), dma((8,)),
            dma((32,)), dma((32,)), dma,
        ],
        compiler_params=pltpu.CompilerParams(
            vmem_limit_bytes=VMEM_LIMIT, collective_id=0, has_side_effects=True
        ),
        name="finish",
    )(dense_terms, outgoing, requested)


def body(
    embed_table, owner_shard, slot_row, lengths, send_order, proj_weight, out_weight, upstream
):
    order = send_order[0]
    ids = owner_shard[..., 0] * ROWS_DEV + slot_row
    ids = jnp.swapaxes(ids, 1, 2).reshape(HIST, 2 * SEQ)
    message = jnp.concatenate([ids, lengths[:, None]], axis=1)[order]
    message = lax.all_to_all(message, "dp", split_axis=0, concat_axis=0, tiled=True)
    ids, length = message[:, : 2 * SEQ], message[:, 2 * SEQ]
    owner, row = ids // ROWS_DEV, ids % ROWS_DEV
    same = owner[:, :, None] == owner[:, None, :]
    earlier = jnp.tril(jnp.ones((2 * SEQ, 2 * SEQ), jnp.bool_), -1)
    rank = jnp.sum((same & earlier[None]).astype(jnp.int32), axis=2)
    slot = owner * MOST + rank
    hit = slot[:, None, :] == jnp.arange(N_TABLE * MOST)[None, :, None]
    request = jnp.sum(jnp.where(hit, row[:, None, :] + 1, 0), axis=2) - 1
    request = request.reshape(HIST, N_TABLE, MOST).transpose(1, 0, 2).reshape(N_TABLE, 64)
    requested = lax.all_to_all(request, "table", split_axis=0, concat_axis=0, tiled=True)

    picked = gather_rows(requested.reshape(-1, 1), embed_table).reshape(N_TABLE, 64, EMB)
    replies = lax.all_to_all(picked, "table", split_axis=0, concat_axis=0, tiled=True)

    in_pair = owner * 16 + (jnp.arange(HIST) % 2)[:, None] * MOST + rank
    in_pair = in_pair.reshape(PAIRS, 2, 2, SEQ)
    rows = jnp.swapaxes(in_pair, 1, 2).reshape(PAIRS, 2, TOK)
    cols = jnp.stack(
        [
            in_pair[:, :, 0].reshape(-1),
            in_pair[:, :, 1].reshape(-1),
            jnp.broadcast_to(length[:, None], (HIST, SEQ)).reshape(-1),
        ],
        axis=1,
    )
    outgoing, dense_terms = layer(
        replies.reshape(N_TABLE, PAIRS, 16, EMB),
        cols,
        rows,
        upstream.reshape(HIST * SEQ, D),
        proj_weight,
        out_weight,
    )
    dense, table = finish(
        dense_terms, outgoing.reshape(N_TABLE, 64, EMB), requested.reshape(1, -1)
    )
    table = jnp.concatenate([table[:, :64], table[:, 64:]], axis=0)
    return table, dense[:, :384], dense[:, 384:]


def solution(mesh):
    in_specs = (
        P("table", None),
        P(("dp", "table"), None, None, None),
        P(("dp", "table"), None, None),
        P(("dp", "table")),
        P(("dp", "table"), None),
        P(),
        P(),
        P(("dp", "table"), None, None),
    )
    out_specs = (P("table", "dp"), P("table", "dp"), P("table", "dp"))
    return jax.shard_map(body, mesh=mesh, in_specs=in_specs, out_specs=out_specs, check_vma=False)
```

```python
import functools

import jax
import jax.numpy as jnp
from jax import lax
from jax.experimental import pallas as pl
from jax.experimental.pallas import tpu as pltpu
from jax.sharding import PartitionSpec as P

D = 1024
EMB = 512
HEADS = 8
QK = 64
PROJ = 3072
SEQ = 64
HIST = 8
ROWS_DEV = 2048
MOST = 8
N_DP = 8
N_TABLE = 32
PAIRS = HIST // 2
TOK = 2 * SEQ
SLOTS = 2 * N_TABLE * MOST
EPSILON = 1e-06
SCALE = float(2048 * 64) ** (-0.5)
MESH = pl.DeviceIdType.MESH
VMEM_LIMIT = 60 * 1024 * 1024
F32 = jnp.float32
BF16 = jnp.bfloat16


def mm(a, b):
    return lax.dot_general(a, b, (((1,), (0,)), ((), ())), preferred_element_type=F32)


def mm_nt(a, b):
    return lax.dot_general(a, b, (((1,), (1,)), ((), ())), preferred_element_type=F32)


def mm_tn(a, b):
    return lax.dot_general(a, b, (((0,), (0,)), ((), ())), preferred_element_type=F32)


def sigmoid(x):
    return 0.5 * jnp.tanh(0.5 * x) + 0.5


class Ring:
    def __init__(self, place, to_right, to_left, chunk, half, far, near, send, recv):
        self.place, self.right, self.left = place, to_right, to_left
        self.chunk, self.half, self.far, self.near = chunk, half, far, near
        self.send, self.recv = send, recv

    def copy(self, number, src, dst, device):
        return pltpu.make_async_remote_copy(
            src_ref=src, dst_ref=dst, send_sem=self.send.at[number], recv_sem=self.recv.at[number],
            device_id=device, device_id_type=MESH,
        )

    def begin(self):
        across, after, ahead = (lax.rem(self.place + k, 4) for k in (2, 1, 3))
        self.after, self.ahead = after, ahead
        part, half, far, near = self.chunk, self.half, self.far, self.near
        self.copies = [
            self.copy(0, half(part(across), 0), far.at[0], self.right),
            self.copy(1, half(part(across), 1), far.at[1], self.left),
            self.copy(2, half(part(after), 1), half(near.at[0], 1), self.right),
            self.copy(3, half(part(ahead), 0), half(near.at[1], 0), self.left),
            self.copy(4, half(part(after), 0), half(near.at[0], 0), self.right),
            self.copy(5, half(part(ahead), 1), half(near.at[1], 1), self.left),
        ]
        for k in range(4):
            self.copies[k].start()

    def forward(self, add):
        self.copies[0].wait_recv()
        add(self.half(self.chunk(self.after), 0), self.far.at[0])
        self.copies[4].start()
        self.copies[1].wait_recv()
        add(self.half(self.chunk(self.ahead), 1), self.far.at[1])
        self.copies[5].start()

    def arrive(self):
        for k in range(2, 6):
            self.copies[k].wait_recv()

    def end(self):
        for k in range(6):
            self.copies[k].wait_send()


def add_into(target, other):
    for n in range(target.shape[0]):
        target[n] = (target[n].astype(F32) + other[n].astype(F32)).astype(BF16)


def layer_pair(replies, cols, rows, upstream, wp, wo):
    item_at, action_at, length = cols[:, 0:1], cols[:, 1:2], cols[:, 2:3]
    places = lax.broadcasted_iota(jnp.int32, (TOK, SLOTS), 1)
    left = mm((places == item_at).astype(BF16), replies)
    right = mm((places == action_at).astype(BF16), replies)
    fetched = jnp.concatenate([left, right], axis=1)
    average = jnp.mean(fetched, axis=1, keepdims=True)
    centred = fetched - average
    rstd = lax.rsqrt(jnp.mean(centred * centred, axis=1, keepdims=True) + EPSILON)
    normed_full = centred * rstd
    normed = normed_full.astype(BF16)

    before = mm(normed, wp[...])
    gate = sigmoid(before)
    slope = gate * (1.0 + before * (1.0 - gate))
    projected = (before * gate).astype(BF16)
    u = projected[:, :D].astype(F32)
    values = projected[:, D : 2 * D]
    queries = projected[:, 2 * D : 2 * D + HEADS * QK]
    keys = projected[:, 2 * D + HEADS * QK :]

    at = lax.broadcasted_iota(jnp.int32, (TOK, TOK), 0)
    source = lax.broadcasted_iota(jnp.int32, (TOK, TOK), 1)
    seen = (source <= at) & ((at // SEQ) == (source // SEQ))
    share = jnp.where(seen, 1.0 / length.astype(F32), 0.0)
    parts = (source < QK, source >= QK)
    zero = jnp.zeros((TOK, TOK), BF16)

    weights, factors, attended = [], [], []
    for h in range(HEADS):
        two = slice((h // 2) * TOK, (h // 2 + 1) * TOK)
        key = jnp.where(parts[h % 2], keys[:, two], zero)
        score = mm_nt(queries[:, two], key)
        open_ = sigmoid(score)
        weight = (score * open_ * share).astype(BF16)
        weights.append(weight)
        factors.append(open_ * (1.0 + score * (1.0 - open_)) * share)
        attended.append(mm(weight, values[:, h * TOK : (h + 1) * TOK]))
    attended = jnp.concatenate(attended, axis=1)
    average = jnp.mean(attended, axis=1, keepdims=True)
    centred = attended - average
    spread = lax.rsqrt(jnp.mean(centred * centred, axis=1, keepdims=True) + EPSILON)
    inner = centred * spread
    mixed = inner * u

    place = lax.broadcasted_iota(jnp.int32, (TOK, D), 0) % SEQ
    top = jnp.where(place < length, upstream.astype(F32), 0.0)
    top_low = top.astype(BF16)
    grad_mixed = mm_nt(top_low, wo[...]).astype(BF16).astype(F32)
    grad_u = (grad_mixed * inner).astype(BF16)
    grad_inner = grad_mixed * u
    first = jnp.mean(grad_inner, axis=1, keepdims=True)
    second = jnp.mean(grad_inner * inner, axis=1, keepdims=True)
    grad_att = (spread * (grad_inner - first - inner * second)).astype(BF16)

    grad_v, grad_q, grad_k = [], [], []
    for h in range(HEADS):
        own = slice(h * TOK, (h + 1) * TOK)
        two = slice((h // 2) * TOK, (h // 2 + 1) * TOK)
        grad_weight = mm_nt(grad_att[:, own], values[:, own]).astype(BF16).astype(F32)
        grad_v.append(mm_tn(weights[h], grad_att[:, own]).astype(BF16))
        grad_score = (grad_weight * factors[h]).astype(BF16)
        key = jnp.where(parts[h % 2], keys[:, two], zero)
        query = jnp.where(parts[h % 2], queries[:, two], zero)
        gq = mm(grad_score, key)
        gk = mm_tn(grad_score, query)
        if h % 2:
            grad_q[-1] = (grad_q[-1] + gq).astype(BF16)
            grad_k[-1] = (grad_k[-1] + gk).astype(BF16)
        else:
            grad_q.append(gq)
            grad_k.append(gk)
    grad_projected = jnp.concatenate([grad_u] + grad_v + grad_q + grad_k, axis=1)
    grad_before = (grad_projected.astype(F32) * slope).astype(BF16)
    grad_normed = mm_nt(grad_before, wp[...])
    first = jnp.mean(grad_normed, axis=1, keepdims=True)
    second = jnp.mean(grad_normed * normed_full, axis=1, keepdims=True)
    grad_rows = (top + rstd * (grad_normed - first - normed_full * second)).astype(BF16)

    slots = lax.broadcasted_iota(jnp.int32, (SLOTS, TOK), 0)
    back = mm((slots == rows[0:1, :]).astype(BF16), grad_rows[:, :EMB])
    back = back + mm((slots == rows[1:2, :]).astype(BF16), grad_rows[:, EMB:])
    return normed_full.T.astype(BF16), mixed.T.astype(BF16), top_low, grad_before, back.astype(BF16)


def split_number(numbers):
    high = numbers // 256
    return (numbers - 256 * high).astype(BF16), high.astype(BF16)


def program_kernel(
    msg_ref, order_ref, table_hbm, up_hbm, wp_hbm, wo_hbm,
    proj_ref, outw_ref, table_ref,
    table, up, wp, wo, msg_out, msg_in, req_out, req_in, wanted, req_rows, rows_s, cols_s,
    picked, replies, outgoing, incoming, normed_t, mixed_t, tops, gbs,
    g, core_buf, far_a, far_b, near_a, near_b, sum_a, sum_b,
    far_a2, far_b2, near_a2, near_b2, s4, zbuf, t2, t_core, t_far, t_near,
    load_sem, m_send, m_recv, r_send, r_recv, f_send, f_recv, a_send, a_recv,
    core_send, core_recv, ring_send, ring_recv, z_send, z_recv,
):
    dp = lax.axis_index("dp")
    tab = lax.axis_index("table")
    y, c = dp // 2, dp % 2
    x, z = tab // 8, tab % 8
    other = (2 * y + 1 - c, tab)
    y_right = (2 * lax.rem(y + 1, 4) + c, tab)
    y_left = (2 * lax.rem(y + 3, 4) + c, tab)
    x_right = (dp, lax.rem(tab + 8, 32))
    x_left = (dp, lax.rem(tab + 24, 32))

    loads = [
        pltpu.make_async_copy(src, dst, load_sem.at[n])
        for n, (src, dst) in enumerate(
            ((table_hbm, table), (up_hbm, up), (wp_hbm, wp), (wo_hbm, wo))
        )
    ]
    for load in loads:
        load.start()

    barrier = pltpu.get_barrier_semaphore()

    def greet_dp(k, carry):
        pl.semaphore_signal(
            barrier, inc=1, device_id=(lax.rem(dp + k, 8), tab), device_id_type=MESH
        )
        return carry

    def greet_table(k, carry):
        pl.semaphore_signal(
            barrier, inc=1, device_id=(dp, lax.rem(tab + k, 32)), device_id_type=MESH
        )
        return carry

    lax.fori_loop(1, 8, greet_dp, 0)
    lax.fori_loop(1, 32, greet_table, 0)

    order = order_ref[...]
    message = jnp.zeros((HIST, 256), jnp.int32)
    for m in range(HIST):
        message = message + jnp.where(order == m, msg_ref[m : m + 1, :], 0)
    for k in range(HIST):
        msg_out[k] = message[k : k + 1, :]
    pl.semaphore_wait(barrier, 38)

    def msg_copy(k):
        peer = lax.rem(dp + k, 8)
        return pltpu.make_async_remote_copy(
            src_ref=msg_out.at[peer], dst_ref=msg_in.at[dp],
            send_sem=m_send.at[k], recv_sem=m_recv.at[k],
            device_id=(peer, tab), device_id_type=MESH,
        )

    for k in range(1, 8):
        msg_copy(k).start()
    msg_in[dp] = msg_out[dp]
    for k in range(1, 8):
        msg_copy(k).wait_recv()

    got = jnp.concatenate([msg_in[k] for k in range(HIST)], axis=0)
    ids, lengths = got[:, : 2 * SEQ], got[:, 2 * SEQ : 2 * SEQ + 1]
    owner = ids // ROWS_DEV
    ids_col = ids.astype(F32).T.astype(jnp.int32)
    owner_col, row_col = ids_col // ROWS_DEV, ids_col % ROWS_DEV
    sub = lax.broadcasted_iota(jnp.int32, (TOK, TOK), 0)
    lane = lax.broadcasted_iota(jnp.int32, (TOK, TOK), 1)
    ranks = []
    for m in range(HIST):
        same = (owner_col[:, m : m + 1] == owner[m : m + 1, :]) & (sub < lane)
        ranks.append(jnp.sum(jnp.where(same, 1.0, 0.0), axis=0, keepdims=True))
    rank = jnp.concatenate(ranks, axis=0)
    rank_col = rank.T.astype(jnp.int32)
    request = jnp.zeros((N_TABLE, TOK), F32)
    owners = lax.broadcasted_iota(jnp.int32, (N_TABLE, TOK), 0)
    for m in range(HIST):
        low, high = split_number(row_col[:, m : m + 1] + 1)
        spot = m * MOST + rank_col[:, m : m + 1]
        put = jnp.where(lane == spot, low.astype(F32), 0.0)
        put = jnp.where(lane == spot + 64, high.astype(F32), put)
        request = request + mm((owners == owner[m : m + 1, :]).astype(BF16), put.astype(BF16))
    request = request + 256.0 * pltpu.roll(request, 64, 1)
    request = jnp.where(owners >= 0, request, 0.0)
    request = jnp.where(lax.broadcasted_iota(jnp.int32, (N_TABLE, TOK), 1) < 64, request, 0.0)
    request = request.astype(jnp.int32)
    for o in range(N_TABLE):
        req_out[o] = request[o : o + 1, :]

    def req_copy(k):
        peer = lax.rem(tab + k, 32)
        return pltpu.make_async_remote_copy(
            src_ref=req_out.at[peer], dst_ref=req_in.at[tab],
            send_sem=r_send.at[k], recv_sem=r_recv.at[k],
            device_id=(dp, peer), device_id_type=MESH,
        )

    def ask(k, carry):
        req_copy(k).start()
        return carry

    lax.fori_loop(1, 32, ask, 0)
    req_in[tab] = req_out[tab]

    slot = owner * 16 + rank.astype(jnp.int32)
    first_half = lax.broadcasted_iota(jnp.int32, (1, TOK), 1) < SEQ
    for p in range(PAIRS):
        a = slot[2 * p : 2 * p + 1, :]
        b = slot[2 * p + 1 : 2 * p + 2, :] + MOST
        item = jnp.where(first_half, a, pltpu.roll(b, SEQ, 1))
        action = jnp.where(first_half, pltpu.roll(a, SEQ, 1), b)
        length = jnp.where(first_half, lengths[2 * p : 2 * p + 1], lengths[2 * p + 1 : 2 * p + 2])
        block = jnp.concatenate([item, action, length, length] * 2, axis=0)
        rows_s[p] = block
        cols_s[p] = block.astype(F32).T.astype(jnp.int32)

    def asked(k, carry):
        req_copy(k).wait_recv()
        return carry

    lax.fori_loop(1, 32, asked, 0)
    asks = jnp.concatenate([req_in[k] for k in range(N_TABLE)], axis=0)
    low, high = split_number(asks)
    tall = lax.broadcasted_iota(jnp.int32, (SLOTS, N_TABLE), 0) // 16
    tall = (tall == lax.broadcasted_iota(jnp.int32, (SLOTS, N_TABLE), 1)).astype(BF16)
    wanted[...] = mm(tall, low) + 256.0 * mm(tall, high) - 1.0
    wide = lax.broadcasted_iota(jnp.int32, (N_TABLE, SLOTS), 1) // 16
    wide = (wide == lax.broadcasted_iota(jnp.int32, (N_TABLE, SLOTS), 0)).astype(BF16)
    across = mm_tn(low, wide) + 256.0 * mm_tn(high, wide) - 1.0
    at = lax.broadcasted_iota(jnp.int32, (TOK, SLOTS), 0)
    in_owner = lax.broadcasted_iota(jnp.int32, (TOK, SLOTS), 1) % 16
    for p in range(PAIRS):
        line = jnp.sum(jnp.where(at == in_owner + 16 * p, across, 0.0), axis=0, keepdims=True)
        req_rows[:, p * SLOTS : (p + 1) * SLOTS] = line.astype(jnp.int32)

    def fetch_copy(p, k):
        peer = lax.rem(tab + k, 32)
        return pltpu.make_async_remote_copy(
            src_ref=picked.at[p, peer], dst_ref=replies.at[p, tab],
            send_sem=f_send.at[p, k], recv_sem=f_recv.at[p, k],
            device_id=(dp, peer), device_id_type=MESH,
        )

    loads[0].wait()

    def serve(p, carry):
        at = lax.broadcasted_iota(jnp.int32, (SLOTS, TOK), 0) % 16 + 16 * p
        seen = lax.broadcasted_iota(jnp.int32, (SLOTS, TOK), 1) == at
        line = jnp.sum(jnp.where(seen, wanted[...], 0.0), axis=1, keepdims=True)
        line = line.astype(jnp.int32)
        places = lax.broadcasted_iota(jnp.int32, (SLOTS, ROWS_DEV), 1)
        chosen = (places == line).astype(BF16)
        picked[p] = mm(chosen, table[...]).astype(BF16).reshape(N_TABLE, 16, EMB)

        def start(k, inner):
            fetch_copy(p, k).start()
            return inner

        lax.fori_loop(1, 32, start, 0)
        replies[p, tab] = picked[p, tab]
        return carry

    lax.fori_loop(0, PAIRS, serve, 0)

    def give_copy(p, k):
        peer = lax.rem(tab + k, 32)
        return pltpu.make_async_remote_copy(
            src_ref=outgoing.at[p, peer], dst_ref=incoming.at[p, tab],
            send_sem=a_send.at[p, k], recv_sem=a_recv.at[p, k],
            device_id=(dp, peer), device_id_type=MESH,
        )

    for load in loads[1:]:
        load.wait()

    def pair(p, carry):
        def landed(k, inner):
            fetch_copy(p, k).wait_recv()
            return inner

        lax.fori_loop(1, 32, landed, 0)
        tokens = pl.ds(pl.multiple_of(p * TOK, TOK), TOK)
        normed_p, mixed_p, top_p, before_p, back = layer_pair(
            replies[p].reshape(SLOTS, EMB), cols_s[p], rows_s[p], up[tokens, :], wp, wo
        )
        outgoing[p] = back.reshape(N_TABLE, 16, EMB)

        def start(k, inner):
            give_copy(p, k).start()
            return inner

        lax.fori_loop(1, 32, start, 0)
        incoming[p, tab] = outgoing[p, tab]
        normed_t[:, tokens] = normed_p
        mixed_t[:, tokens] = mixed_p
        tops[tokens, :] = top_p
        gbs[tokens, :] = before_p
        return carry

    lax.fori_loop(0, PAIRS, pair, 0)

    def core_copy(k):
        return pltpu.make_async_remote_copy(
            src_ref=g.at[0, k], dst_ref=core_buf.at[k],
            send_sem=core_send.at[k], recv_sem=core_recv.at[k],
            device_id=other, device_id_type=MESH,
        )

    def terms(k, carry):
        first = mm(normed_t[...], gbs[:, pl.ds(pl.multiple_of(k * 768, 768), 768)]) * SCALE
        second = mm(mixed_t[...], tops[:, pl.ds(pl.multiple_of(k * 256, 256), 256)]) * SCALE
        for which, kept in ((0, 1 - c), (1, c)):
            one = first[:, which * 384 : (which + 1) * 384].astype(BF16)
            two = second[:, which * 128 : (which + 1) * 128].astype(BF16)
            g[kept, k, :, :, 0:384] = one.reshape(4, 256, 384)
            g[kept, k, :, :, 384:512] = two.reshape(4, 256, 128)
        core_copy(k).start()
        return carry

    lax.fori_loop(0, 4, terms, 0)
    s1 = g.at[1]

    def merge(k, carry):
        core_copy(k).wait_recv()

        def step(n, inner):
            s1[k, n] = (s1[k, n].astype(F32) + core_buf[k, n].astype(F32)).astype(BF16)
            return inner

        lax.fori_loop(0, 4, step, 0)
        return carry

    lax.fori_loop(0, 4, merge, 0)

    def two(ref, n):
        return ref.at[pl.ds(2 * n, 2)]

    ring_a = Ring(y, y_right, y_left, lambda k: s1.at[k, :, pl.ds(0, 128), :], two, far_a, near_a,
                  ring_send.at[0], ring_recv.at[0])
    ring_b = Ring(x, x_right, x_left, lambda k: s1.at[:, k, pl.ds(128, 128), :], two, far_b, near_b,
                  ring_send.at[1], ring_recv.at[1])
    ring_a.begin()
    ring_b.begin()
    ring_a.forward(add_into)
    ring_b.forward(add_into)
    ring_a.arrive()
    for n in range(4):
        sum_a[n] = (
            s1[y, n, 0:128, :].astype(F32) + near_a[0, n].astype(F32) + near_a[1, n].astype(F32)
        ).astype(BF16)

    def rows64(ref, n):
        return ref.at[pl.ds(64 * n, 64), :]

    def add_flat(target, other_ref):
        target[...] = (target[...].astype(F32) + other_ref[...].astype(F32)).astype(BF16)

    ring_a2 = Ring(x, x_right, x_left, lambda k: sum_a.at[k], rows64, far_a2, near_a2,
                   ring_send.at[2], ring_recv.at[2])
    ring_a2.begin()
    ring_b.arrive()
    for n in range(4):
        sum_b[n] = (
            s1[n, x, 128:256, :].astype(F32) + near_b[0, n].astype(F32) + near_b[1, n].astype(F32)
        ).astype(BF16)
    ring_b2 = Ring(y, y_right, y_left, lambda k: sum_b.at[k], rows64, far_b2, near_b2,
                   ring_send.at[3], ring_recv.at[3])
    ring_b2.begin()
    ring_a2.forward(add_flat)
    ring_b2.forward(add_flat)
    ring_a2.arrive()
    total = sum_a[x].astype(F32) + near_a2[0].astype(F32) + near_a2[1].astype(F32)
    s4[0:4] = total.astype(BF16).reshape(4, 32, 512)
    ring_b2.arrive()
    total = sum_b[y].astype(F32) + near_b2[0].astype(F32) + near_b2[1].astype(F32)
    s4[4:8] = total.astype(BF16).reshape(4, 32, 512)

    def z_copy(k):
        peer = lax.rem(z + k, 8)
        return pltpu.make_async_remote_copy(
            src_ref=s4.at[peer], dst_ref=zbuf.at[k],
            send_sem=z_send.at[k], recv_sem=z_recv.at[k],
            device_id=(dp, 8 * x + peer), device_id_type=MESH,
        )

    for k in range(1, 8):
        z_copy(k).start()

    def given(n, carry):
        give_copy(n // 31, n % 31 + 1).wait_recv()
        return carry

    lax.fori_loop(0, PAIRS * 31, given, 0)

    def rows_of(first):
        places = lax.broadcasted_iota(jnp.int32, (256, ROWS_DEV), 0) + first
        chosen = (places == req_rows[...]).astype(BF16)
        return mm(chosen, incoming[...].reshape(PAIRS * SLOTS, EMB)).astype(BF16).astype(F32)

    def table_block(b, carry):
        upper = rows_of(b * 256)
        lower = rows_of(b * 256 + 1024)
        rows = pl.ds(pl.multiple_of(b * 256, 256), 256)
        is_left = lax.broadcasted_iota(jnp.int32, (256, 128), 1) < 64
        for k in range(4):
            up_k, low_k = upper[:, k * 128 : (k + 1) * 128], lower[:, k * 128 : (k + 1) * 128]
            t2[0, k, rows, :] = jnp.where(is_left, up_k, pltpu.roll(low_k, 64, 1)).astype(BF16)
            t2[1, k, rows, :] = jnp.where(is_left, pltpu.roll(up_k, 64, 1), low_k).astype(BF16)
        return carry

    lax.fori_loop(0, 4, table_block, 0)
    t_copy = pltpu.make_async_remote_copy(
        src_ref=t2.at[1 - c], dst_ref=t_core, send_sem=core_send.at[4], recv_sem=core_recv.at[4],
        device_id=other, device_id_type=MESH,
    )
    t_copy.start()

    total = s4[z].astype(F32)
    for k in range(1, 8):
        z_copy(k).wait_recv()
        total = total + zbuf[k].astype(F32)
    total = total.astype(BF16)
    proj_ref[...] = total[:, :384]
    outw_ref[...] = total[:, 384:]

    t_copy.wait_recv()
    for k in range(4):
        add_flat(t2.at[c, k], t_core.at[k])

    def rows512(ref, n):
        return ref.at[pl.ds(512 * n, 512), :]

    ring_t = Ring(y, y_right, y_left, lambda k: t2.at[c, k], rows512, t_far, t_near,
                  ring_send.at[4], ring_recv.at[4])
    ring_t.begin()
    ring_t.forward(add_flat)
    ring_t.arrive()
    total = t2[c, y].astype(F32) + t_near[0].astype(F32) + t_near[1].astype(F32)
    total = total.T.astype(BF16)
    table_ref[:, 0:1024] = total[0:64]
    table_ref[:, 1024:2048] = total[64:128]

    def sent(k, carry):
        req_copy(k).wait_send()
        for p in range(PAIRS):
            fetch_copy(p, k).wait_send()
            give_copy(p, k).wait_send()
        return carry

    lax.fori_loop(1, 32, sent, 0)
    for k in range(4):
        core_copy(k).wait_send()
    for k in range(1, 8):
        msg_copy(k).wait_send()
        z_copy(k).wait_send()
    t_copy.wait_send()
    for ring in (ring_a, ring_b, ring_a2, ring_b2, ring_t):
        ring.end()


def run(message, order, table, upstream, proj_weight, out_weight):
    whole = pl.BlockSpec(memory_space=pltpu.VMEM)
    anywhere = pl.BlockSpec(memory_space=pl.ANY)
    dma = pltpu.SemaphoreType.DMA
    tokens = HIST * SEQ

    def buf(*shape):
        return pltpu.VMEM(shape, BF16)

    return pl.pallas_call(
        program_kernel,
        out_shape=(
            jax.ShapeDtypeStruct((32, 384), BF16),
            jax.ShapeDtypeStruct((32, 128), BF16),
            jax.ShapeDtypeStruct((64, 2048), BF16),
        ),
        in_specs=[whole] * 2 + [anywhere] * 4,
        out_specs=(whole,) * 3,
        scratch_shapes=[
            buf(ROWS_DEV, EMB), buf(tokens, D), buf(D, PROJ), buf(D, D),
            pltpu.VMEM((HIST, 1, 256), jnp.int32),
            pltpu.VMEM((HIST, 1, 256), jnp.int32),
            pltpu.VMEM((N_TABLE, 1, TOK), jnp.int32),
            pltpu.VMEM((N_TABLE, 1, TOK), jnp.int32),
            pltpu.VMEM((SLOTS, TOK), F32),
            pltpu.VMEM((1, PAIRS * SLOTS), jnp.int32),
            pltpu.VMEM((PAIRS, 8, TOK), jnp.int32),
            pltpu.VMEM((PAIRS, TOK, 8), jnp.int32),
            buf(PAIRS, N_TABLE, 16, EMB), buf(PAIRS, N_TABLE, 16, EMB),
            buf(PAIRS, N_TABLE, 16, EMB), buf(PAIRS, N_TABLE, 16, EMB),
            buf(D, tokens), buf(D, tokens), buf(tokens, D), buf(tokens, PROJ),
            buf(2, 4, 4, 256, 512), buf(4, 4, 256, 512),
            buf(2, 2, 128, 512), buf(2, 2, 128, 512), buf(2, 4, 128, 512), buf(2, 4, 128, 512),
            buf(4, 128, 512), buf(4, 128, 512),
            buf(2, 64, 512), buf(2, 64, 512), buf(2, 128, 512), buf(2, 128, 512),
            buf(8, 32, 512), buf(8, 32, 512),
            buf(2, 4, 1024, 128), buf(4, 1024, 128), buf(2, 512, 128), buf(2, 1024, 128),
            dma((4,)), dma((8,)), dma((8,)), dma((32,)), dma((32,)),
            dma((PAIRS, 32)), dma((PAIRS, 32)), dma((PAIRS, 32)), dma((PAIRS, 32)),
            dma((5,)), dma((5,)), dma((5, 6)), dma((5, 6)), dma((8,)), dma((8,)),
        ],
        compiler_params=pltpu.CompilerParams(
            vmem_limit_bytes=VMEM_LIMIT, collective_id=0, has_side_effects=True
        ),
        name="whole_program",
    )(message, order, table, upstream, proj_weight, out_weight)


def body(
    embed_table, owner_shard, slot_row, lengths, send_order, proj_weight, out_weight, upstream
):
    ids = owner_shard[..., 0] * ROWS_DEV + slot_row
    ids = jnp.swapaxes(ids, 1, 2).reshape(HIST, 2 * SEQ)
    lengths = jnp.broadcast_to(lengths[:, None], (HIST, 2 * SEQ))
    message = jnp.concatenate([ids, lengths], axis=1)
    proj, outw, table = run(
        message, send_order.reshape(HIST, 1), embed_table, upstream.reshape(HIST * SEQ, D),
        proj_weight, out_weight,
    )
    return table.T, proj, outw


def solution(mesh):
    in_specs = (
        P("table", None),
        P(("dp", "table"), None, None, None),
        P(("dp", "table"), None, None),
        P(("dp", "table")),
        P(("dp", "table"), None),
        P(),
        P(),
        P(("dp", "table"), None, None),
    )
    out_specs = (P("table", "dp"), P("table", "dp"), P("table", "dp"))
    return jax.shard_map(body, mesh=mesh, in_specs=in_specs, out_specs=out_specs, check_vma=False)
```

```python
import functools

import jax
import jax.numpy as jnp
from jax import lax
from jax.experimental import pallas as pl
from jax.experimental.pallas import tpu as pltpu
from jax.sharding import PartitionSpec as P

D = 1024
EMB = 512
HEADS = 8
QK = 64
PROJ = 3072
SEQ = 64
HIST = 8
ROWS_DEV = 2048
MOST = 8
N_DP = 8
N_TABLE = 32
PAIRS = HIST // 2
TOK = 2 * SEQ
SLOTS = 2 * N_TABLE * MOST
EPSILON = 1e-06
SCALE = float(2048 * 64) ** (-0.5)
MESH = pl.DeviceIdType.MESH
VMEM_LIMIT = 60 * 1024 * 1024
CUT = 160
F32 = jnp.float32
BF16 = jnp.bfloat16


def mm(a, b):
    return lax.dot_general(a, b, (((1,), (0,)), ((), ())), preferred_element_type=F32)


def mm_nt(a, b):
    return lax.dot_general(a, b, (((1,), (1,)), ((), ())), preferred_element_type=F32)


def mm_tn(a, b):
    return lax.dot_general(a, b, (((0,), (0,)), ((), ())), preferred_element_type=F32)


def sigmoid(x):
    return 0.5 * jnp.tanh(0.5 * x) + 0.5


class Ring:
    def __init__(self, place, to_right, to_left, chunk, half, far, near, send, recv):
        self.place, self.right, self.left = place, to_right, to_left
        self.chunk, self.half, self.far, self.near = chunk, half, far, near
        self.send, self.recv = send, recv

    def copy(self, number, src, dst, device):
        return pltpu.make_async_remote_copy(
            src_ref=src, dst_ref=dst, send_sem=self.send.at[number], recv_sem=self.recv.at[number],
            device_id=device, device_id_type=MESH,
        )

    def make(self):
        across, after, ahead = (lax.rem(self.place + k, 4) for k in (2, 1, 3))
        self.after, self.ahead = after, ahead
        part, half, far, near = self.chunk, self.half, self.far, self.near
        self.copies = [
            self.copy(0, half(part(across), 0), far.at[0], self.right),
            self.copy(1, half(part(across), 1), far.at[1], self.left),
            self.copy(2, half(part(after), 1), half(near.at[0], 1), self.right),
            self.copy(3, half(part(ahead), 0), half(near.at[1], 0), self.left),
            self.copy(4, half(part(after), 0), half(near.at[0], 0), self.right),
            self.copy(5, half(part(ahead), 1), half(near.at[1], 1), self.left),
        ]

    def start_half(self, number):
        for k in ((0, 3), (1, 2))[number]:
            self.copies[k].start()

    def start(self):
        self.start_half(0)
        self.start_half(1)

    def forward(self, add):
        self.copies[0].wait_recv()
        add(self.half(self.chunk(self.after), 0), self.far.at[0])
        self.copies[4].start()
        self.copies[1].wait_recv()
        add(self.half(self.chunk(self.ahead), 1), self.far.at[1])
        self.copies[5].start()

    def arrive(self):
        for k in range(2, 6):
            self.copies[k].wait_recv()

    def end(self):
        for k in range(6):
            self.copies[k].wait_send()


def add_into(target, other):
    for n in range(target.shape[0]):
        target[n] = (target[n].astype(F32) + other[n].astype(F32)).astype(BF16)


def layer_pair(replies, cols, rows, upstream, wp, wo):
    item_at, action_at, length = cols[:, 0:1], cols[:, 1:2], cols[:, 2:3]
    places = lax.broadcasted_iota(jnp.int32, (TOK, SLOTS), 1)
    left = mm((places == item_at).astype(BF16), replies)
    right = mm((places == action_at).astype(BF16), replies)
    fetched = jnp.concatenate([left, right], axis=1)
    average = jnp.mean(fetched, axis=1, keepdims=True)
    centred = fetched - average
    rstd = lax.rsqrt(jnp.mean(centred * centred, axis=1, keepdims=True) + EPSILON)
    normed_full = centred * rstd
    normed = normed_full.astype(BF16)

    before = mm(normed, wp[...])
    gate = sigmoid(before)
    slope = gate * (1.0 + before * (1.0 - gate))
    projected = (before * gate).astype(BF16)
    u = projected[:, :D].astype(F32)
    values = projected[:, D : 2 * D]
    queries = projected[:, 2 * D : 2 * D + HEADS * QK]
    keys = projected[:, 2 * D + HEADS * QK :]

    at = lax.broadcasted_iota(jnp.int32, (TOK, TOK), 0)
    source = lax.broadcasted_iota(jnp.int32, (TOK, TOK), 1)
    seen = (source <= at) & ((at // SEQ) == (source // SEQ))
    share = jnp.where(seen, 1.0 / length.astype(F32), 0.0)
    parts = (source < QK, source >= QK)
    zero = jnp.zeros((TOK, TOK), BF16)

    weights, factors, attended = [], [], []
    for h in range(HEADS):
        two = slice((h // 2) * TOK, (h // 2 + 1) * TOK)
        key = jnp.where(parts[h % 2], keys[:, two], zero)
        score = mm_nt(queries[:, two], key)
        open_ = sigmoid(score)
        weight = (score * open_ * share).astype(BF16)
        weights.append(weight)
        factors.append(open_ * (1.0 + score * (1.0 - open_)) * share)
        attended.append(mm(weight, values[:, h * TOK : (h + 1) * TOK]))
    attended = jnp.concatenate(attended, axis=1)
    average = jnp.mean(attended, axis=1, keepdims=True)
    centred = attended - average
    spread = lax.rsqrt(jnp.mean(centred * centred, axis=1, keepdims=True) + EPSILON)
    inner = centred * spread
    mixed = inner * u

    place = lax.broadcasted_iota(jnp.int32, (TOK, D), 0) % SEQ
    top = jnp.where(place < length, upstream.astype(F32), 0.0)
    top_low = top.astype(BF16)
    grad_mixed = mm_nt(top_low, wo[...]).astype(BF16).astype(F32)
    grad_u = (grad_mixed * inner).astype(BF16)
    grad_inner = grad_mixed * u
    first = jnp.mean(grad_inner, axis=1, keepdims=True)
    second = jnp.mean(grad_inner * inner, axis=1, keepdims=True)
    grad_att = (spread * (grad_inner - first - inner * second)).astype(BF16)

    grad_v, grad_q, grad_k = [], [], []
    for h in range(HEADS):
        own = slice(h * TOK, (h + 1) * TOK)
        two = slice((h // 2) * TOK, (h // 2 + 1) * TOK)
        grad_weight = mm_nt(grad_att[:, own], values[:, own]).astype(BF16).astype(F32)
        grad_v.append(mm_tn(weights[h], grad_att[:, own]).astype(BF16))
        grad_score = (grad_weight * factors[h]).astype(BF16)
        key = jnp.where(parts[h % 2], keys[:, two], zero)
        query = jnp.where(parts[h % 2], queries[:, two], zero)
        gq = mm(grad_score, key)
        gk = mm_tn(grad_score, query)
        if h % 2:
            grad_q[-1] = (grad_q[-1] + gq).astype(BF16)
            grad_k[-1] = (grad_k[-1] + gk).astype(BF16)
        else:
            grad_q.append(gq)
            grad_k.append(gk)
    grad_projected = jnp.concatenate([grad_u] + grad_v + grad_q + grad_k, axis=1)
    grad_before = (grad_projected.astype(F32) * slope).astype(BF16)
    grad_normed = mm_nt(grad_before, wp[...])
    first = jnp.mean(grad_normed, axis=1, keepdims=True)
    second = jnp.mean(grad_normed * normed_full, axis=1, keepdims=True)
    grad_rows = (top + rstd * (grad_normed - first - normed_full * second)).astype(BF16)

    slots = lax.broadcasted_iota(jnp.int32, (SLOTS, TOK), 0)
    back = mm((slots == rows[0:1, :]).astype(BF16), grad_rows[:, :EMB])
    back = back + mm((slots == rows[1:2, :]).astype(BF16), grad_rows[:, EMB:])
    return normed_full.T.astype(BF16), mixed.T.astype(BF16), top_low, grad_before, back.astype(BF16)


def split_number(numbers):
    high = numbers // 256
    return (numbers - 256 * high).astype(BF16), high.astype(BF16)


def program_kernel(
    owner_ref, slot_ref, length_ref, order_ref, table_hbm, up_hbm, wp_hbm, wo_hbm,
    dense_ref, table_ref,
    table, up, wp, wo, msg_out, msg_in, req_out, req_in, wanted, req_rows, rows_s, cols_s,
    picked, replies, incoming, normed_t, mixed_t, gbs,
    g, core_buf, sums, far_a, far_b, near_a, near_b, sum_a, sum_b,
    far_a2, far_b2, near_a2, near_b2, s4, zbuf, t_core, t_far, t_near,
    load_sem, m_send, m_recv, r_send, r_recv, f_send, f_recv, a_send, a_recv,
    core_send, core_recv, ring_send, ring_recv, z_send, z_recv,
):
    dp = lax.axis_index("dp")
    tab = lax.axis_index("table")
    y, c = dp // 2, dp % 2
    x, z = tab // 8, tab % 8
    other = (2 * y + 1 - c, tab)
    y_right = (2 * lax.rem(y + 1, 4) + c, tab)
    y_left = (2 * lax.rem(y + 3, 4) + c, tab)
    x_right = (dp, lax.rem(tab + 8, 32))
    x_left = (dp, lax.rem(tab + 24, 32))

    loads = [
        pltpu.make_async_copy(src, dst, load_sem.at[n])
        for n, (src, dst) in enumerate(
            ((table_hbm, table), (up_hbm, up), (wp_hbm, wp), (wo_hbm, wo))
        )
    ]
    for load in loads:
        load.start()

    barrier = pltpu.get_barrier_semaphore()

    def greet_dp(k, carry):
        pl.semaphore_signal(
            barrier, inc=1, device_id=(lax.rem(dp + k, 8), tab), device_id_type=MESH
        )
        return carry

    def greet_table(k, carry):
        pl.semaphore_signal(
            barrier, inc=1, device_id=(dp, lax.rem(tab + k, 32)), device_id_type=MESH
        )
        return carry

    lax.fori_loop(1, 8, greet_dp, 0)
    lax.fori_loop(1, 32, greet_table, 0)

    order = order_ref[...]
    rows_of_table = [owner_ref[m] * ROWS_DEV + slot_ref[m] for m in range(HIST)]
    for k in range(HIST):
        at = order[:, k : k + 1]
        lookups = jnp.zeros((2, SEQ), jnp.int32)
        length = jnp.zeros((1, 1), jnp.int32)
        for m in range(HIST):
            lookups = jnp.where(jnp.broadcast_to(at, (2, SEQ)) == m, rows_of_table[m], lookups)
            length = jnp.where(at == m, length_ref[:, m : m + 1], length)
        msg_out[k, 0:2, 0:SEQ] = lookups
        msg_out[k, 2:3, 0:SEQ] = jnp.broadcast_to(length, (1, SEQ))
    pl.semaphore_wait(barrier, 38)

    def msg_copy(k):
        peer = lax.rem(dp + k, 8)
        return pltpu.make_async_remote_copy(
            src_ref=msg_out.at[peer], dst_ref=msg_in.at[dp],
            send_sem=m_send.at[k], recv_sem=m_recv.at[k],
            device_id=(peer, tab), device_id_type=MESH,
        )

    for k in range(1, 8):
        msg_copy(k).start()
    msg_in[dp] = msg_out[dp]
    for k in range(1, 8):
        msg_copy(k).wait_recv()

    items = jnp.concatenate([msg_in[k, 0:1, :] for k in range(HIST)], axis=0)
    actions = jnp.concatenate([msg_in[k, 1:2, :] for k in range(HIST)], axis=0)
    lengths = jnp.concatenate([msg_in[k, 2:3, :] for k in range(HIST)], axis=0)[:, 0:1]
    is_item = lax.broadcasted_iota(jnp.int32, (HIST, TOK), 1) < SEQ
    ids = jnp.where(is_item, items, pltpu.roll(actions, SEQ, 1))
    owner = ids // ROWS_DEV
    ids_col = ids.astype(F32).T.astype(jnp.int32)
    owner_col, row_col = ids_col // ROWS_DEV, ids_col % ROWS_DEV
    sub = lax.broadcasted_iota(jnp.int32, (TOK, TOK), 0)
    lane = lax.broadcasted_iota(jnp.int32, (TOK, TOK), 1)
    ranks = []
    for m in range(HIST):
        same = (owner_col[:, m : m + 1] == owner[m : m + 1, :]) & (sub < lane)
        ranks.append(jnp.sum(jnp.where(same, 1.0, 0.0), axis=0, keepdims=True))
    rank = jnp.concatenate(ranks, axis=0)
    rank_col = rank.T.astype(jnp.int32)
    request = jnp.zeros((N_TABLE, TOK), F32)
    owners = lax.broadcasted_iota(jnp.int32, (N_TABLE, TOK), 0)
    for m in range(HIST):
        low, high = split_number(row_col[:, m : m + 1] + 1)
        spot = m * MOST + rank_col[:, m : m + 1]
        put = jnp.where(lane == spot, low.astype(F32), 0.0)
        put = jnp.where(lane == spot + 64, high.astype(F32), put)
        request = request + mm((owners == owner[m : m + 1, :]).astype(BF16), put.astype(BF16))
    request = request + 256.0 * pltpu.roll(request, 64, 1)
    request = jnp.where(owners >= 0, request, 0.0)
    request = jnp.where(lax.broadcasted_iota(jnp.int32, (N_TABLE, TOK), 1) < 64, request, 0.0)
    request = request.astype(jnp.int32)
    for o in range(N_TABLE):
        req_out[o] = request[o : o + 1, :]

    def req_copy(k):
        peer = lax.rem(tab + k, 32)
        return pltpu.make_async_remote_copy(
            src_ref=req_out.at[peer], dst_ref=req_in.at[tab],
            send_sem=r_send.at[k], recv_sem=r_recv.at[k],
            device_id=(dp, peer), device_id_type=MESH,
        )

    def ask(k, carry):
        req_copy(k).start()
        return carry

    lax.fori_loop(1, 32, ask, 0)
    req_in[tab] = req_out[tab]

    slot = owner * 16 + rank.astype(jnp.int32)
    first_half = lax.broadcasted_iota(jnp.int32, (1, TOK), 1) < SEQ
    for p in range(PAIRS):
        a = slot[2 * p : 2 * p + 1, :]
        b = slot[2 * p + 1 : 2 * p + 2, :] + MOST
        item = jnp.where(first_half, a, pltpu.roll(b, SEQ, 1))
        action = jnp.where(first_half, pltpu.roll(a, SEQ, 1), b)
        length = jnp.where(first_half, lengths[2 * p : 2 * p + 1], lengths[2 * p + 1 : 2 * p + 2])
        block = jnp.concatenate([item, action, length, length] * 2, axis=0)
        rows_s[p] = block
        cols_s[p] = block.astype(F32).T.astype(jnp.int32)

    def asked(k, carry):
        req_copy(k).wait_recv()
        return carry

    lax.fori_loop(1, 32, asked, 0)
    asks = jnp.concatenate([req_in[k] for k in range(N_TABLE)], axis=0)
    low, high = split_number(asks)
    tall = lax.broadcasted_iota(jnp.int32, (SLOTS, N_TABLE), 0) // 16
    tall = (tall == lax.broadcasted_iota(jnp.int32, (SLOTS, N_TABLE), 1)).astype(BF16)
    wanted[...] = mm(tall, low) + 256.0 * mm(tall, high) - 1.0
    wide = lax.broadcasted_iota(jnp.int32, (N_TABLE, SLOTS), 1) // 16
    wide = (wide == lax.broadcasted_iota(jnp.int32, (N_TABLE, SLOTS), 0)).astype(BF16)
    across = mm_tn(low, wide) + 256.0 * mm_tn(high, wide) - 1.0
    at = lax.broadcasted_iota(jnp.int32, (TOK, SLOTS), 0)
    in_owner = lax.broadcasted_iota(jnp.int32, (TOK, SLOTS), 1) % 16
    for p in range(PAIRS):
        line = jnp.sum(jnp.where(at == in_owner + 16 * p, across, 0.0), axis=0, keepdims=True)
        req_rows[:, p * SLOTS : (p + 1) * SLOTS] = line.astype(jnp.int32)

    def fetch_copy(p, k):
        peer = lax.rem(tab + k, 32)
        return pltpu.make_async_remote_copy(
            src_ref=picked.at[p, peer], dst_ref=replies.at[p, tab],
            send_sem=f_send.at[p, k], recv_sem=f_recv.at[p, k],
            device_id=(dp, peer), device_id_type=MESH,
        )

    loads[0].wait()

    def serve(p, carry):
        at = lax.broadcasted_iota(jnp.int32, (SLOTS, TOK), 0) % 16 + 16 * p
        seen = lax.broadcasted_iota(jnp.int32, (SLOTS, TOK), 1) == at
        line = jnp.sum(jnp.where(seen, wanted[...], 0.0), axis=1, keepdims=True)
        line = line.astype(jnp.int32)
        places = lax.broadcasted_iota(jnp.int32, (SLOTS, ROWS_DEV), 1)
        chosen = (places == line).astype(BF16)
        picked[p] = mm(chosen, table[...]).astype(BF16).reshape(N_TABLE, 16, EMB)

        def start(k, inner):
            fetch_copy(p, k).start()
            return inner

        lax.fori_loop(1, 32, start, 0)
        replies[p, tab] = picked[p, tab]
        return carry

    lax.fori_loop(0, PAIRS, serve, 0)

    outgoing = picked

    def give_copy(p, k):
        peer = lax.rem(tab + k, 32)
        return pltpu.make_async_remote_copy(
            src_ref=outgoing.at[p, peer], dst_ref=incoming.at[p, tab],
            send_sem=a_send.at[p, k], recv_sem=a_recv.at[p, k],
            device_id=(dp, peer), device_id_type=MESH,
        )

    for load in loads[1:]:
        load.wait()

    def give(n, carry):
        give_copy(n // 31, n % 31 + 1).start()
        return carry

    def fetched(p):
        def landed(k, carry):
            fetch_copy(p, k).wait_recv()
            fetch_copy(p, k).wait_send()
            return carry

        lax.fori_loop(1, 32, landed, 0)

    def pair(p, carry):
        fetched(p)

        @pl.when(p == PAIRS - 1)
        def _():
            lax.fori_loop(0, (PAIRS - 1) * 31, give, 0)

        tokens = pl.ds(pl.multiple_of(p * TOK, TOK), TOK)
        normed_p, mixed_p, top_p, before_p, back = layer_pair(
            replies[p].reshape(SLOTS, EMB), cols_s[p], rows_s[p], up[tokens, :], wp, wo
        )
        outgoing[p] = back.reshape(N_TABLE, 16, EMB)
        incoming[p, tab] = outgoing[p, tab]
        normed_t[:, tokens] = normed_p
        mixed_t[:, tokens] = mixed_p
        up[tokens, :] = top_p
        gbs[tokens, :] = before_p
        return carry

    lax.fori_loop(0, PAIRS, pair, 0)
    lax.fori_loop((PAIRS - 1) * 31, PAIRS * 31, give, 0)

    def core_copy(k):
        return pltpu.make_async_remote_copy(
            src_ref=g.at[0, k], dst_ref=core_buf.at[k],
            send_sem=core_send.at[k], recv_sem=core_recv.at[k],
            device_id=other, device_id_type=MESH,
        )

    def terms(k, carry):
        first = mm(normed_t[...], gbs[:, pl.ds(pl.multiple_of(k * 768, 768), 768)]) * SCALE
        second = mm(mixed_t[...], up[:, pl.ds(pl.multiple_of(k * 256, 256), 256)]) * SCALE
        for which, kept in ((0, 1 - c), (1, c)):
            one = first[:, which * 384 : (which + 1) * 384].astype(BF16)
            two = second[:, which * 128 : (which + 1) * 128].astype(BF16)
            g[kept, k, :, :, 0:384] = one.reshape(4, 256, 384)
            g[kept, k, :, :, 384:512] = two.reshape(4, 256, 128)
        core_copy(k).start()
        return carry

    lax.fori_loop(0, 4, terms, 0)
    s1 = g.at[1]
    t2 = g.at[0]

    def merge(k, carry):
        core_copy(k).wait_recv()
        core_copy(k).wait_send()

        def step(n, inner):
            s1[k, n] = (s1[k, n].astype(F32) + core_buf[k, n].astype(F32)).astype(BF16)
            return inner

        lax.fori_loop(0, 4, step, 0)
        return carry

    lax.fori_loop(0, 4, merge, 0)

    def two(ref, n):
        return ref.at[pl.ds(2 * n, 2)]

    def add_flat(target, other_ref):
        target[...] = (target[...].astype(F32) + other_ref[...].astype(F32)).astype(BF16)

    def chosen_rows(p, first, count):
        places = lax.broadcasted_iota(jnp.int32, (count, SLOTS), 0) + first
        return (places == req_rows[:, p * SLOTS : (p + 1) * SLOTS]).astype(BF16)

    def take_in(p):
        def given(k, carry):
            give_copy(p, k).wait_recv()
            return carry

        lax.fori_loop(1, 32, given, 0)

    def add_rows(p):
        take_in(p)

        def block(b, carry):
            first = b * 512
            part = mm(chosen_rows(p, first, 512), incoming[p].reshape(SLOTS, EMB))
            rows = pl.ds(pl.multiple_of(first, 512), 512)
            sums[rows, :] = part if p == 0 else sums[rows, :] + part
            return carry

        lax.fori_loop(0, 4, block, 0)

    ring_a = Ring(y, y_right, y_left, lambda k: s1.at[k, :, pl.ds(0, CUT), :], two, far_a, near_a,
                  ring_send.at[0], ring_recv.at[0])
    ring_b = Ring(x, x_right, x_left, lambda k: s1.at[:, k, pl.ds(CUT, 256 - CUT), :], two, far_b,
                  near_b, ring_send.at[1], ring_recv.at[1])
    for ring in (ring_a, ring_b):
        ring.make()
        ring.start()
    add_rows(0)
    ring_a.forward(add_into)
    ring_b.forward(add_into)
    add_rows(1)
    ring_b.arrive()
    for n in range(4):
        sum_b[n] = (
            s1[n, x, CUT:256, :].astype(F32) + near_b[0, n].astype(F32) + near_b[1, n].astype(F32)
        ).astype(BF16)
    ring_b2 = Ring(y, y_right, y_left, lambda k: sum_b.at[k],
                   lambda ref, n: ref.at[pl.ds((256 - CUT) // 2 * n, (256 - CUT) // 2), :],
                   far_b2, near_b2, ring_send.at[3], ring_recv.at[3])
    ring_b2.make()
    ring_b2.start()
    ring_a.arrive()
    for n in range(4):
        sum_a[n] = (
            s1[y, n, 0:CUT, :].astype(F32) + near_a[0, n].astype(F32) + near_a[1, n].astype(F32)
        ).astype(BF16)
    ring_a2 = Ring(x, x_right, x_left, lambda k: sum_a.at[k],
                   lambda ref, n: ref.at[pl.ds(CUT // 2 * n, CUT // 2), :], far_a2, near_a2,
                   ring_send.at[2], ring_recv.at[2])
    ring_a2.make()
    ring_a2.start()
    ring_b2.forward(add_flat)
    ring_a2.forward(add_flat)
    add_rows(2)
    ring_b2.arrive()
    total = sum_b[y].astype(F32) + near_b2[0].astype(F32) + near_b2[1].astype(F32)
    s4[CUT // 32 : 8] = total.astype(BF16).reshape(8 - CUT // 32, 32, 512)
    ring_a2.arrive()
    total = sum_a[x].astype(F32) + near_a2[0].astype(F32) + near_a2[1].astype(F32)
    s4[0 : CUT // 32] = total.astype(BF16).reshape(CUT // 32, 32, 512)

    def z_copy(k):
        peer = lax.rem(z + k, 8)
        return pltpu.make_async_remote_copy(
            src_ref=s4.at[peer], dst_ref=zbuf.at[k],
            send_sem=z_send.at[k], recv_sem=z_recv.at[k],
            device_id=(dp, 8 * x + peer), device_id_type=MESH,
        )

    for k in range(1, 8):
        z_copy(k).start()

    take_in(PAIRS - 1)

    def rows_of(first):
        part = mm(chosen_rows(PAIRS - 1, first, 256), incoming[PAIRS - 1].reshape(SLOTS, EMB))
        rows = pl.ds(pl.multiple_of(first, 256), 256)
        return (sums[rows, :] + part).astype(BF16).astype(F32)

    def t_copy(b):
        lanes = pl.ds(pl.multiple_of(b * 128, 128), 128)
        return pltpu.make_async_remote_copy(
            src_ref=t2.at[1 - c, :, :, lanes], dst_ref=t_core.at[:, :, lanes],
            send_sem=core_send.at[4 + b], recv_sem=core_recv.at[4 + b],
            device_id=other, device_id_type=MESH,
        )

    def table_block(b, carry):
        upper = rows_of(b * 256)
        lower = rows_of(b * 256 + 1024)
        lanes = pl.ds(pl.multiple_of(b * 128, 128), 128)
        is_left = lax.broadcasted_iota(jnp.int32, (256, 128), 1) < 64
        for k in range(4):
            up_k, low_k = upper[:, k * 128 : (k + 1) * 128], lower[:, k * 128 : (k + 1) * 128]
            t2[0, k, :, lanes] = jnp.where(is_left, up_k, pltpu.roll(low_k, 64, 1)).astype(BF16)
            t2[1, k, :, lanes] = jnp.where(is_left, pltpu.roll(up_k, 64, 1), low_k).astype(BF16)
        t_copy(b).start()
        return carry

    def table_merge(b, carry):
        t_copy(b).wait_recv()
        lanes = pl.ds(pl.multiple_of(b * 128, 128), 128)
        for k in range(4):
            mine = t2[c, k, :, lanes].astype(F32) + t_core[k, :, lanes].astype(F32)
            t2[c, k, :, lanes] = mine.astype(BF16)
        return carry

    ring_t = Ring(y, y_right, y_left, lambda k: t2.at[c, k],
                  lambda ref, n: ref.at[:, pl.ds(256 * n, 256)], t_far, t_near,
                  ring_send.at[4], ring_recv.at[4])
    ring_t.make()
    lax.fori_loop(0, 3, table_block, 0)
    lax.fori_loop(0, 2, table_merge, 0)
    ring_t.start_half(0)
    lax.fori_loop(3, 4, table_block, 0)
    lax.fori_loop(2, 4, table_merge, 0)
    ring_t.start_half(1)

    total = s4[z].astype(F32)
    for k in range(1, 8):
        z_copy(k).wait_recv()
        total = total + zbuf[k].astype(F32)
    dense_ref[...] = total.astype(BF16)

    ring_t.forward(add_flat)
    ring_t.arrive()
    total = t2[c, y].astype(F32) + t_near[0].astype(F32) + t_near[1].astype(F32)
    table_ref[...] = total.astype(BF16)

    def sent(k, carry):
        req_copy(k).wait_send()
        for p in range(PAIRS):
            give_copy(p, k).wait_send()
        return carry

    lax.fori_loop(1, 32, sent, 0)
    for k in range(4):
        t_copy(k).wait_send()
    for k in range(1, 8):
        msg_copy(k).wait_send()
        z_copy(k).wait_send()
    for ring in (ring_a, ring_b, ring_a2, ring_b2, ring_t):
        ring.end()


def output_kernel(dense_ref, sums_ref, proj_ref, outw_ref, table_ref):
    proj_ref[...] = dense_ref[:, :384]
    outw_ref[...] = dense_ref[:, 384:]
    across = sums_ref[...].astype(F32).T.astype(BF16)
    for b in range(4):
        for half in range(2):
            part = across[b * 128 + half * 64 : b * 128 + half * 64 + 64]
            table_ref[:, half * 1024 + b * 256 : half * 1024 + (b + 1) * 256] = part


def run(*arrays):
    whole = pl.BlockSpec(memory_space=pltpu.VMEM)
    anywhere = pl.BlockSpec(memory_space=pl.ANY)
    dma = pltpu.SemaphoreType.DMA
    tokens = HIST * SEQ

    def buf(*shape):
        return pltpu.VMEM(shape, BF16)

    parts = pl.pallas_call(
        program_kernel,
        out_shape=(
            jax.ShapeDtypeStruct((32, 512), BF16),
            jax.ShapeDtypeStruct((256, 512), BF16),
        ),
        in_specs=[whole] * 4 + [anywhere] * 4,
        out_specs=(whole,) * 2,
        scratch_shapes=[
            buf(ROWS_DEV, EMB), buf(tokens, D), buf(D, PROJ), buf(D, D),
            pltpu.VMEM((HIST, 8, TOK), jnp.int32),
            pltpu.VMEM((HIST, 8, TOK), jnp.int32),
            pltpu.VMEM((N_TABLE, 1, TOK), jnp.int32),
            pltpu.VMEM((N_TABLE, 1, TOK), jnp.int32),
            pltpu.VMEM((SLOTS, TOK), F32),
            pltpu.VMEM((1, PAIRS * SLOTS), jnp.int32),
            pltpu.VMEM((PAIRS, 8, TOK), jnp.int32),
            pltpu.VMEM((PAIRS, TOK, 8), jnp.int32),
            buf(PAIRS, N_TABLE, 16, EMB), buf(PAIRS, N_TABLE, 16, EMB),
            buf(PAIRS, N_TABLE, 16, EMB),
            buf(D, tokens), buf(D, tokens), buf(tokens, PROJ),
            buf(2, 4, 4, 256, 512), buf(4, 4, 256, 512), pltpu.VMEM((ROWS_DEV, EMB), F32),
            buf(2, 2, CUT, 512), buf(2, 2, 256 - CUT, 512),
            buf(2, 4, CUT, 512), buf(2, 4, 256 - CUT, 512),
            buf(4, CUT, 512), buf(4, 256 - CUT, 512),
            buf(2, CUT // 2, 512), buf(2, (256 - CUT) // 2, 512),
            buf(2, CUT, 512), buf(2, 256 - CUT, 512),
            buf(8, 32, 512), buf(8, 32, 512),
            buf(4, 256, 512), buf(2, 256, 256), buf(2, 256, 512),
            dma((4,)), dma((8,)), dma((8,)), dma((32,)), dma((32,)),
            dma((PAIRS, 32)), dma((PAIRS, 32)), dma((PAIRS, 32)), dma((PAIRS, 32)),
            dma((8,)), dma((8,)), dma((5, 6)), dma((5, 6)), dma((8,)), dma((8,)),
        ],
        compiler_params=pltpu.CompilerParams(
            vmem_limit_bytes=VMEM_LIMIT, collective_id=0, has_side_effects=True
        ),
        name="whole_program",
    )(*arrays)
    return pl.pallas_call(
        output_kernel,
        out_shape=(
            jax.ShapeDtypeStruct((32, 384), BF16),
            jax.ShapeDtypeStruct((32, 128), BF16),
            jax.ShapeDtypeStruct((64, 2048), BF16),
        ),
        in_specs=[whole] * 2,
        out_specs=(whole,) * 3,
        name="outputs",
    )(*parts)


def body(
    embed_table, owner_shard, slot_row, lengths, send_order, proj_weight, out_weight, upstream
):
    proj, outw, table = run(
        jnp.swapaxes(owner_shard[..., 0], 1, 2), jnp.swapaxes(slot_row, 1, 2),
        lengths.reshape(1, HIST), send_order, embed_table, upstream.reshape(HIST * SEQ, D),
        proj_weight, out_weight,
    )
    return table.T, proj, outw


def solution(mesh):
    in_specs = (
        P("table", None),
        P(("dp", "table"), None, None, None),
        P(("dp", "table"), None, None),
        P(("dp", "table")),
        P(("dp", "table"), None),
        P(),
        P(),
        P(("dp", "table"), None, None),
    )
    out_specs = (P("table", "dp"), P("table", "dp"), P("table", "dp"))
    return jax.shard_map(body, mesh=mesh, in_specs=in_specs, out_specs=out_specs, check_vma=False)
```

```python
import functools

import jax
import jax.numpy as jnp
from jax import lax
from jax.experimental import pallas as pl
from jax.experimental.pallas import tpu as pltpu
from jax.sharding import PartitionSpec as P

D = 1024
EMB = 512
HEADS = 8
QK = 64
PROJ = 3072
SEQ = 64
HIST = 8
ROWS_DEV = 2048
MOST = 8
N_DP = 8
N_TABLE = 32
PAIRS = HIST // 2
TOK = 2 * SEQ
SLOTS = 2 * N_TABLE * MOST
EPSILON = 1e-06
SCALE = float(2048 * 64) ** (-0.5)
MESH = pl.DeviceIdType.MESH
VMEM_LIMIT = 60 * 1024 * 1024
CUT = 160
F32 = jnp.float32
BF16 = jnp.bfloat16


def mm(a, b):
    return lax.dot_general(a, b, (((1,), (0,)), ((), ())), preferred_element_type=F32)


def mm_nt(a, b):
    return lax.dot_general(a, b, (((1,), (1,)), ((), ())), preferred_element_type=F32)


def mm_tn(a, b):
    return lax.dot_general(a, b, (((0,), (0,)), ((), ())), preferred_element_type=F32)


def sigmoid(x):
    return 0.5 * jnp.tanh(0.5 * x) + 0.5


class Ring:
    def __init__(self, place, to_right, to_left, chunk, half, far, near, send, recv):
        self.place, self.right, self.left = place, to_right, to_left
        self.chunk, self.half, self.far, self.near = chunk, half, far, near
        self.send, self.recv = send, recv

    def copy(self, number, src, dst, device):
        return pltpu.make_async_remote_copy(
            src_ref=src, dst_ref=dst, send_sem=self.send.at[number], recv_sem=self.recv.at[number],
            device_id=device, device_id_type=MESH,
        )

    def make(self):
        across, after, ahead = (lax.rem(self.place + k, 4) for k in (2, 1, 3))
        self.after, self.ahead = after, ahead
        part, half, far, near = self.chunk, self.half, self.far, self.near
        self.copies = [
            self.copy(0, half(part(across), 0), far.at[0], self.right),
            self.copy(1, half(part(across), 1), far.at[1], self.left),
            self.copy(2, half(part(after), 1), half(near.at[0], 1), self.right),
            self.copy(3, half(part(ahead), 0), half(near.at[1], 0), self.left),
            self.copy(4, half(part(after), 0), half(near.at[0], 0), self.right),
            self.copy(5, half(part(ahead), 1), half(near.at[1], 1), self.left),
        ]

    def start_half(self, number):
        for k in ((0, 3), (1, 2))[number]:
            self.copies[k].start()

    def start(self):
        self.start_half(0)
        self.start_half(1)

    def forward(self, add):
        self.copies[0].wait_recv()
        add(self.half(self.chunk(self.after), 0), self.far.at[0])
        self.copies[4].start()
        self.copies[1].wait_recv()
        add(self.half(self.chunk(self.ahead), 1), self.far.at[1])
        self.copies[5].start()

    def arrive(self):
        for k in range(2, 6):
            self.copies[k].wait_recv()

    def end(self):
        for k in range(6):
            self.copies[k].wait_send()


def add_into(target, other):
    for n in range(target.shape[0]):
        target[n] = (target[n].astype(F32) + other[n].astype(F32)).astype(BF16)


def layer_pair(replies, cols, rows, upstream, wp, wo):
    item_at, action_at, length = cols[:, 0:1], cols[:, 1:2], cols[:, 2:3]
    places = lax.broadcasted_iota(jnp.int32, (TOK, SLOTS), 1)
    left = mm((places == item_at).astype(BF16), replies)
    right = mm((places == action_at).astype(BF16), replies)
    fetched = jnp.concatenate([left, right], axis=1)
    average = jnp.mean(fetched, axis=1, keepdims=True)
    centred = fetched - average
    rstd = lax.rsqrt(jnp.mean(centred * centred, axis=1, keepdims=True) + EPSILON)
    normed_full = centred * rstd
    normed = normed_full.astype(BF16)

    before = mm(normed, wp[...])
    gate = sigmoid(before)
    slope = gate * (1.0 + before * (1.0 - gate))
    projected = (before * gate).astype(BF16)
    u = projected[:, :D].astype(F32)
    values = projected[:, D : 2 * D]
    queries = projected[:, 2 * D : 2 * D + HEADS * QK]
    keys = projected[:, 2 * D + HEADS * QK :]

    at = lax.broadcasted_iota(jnp.int32, (TOK, TOK), 0)
    source = lax.broadcasted_iota(jnp.int32, (TOK, TOK), 1)
    seen = (source <= at) & ((at // SEQ) == (source // SEQ))
    share = jnp.where(seen, 1.0 / length.astype(F32), 0.0)
    parts = (source < QK, source >= QK)
    zero = jnp.zeros((TOK, TOK), BF16)

    weights, factors, attended = [], [], []
    for h in range(HEADS):
        two = slice((h // 2) * TOK, (h // 2 + 1) * TOK)
        key = jnp.where(parts[h % 2], keys[:, two], zero)
        score = mm_nt(queries[:, two], key)
        open_ = sigmoid(score)
        weight = (score * open_ * share).astype(BF16)
        weights.append(weight)
        factors.append(open_ * (1.0 + score * (1.0 - open_)) * share)
        attended.append(mm(weight, values[:, h * TOK : (h + 1) * TOK]))
    attended = jnp.concatenate(attended, axis=1)
    average = jnp.mean(attended, axis=1, keepdims=True)
    centred = attended - average
    spread = lax.rsqrt(jnp.mean(centred * centred, axis=1, keepdims=True) + EPSILON)
    inner = centred * spread
    mixed = inner * u

    place = lax.broadcasted_iota(jnp.int32, (TOK, D), 0) % SEQ
    top = jnp.where(place < length, upstream.astype(F32), 0.0)
    top_low = top.astype(BF16)
    grad_mixed = mm_nt(top_low, wo[...]).astype(BF16).astype(F32)
    grad_u = (grad_mixed * inner).astype(BF16)
    grad_inner = grad_mixed * u
    first = jnp.mean(grad_inner, axis=1, keepdims=True)
    second = jnp.mean(grad_inner * inner, axis=1, keepdims=True)
    grad_att = (spread * (grad_inner - first - inner * second)).astype(BF16)

    grad_v, grad_q, grad_k = [], [], []
    for h in range(HEADS):
        own = slice(h * TOK, (h + 1) * TOK)
        two = slice((h // 2) * TOK, (h // 2 + 1) * TOK)
        grad_weight = mm_nt(grad_att[:, own], values[:, own]).astype(BF16).astype(F32)
        grad_v.append(mm_tn(weights[h], grad_att[:, own]).astype(BF16))
        grad_score = (grad_weight * factors[h]).astype(BF16)
        key = jnp.where(parts[h % 2], keys[:, two], zero)
        query = jnp.where(parts[h % 2], queries[:, two], zero)
        gq = mm(grad_score, key)
        gk = mm_tn(grad_score, query)
        if h % 2:
            grad_q[-1] = (grad_q[-1] + gq).astype(BF16)
            grad_k[-1] = (grad_k[-1] + gk).astype(BF16)
        else:
            grad_q.append(gq)
            grad_k.append(gk)
    grad_projected = jnp.concatenate([grad_u] + grad_v + grad_q + grad_k, axis=1)
    grad_before = (grad_projected.astype(F32) * slope).astype(BF16)
    grad_normed = mm_nt(grad_before, wp[...])
    first = jnp.mean(grad_normed, axis=1, keepdims=True)
    second = jnp.mean(grad_normed * normed_full, axis=1, keepdims=True)
    grad_rows = (top + rstd * (grad_normed - first - normed_full * second)).astype(BF16)

    slots = lax.broadcasted_iota(jnp.int32, (SLOTS, TOK), 0)
    back = mm((slots == rows[0:1, :]).astype(BF16), grad_rows[:, :EMB])
    back = back + mm((slots == rows[1:2, :]).astype(BF16), grad_rows[:, EMB:])
    return normed_full.T.astype(BF16), mixed.T.astype(BF16), top_low, grad_before, back.astype(BF16)


def split_number(numbers):
    high = numbers // 256
    return (numbers - 256 * high).astype(BF16), high.astype(BF16)


def program_kernel(
    owner_ref, slot_ref, length_ref, order_ref, table_hbm, up_hbm, wp_hbm, wo_hbm,
    dense_ref, table_ref,
    table, up, wp, wo, msg_out, msg_in, req_out, req_in, wanted, req_rows, rows_s, cols_s,
    picked, replies, incoming, normed_t, mixed_t, gbs,
    g, core_buf, sums, far_a, far_b, near_a, near_b, sum_a, sum_b,
    far_a2, far_b2, near_a2, near_b2, s4, zbuf, t_core, t_far, t_near,
    load_sem, m_send, m_recv, r_send, r_recv, f_send, f_recv, a_send, a_recv,
    core_send, core_recv, ring_send, ring_recv, z_send, z_recv,
):
    dp = lax.axis_index("dp")
    tab = lax.axis_index("table")
    y, c = dp // 2, dp % 2
    x, z = tab // 8, tab % 8
    other = (2 * y + 1 - c, tab)
    y_right = (2 * lax.rem(y + 1, 4) + c, tab)
    y_left = (2 * lax.rem(y + 3, 4) + c, tab)
    x_right = (dp, lax.rem(tab + 8, 32))
    x_left = (dp, lax.rem(tab + 24, 32))

    loads = [
        pltpu.make_async_copy(src, dst, load_sem.at[n])
        for n, (src, dst) in enumerate(
            ((table_hbm, table), (up_hbm, up), (wp_hbm, wp), (wo_hbm, wo))
        )
    ]
    for load in loads:
        load.start()

    barrier = pltpu.get_barrier_semaphore()

    def greet_dp(k, carry):
        pl.semaphore_signal(
            barrier, inc=1, device_id=(lax.rem(dp + k, 8), tab), device_id_type=MESH
        )
        return carry

    def greet_table(k, carry):
        pl.semaphore_signal(
            barrier, inc=1, device_id=(dp, lax.rem(tab + k, 32)), device_id_type=MESH
        )
        return carry

    lax.fori_loop(1, 8, greet_dp, 0)
    lax.fori_loop(1, 32, greet_table, 0)

    order = order_ref[...]
    rows_of_table = [owner_ref[m] * ROWS_DEV + slot_ref[m] for m in range(HIST)]
    for k in range(HIST):
        at = order[:, k : k + 1]
        lookups = jnp.zeros((2, SEQ), jnp.int32)
        length = jnp.zeros((1, 1), jnp.int32)
        for m in range(HIST):
            lookups = jnp.where(jnp.broadcast_to(at, (2, SEQ)) == m, rows_of_table[m], lookups)
            length = jnp.where(at == m, length_ref[:, m : m + 1], length)
        msg_out[k, 0:2, 0:SEQ] = lookups
        msg_out[k, 2:3, 0:SEQ] = jnp.broadcast_to(length, (1, SEQ))
    pl.semaphore_wait(barrier, 38)

    def msg_copy(k):
        peer = lax.rem(dp + k, 8)
        return pltpu.make_async_remote_copy(
            src_ref=msg_out.at[peer], dst_ref=msg_in.at[dp],
            send_sem=m_send.at[k], recv_sem=m_recv.at[k],
            device_id=(peer, tab), device_id_type=MESH,
        )

    for k in range(1, 8):
        msg_copy(k).start()
    msg_in[dp] = msg_out[dp]
    for k in range(1, 8):
        msg_copy(k).wait_recv()

    items = jnp.concatenate([msg_in[k, 0:1, :] for k in range(HIST)], axis=0)
    actions = jnp.concatenate([msg_in[k, 1:2, :] for k in range(HIST)], axis=0)
    lengths = jnp.concatenate([msg_in[k, 2:3, :] for k in range(HIST)], axis=0)[:, 0:1]
    is_item = lax.broadcasted_iota(jnp.int32, (HIST, TOK), 1) < SEQ
    ids = jnp.where(is_item, items, pltpu.roll(actions, SEQ, 1))
    owner = ids // ROWS_DEV
    ids_col = ids.astype(F32).T.astype(jnp.int32)
    owner_col, row_col = ids_col // ROWS_DEV, ids_col % ROWS_DEV
    sub = lax.broadcasted_iota(jnp.int32, (TOK, TOK), 0)
    lane = lax.broadcasted_iota(jnp.int32, (TOK, TOK), 1)
    ranks = []
    for m in range(HIST):
        same = (owner_col[:, m : m + 1] == owner[m : m + 1, :]) & (sub < lane)
        ranks.append(jnp.sum(jnp.where(same, 1.0, 0.0), axis=0, keepdims=True))
    rank = jnp.concatenate(ranks, axis=0)
    rank_col = rank.T.astype(jnp.int32)
    request = jnp.zeros((N_TABLE, TOK), F32)
    owners = lax.broadcasted_iota(jnp.int32, (N_TABLE, TOK), 0)
    for m in range(HIST):
        low, high = split_number(row_col[:, m : m + 1] + 1)
        spot = m * MOST + rank_col[:, m : m + 1]
        put = jnp.where(lane == spot, low.astype(F32), 0.0)
        put = jnp.where(lane == spot + 64, high.astype(F32), put)
        request = request + mm((owners == owner[m : m + 1, :]).astype(BF16), put.astype(BF16))
    request = request + 256.0 * pltpu.roll(request, 64, 1)
    request = jnp.where(owners >= 0, request, 0.0)
    request = jnp.where(lax.broadcasted_iota(jnp.int32, (N_TABLE, TOK), 1) < 64, request, 0.0)
    request = request.astype(jnp.int32)
    for o in range(N_TABLE):
        req_out[o] = request[o : o + 1, :]

    def req_copy(k):
        peer = lax.rem(tab + k, 32)
        return pltpu.make_async_remote_copy(
            src_ref=req_out.at[peer], dst_ref=req_in.at[tab],
            send_sem=r_send.at[k], recv_sem=r_recv.at[k],
            device_id=(dp, peer), device_id_type=MESH,
        )

    def ask(k, carry):
        req_copy(k).start()
        return carry

    lax.fori_loop(1, 32, ask, 0)
    req_in[tab] = req_out[tab]

    slot = owner * 16 + rank.astype(jnp.int32)
    first_half = lax.broadcasted_iota(jnp.int32, (1, TOK), 1) < SEQ
    for p in range(PAIRS):
        a = slot[2 * p : 2 * p + 1, :]
        b = slot[2 * p + 1 : 2 * p + 2, :] + MOST
        item = jnp.where(first_half, a, pltpu.roll(b, SEQ, 1))
        action = jnp.where(first_half, pltpu.roll(a, SEQ, 1), b)
        length = jnp.where(first_half, lengths[2 * p : 2 * p + 1], lengths[2 * p + 1 : 2 * p + 2])
        block = jnp.concatenate([item, action, length, length] * 2, axis=0)
        rows_s[p] = block
        cols_s[p] = block.astype(F32).T.astype(jnp.int32)

    def asked(k, carry):
        req_copy(k).wait_recv()
        return carry

    lax.fori_loop(1, 32, asked, 0)
    asks = jnp.concatenate([req_in[k] for k in range(N_TABLE)], axis=0)
    low, high = split_number(asks)
    tall = lax.broadcasted_iota(jnp.int32, (SLOTS, N_TABLE), 0) // 16
    tall = (tall == lax.broadcasted_iota(jnp.int32, (SLOTS, N_TABLE), 1)).astype(BF16)
    wanted[...] = mm(tall, low) + 256.0 * mm(tall, high) - 1.0
    wide = lax.broadcasted_iota(jnp.int32, (N_TABLE, SLOTS), 1) // 16
    wide = (wide == lax.broadcasted_iota(jnp.int32, (N_TABLE, SLOTS), 0)).astype(BF16)
    across = mm_tn(low, wide) + 256.0 * mm_tn(high, wide) - 1.0
    at = lax.broadcasted_iota(jnp.int32, (TOK, SLOTS), 0)
    in_owner = lax.broadcasted_iota(jnp.int32, (TOK, SLOTS), 1) % 16
    for p in range(PAIRS):
        line = jnp.sum(jnp.where(at == in_owner + 16 * p, across, 0.0), axis=0, keepdims=True)
        req_rows[:, p * SLOTS : (p + 1) * SLOTS] = line.astype(jnp.int32)

    def fetch_copy(p, k):
        peer = lax.rem(tab + k, 32)
        return pltpu.make_async_remote_copy(
            src_ref=picked.at[p, peer], dst_ref=replies.at[p, tab],
            send_sem=f_send.at[p, k], recv_sem=f_recv.at[p, k],
            device_id=(dp, peer), device_id_type=MESH,
        )

    loads[0].wait()

    def serve(p, carry):
        at = lax.broadcasted_iota(jnp.int32, (SLOTS, TOK), 0) % 16 + 16 * p
        seen = lax.broadcasted_iota(jnp.int32, (SLOTS, TOK), 1) == at
        line = jnp.sum(jnp.where(seen, wanted[...], 0.0), axis=1, keepdims=True)
        line = line.astype(jnp.int32)
        places = lax.broadcasted_iota(jnp.int32, (SLOTS, ROWS_DEV), 1)
        chosen = (places == line).astype(BF16)
        picked[p] = mm(chosen, table[...]).astype(BF16).reshape(N_TABLE, 16, EMB)

        def start(k, inner):
            fetch_copy(p, k).start()
            return inner

        lax.fori_loop(1, 32, start, 0)
        replies[p, tab] = picked[p, tab]
        return carry

    lax.fori_loop(0, PAIRS, serve, 0)

    outgoing = picked

    def give_copy(p, k):
        peer = lax.rem(tab + k, 32)
        return pltpu.make_async_remote_copy(
            src_ref=outgoing.at[p, peer], dst_ref=incoming.at[p, tab],
            send_sem=a_send.at[p, k], recv_sem=a_recv.at[p, k],
            device_id=(dp, peer), device_id_type=MESH,
        )

    for load in loads[1:]:
        load.wait()

    def give(n, carry):
        give_copy(n // 31, n % 31 + 1).start()
        return carry

    def fetched(p):
        def landed(k, carry):
            fetch_copy(p, k).wait_recv()
            fetch_copy(p, k).wait_send()
            return carry

        lax.fori_loop(1, 32, landed, 0)

    def pair(p, carry):
        fetched(p)

        @pl.when(p == PAIRS - 1)
        def _():
            lax.fori_loop(0, (PAIRS - 1) * 31, give, 0)

        tokens = pl.ds(pl.multiple_of(p * TOK, TOK), TOK)
        normed_p, mixed_p, top_p, before_p, back = layer_pair(
            replies[p].reshape(SLOTS, EMB), cols_s[p], rows_s[p], up[tokens, :], wp, wo
        )
        outgoing[p] = back.reshape(N_TABLE, 16, EMB)
        incoming[p, tab] = outgoing[p, tab]
        normed_t[:, tokens] = normed_p
        mixed_t[:, tokens] = mixed_p
        up[tokens, :] = top_p
        gbs[tokens, :] = before_p
        return carry

    lax.fori_loop(0, PAIRS, pair, 0)
    lax.fori_loop((PAIRS - 1) * 31, PAIRS * 31, give, 0)

    def core_copy(k):
        return pltpu.make_async_remote_copy(
            src_ref=g.at[0, k], dst_ref=core_buf.at[k],
            send_sem=core_send.at[k], recv_sem=core_recv.at[k],
            device_id=other, device_id_type=MESH,
        )

    s1 = g.at[1]
    t2 = g.at[0]

    def merge(k):
        core_copy(k).wait_recv()
        core_copy(k).wait_send()

        def step(n, inner):
            s1[k, n] = (s1[k, n].astype(F32) + core_buf[k, n].astype(F32)).astype(BF16)
            return inner

        lax.fori_loop(0, 4, step, 0)

    def two(ref, n):
        return ref.at[pl.ds(2 * n, 2)]

    def add_flat(target, other_ref):
        target[...] = (target[...].astype(F32) + other_ref[...].astype(F32)).astype(BF16)

    def chosen_rows(p, first, count):
        places = lax.broadcasted_iota(jnp.int32, (count, SLOTS), 0) + first
        return (places == req_rows[:, p * SLOTS : (p + 1) * SLOTS]).astype(BF16)

    def take_in(p):
        def given(k, carry):
            give_copy(p, k).wait_recv()
            return carry

        lax.fori_loop(1, 32, given, 0)

    def add_rows(p):
        take_in(p)

        def block(b, carry):
            first = b * 512
            part = mm(chosen_rows(p, first, 512), incoming[p].reshape(SLOTS, EMB))
            rows = pl.ds(pl.multiple_of(first, 512), 512)
            sums[rows, :] = part if p == 0 else sums[rows, :] + part
            return carry

        lax.fori_loop(0, 4, block, 0)

    ring_a = Ring(y, y_right, y_left, lambda k: s1.at[k, :, pl.ds(0, CUT), :], two, far_a, near_a,
                  ring_send.at[0], ring_recv.at[0])
    ring_b = Ring(x, x_right, x_left, lambda k: s1.at[:, k, pl.ds(CUT, 256 - CUT), :], two, far_b,
                  near_b, ring_send.at[1], ring_recv.at[1])
    ring_a.make()

    def chunk_at(n):
        return lax.rem(y + 2 + n + (n // 2) * (1 - 2 * (n % 2)), 4)

    def terms(n, carry):
        k = chunk_at(n)
        first = mm(normed_t[...], gbs[:, pl.ds(pl.multiple_of(k * 768, 768), 768)]) * SCALE
        second = mm(mixed_t[...], up[:, pl.ds(pl.multiple_of(k * 256, 256), 256)]) * SCALE
        for which, kept in ((0, 1 - c), (1, c)):
            one = first[:, which * 384 : (which + 1) * 384].astype(BF16)
            two_ = second[:, which * 128 : (which + 1) * 128].astype(BF16)
            g[kept, k, :, :, 0:384] = one.reshape(4, 256, 384)
            g[kept, k, :, :, 384:512] = two_.reshape(4, 256, 128)
        core_copy(k).start()

        @pl.when(n > 0)
        def _():
            merge(chunk_at(n - 1))

        @pl.when(n == 1)
        def _():
            ring_a.copies[0].start()
            ring_a.copies[1].start()

        @pl.when(n == 2)
        def _():
            ring_a.copies[3].start()

        @pl.when(n == 3)
        def _():
            ring_a.copies[2].start()

        return carry

    lax.fori_loop(0, 4, terms, 0)
    merge(y)
    ring_b.make()
    ring_b.start()
    add_rows(0)
    ring_a.forward(add_into)
    add_rows(1)
    ring_b.forward(add_into)
    ring_a.arrive()
    for n in range(4):
        sum_a[n] = (
            s1[y, n, 0:CUT, :].astype(F32) + near_a[0, n].astype(F32) + near_a[1, n].astype(F32)
        ).astype(BF16)
    ring_a2 = Ring(x, x_right, x_left, lambda k: sum_a.at[k],
                   lambda ref, n: ref.at[pl.ds(CUT // 2 * n, CUT // 2), :], far_a2, near_a2,
                   ring_send.at[2], ring_recv.at[2])
    ring_a2.make()
    ring_a2.start()
    ring_b.arrive()
    for n in range(4):
        sum_b[n] = (
            s1[n, x, CUT:256, :].astype(F32) + near_b[0, n].astype(F32) + near_b[1, n].astype(F32)
        ).astype(BF16)
    ring_b2 = Ring(y, y_right, y_left, lambda k: sum_b.at[k],
                   lambda ref, n: ref.at[pl.ds((256 - CUT) // 2 * n, (256 - CUT) // 2), :],
                   far_b2, near_b2, ring_send.at[3], ring_recv.at[3])
    ring_b2.make()
    ring_b2.start()
    ring_a2.forward(add_flat)
    ring_b2.forward(add_flat)
    add_rows(2)
    ring_a2.arrive()
    total = sum_a[x].astype(F32) + near_a2[0].astype(F32) + near_a2[1].astype(F32)
    s4[0 : CUT // 32] = total.astype(BF16).reshape(CUT // 32, 32, 512)
    ring_b2.arrive()
    total = sum_b[y].astype(F32) + near_b2[0].astype(F32) + near_b2[1].astype(F32)
    s4[CUT // 32 : 8] = total.astype(BF16).reshape(8 - CUT // 32, 32, 512)

    def z_copy(k):
        peer = lax.rem(z + k, 8)
        return pltpu.make_async_remote_copy(
            src_ref=s4.at[peer], dst_ref=zbuf.at[k],
            send_sem=z_send.at[k], recv_sem=z_recv.at[k],
            device_id=(dp, 8 * x + peer), device_id_type=MESH,
        )

    for k in range(1, 8):
        z_copy(k).start()

    take_in(PAIRS - 1)

    def rows_of(first):
        part = mm(chosen_rows(PAIRS - 1, first, 256), incoming[PAIRS - 1].reshape(SLOTS, EMB))
        rows = pl.ds(pl.multiple_of(first, 256), 256)
        return (sums[rows, :] + part).astype(BF16).astype(F32)

    def t_copy(b):
        lanes = pl.ds(pl.multiple_of(b * 128, 128), 128)
        return pltpu.make_async_remote_copy(
            src_ref=t2.at[1 - c, :, :, lanes], dst_ref=t_core.at[:, :, lanes],
            send_sem=core_send.at[4 + b], recv_sem=core_recv.at[4 + b],
            device_id=other, device_id_type=MESH,
        )

    def table_block(b, carry):
        upper = rows_of(b * 256)
        lower = rows_of(b * 256 + 1024)
        lanes = pl.ds(pl.multiple_of(b * 128, 128), 128)
        is_left = lax.broadcasted_iota(jnp.int32, (256, 128), 1) < 64
        for k in range(4):
            up_k, low_k = upper[:, k * 128 : (k + 1) * 128], lower[:, k * 128 : (k + 1) * 128]
            t2[0, k, :, lanes] = jnp.where(is_left, up_k, pltpu.roll(low_k, 64, 1)).astype(BF16)
            t2[1, k, :, lanes] = jnp.where(is_left, pltpu.roll(up_k, 64, 1), low_k).astype(BF16)
        t_copy(b).start()
        return carry

    def table_merge(b, carry):
        t_copy(b).wait_recv()
        lanes = pl.ds(pl.multiple_of(b * 128, 128), 128)
        for k in range(4):
            mine = t2[c, k, :, lanes].astype(F32) + t_core[k, :, lanes].astype(F32)
            t2[c, k, :, lanes] = mine.astype(BF16)
        return carry

    ring_t = Ring(y, y_right, y_left, lambda k: t2.at[c, k],
                  lambda ref, n: ref.at[:, pl.ds(256 * n, 256)], t_far, t_near,
                  ring_send.at[4], ring_recv.at[4])
    ring_t.make()
    lax.fori_loop(0, 3, table_block, 0)
    lax.fori_loop(0, 2, table_merge, 0)
    ring_t.start_half(0)
    lax.fori_loop(3, 4, table_block, 0)
    lax.fori_loop(2, 4, table_merge, 0)
    ring_t.start_half(1)

    ring_t.forward(add_flat)
    total = s4[z].astype(F32)
    for k in range(1, 8):
        z_copy(k).wait_recv()
        total = total + zbuf[k].astype(F32)
    dense_ref[...] = total.astype(BF16)
    ring_t.arrive()
    total = t2[c, y].astype(F32) + t_near[0].astype(F32) + t_near[1].astype(F32)
    table_ref[...] = total.astype(BF16)

    def sent(k, carry):
        req_copy(k).wait_send()
        for p in range(PAIRS):
            give_copy(p, k).wait_send()
        return carry

    lax.fori_loop(1, 32, sent, 0)
    for k in range(4):
        t_copy(k).wait_send()
    for k in range(1, 8):
        msg_copy(k).wait_send()
        z_copy(k).wait_send()
    for ring in (ring_a, ring_b, ring_a2, ring_b2, ring_t):
        ring.end()


def output_kernel(dense_ref, sums_ref, proj_ref, outw_ref, table_ref):
    proj_ref[...] = dense_ref[:, :384]
    outw_ref[...] = dense_ref[:, 384:]
    across = sums_ref[...].astype(F32).T.astype(BF16)
    for b in range(4):
        for half in range(2):
            part = across[b * 128 + half * 64 : b * 128 + half * 64 + 64]
            table_ref[:, half * 1024 + b * 256 : half * 1024 + (b + 1) * 256] = part


def run(*arrays):
    whole = pl.BlockSpec(memory_space=pltpu.VMEM)
    anywhere = pl.BlockSpec(memory_space=pl.ANY)
    dma = pltpu.SemaphoreType.DMA
    tokens = HIST * SEQ

    def buf(*shape):
        return pltpu.VMEM(shape, BF16)

    parts = pl.pallas_call(
        program_kernel,
        out_shape=(
            jax.ShapeDtypeStruct((32, 512), BF16),
            jax.ShapeDtypeStruct((256, 512), BF16),
        ),
        in_specs=[whole] * 4 + [anywhere] * 4,
        out_specs=(whole,) * 2,
        scratch_shapes=[
            buf(ROWS_DEV, EMB), buf(tokens, D), buf(D, PROJ), buf(D, D),
            pltpu.VMEM((HIST, 8, TOK), jnp.int32),
            pltpu.VMEM((HIST, 8, TOK), jnp.int32),
            pltpu.VMEM((N_TABLE, 1, TOK), jnp.int32),
            pltpu.VMEM((N_TABLE, 1, TOK), jnp.int32),
            pltpu.VMEM((SLOTS, TOK), F32),
            pltpu.VMEM((1, PAIRS * SLOTS), jnp.int32),
            pltpu.VMEM((PAIRS, 8, TOK), jnp.int32),
            pltpu.VMEM((PAIRS, TOK, 8), jnp.int32),
            buf(PAIRS, N_TABLE, 16, EMB), buf(PAIRS, N_TABLE, 16, EMB),
            buf(PAIRS, N_TABLE, 16, EMB),
            buf(D, tokens), buf(D, tokens), buf(tokens, PROJ),
            buf(2, 4, 4, 256, 512), buf(4, 4, 256, 512), pltpu.VMEM((ROWS_DEV, EMB), F32),
            buf(2, 2, CUT, 512), buf(2, 2, 256 - CUT, 512),
            buf(2, 4, CUT, 512), buf(2, 4, 256 - CUT, 512),
            buf(4, CUT, 512), buf(4, 256 - CUT, 512),
            buf(2, CUT // 2, 512), buf(2, (256 - CUT) // 2, 512),
            buf(2, CUT, 512), buf(2, 256 - CUT, 512),
            buf(8, 32, 512), buf(8, 32, 512),
            buf(4, 256, 512), buf(2, 256, 256), buf(2, 256, 512),
            dma((4,)), dma((8,)), dma((8,)), dma((32,)), dma((32,)),
            dma((PAIRS, 32)), dma((PAIRS, 32)), dma((PAIRS, 32)), dma((PAIRS, 32)),
            dma((8,)), dma((8,)), dma((5, 6)), dma((5, 6)), dma((8,)), dma((8,)),
        ],
        compiler_params=pltpu.CompilerParams(
            vmem_limit_bytes=VMEM_LIMIT, collective_id=0, has_side_effects=True
        ),
        name="whole_program",
    )(*arrays)
    return pl.pallas_call(
        output_kernel,
        out_shape=(
            jax.ShapeDtypeStruct((32, 384), BF16),
            jax.ShapeDtypeStruct((32, 128), BF16),
            jax.ShapeDtypeStruct((64, 2048), BF16),
        ),
        in_specs=[whole] * 2,
        out_specs=(whole,) * 3,
        name="outputs",
    )(*parts)


def body(
    embed_table, owner_shard, slot_row, lengths, send_order, proj_weight, out_weight, upstream
):
    proj, outw, table = run(
        jnp.swapaxes(owner_shard[..., 0], 1, 2), jnp.swapaxes(slot_row, 1, 2),
        lengths.reshape(1, HIST), send_order, embed_table, upstream.reshape(HIST * SEQ, D),
        proj_weight, out_weight,
    )
    return table.T, proj, outw


def solution(mesh):
    in_specs = (
        P("table", None),
        P(("dp", "table"), None, None, None),
        P(("dp", "table"), None, None),
        P(("dp", "table")),
        P(("dp", "table"), None),
        P(),
        P(),
        P(("dp", "table"), None, None),
    )
    out_specs = (P("table", "dp"), P("table", "dp"), P("table", "dp"))
    return jax.shard_map(body, mesh=mesh, in_specs=in_specs, out_specs=out_specs, check_vma=False)
```

```python
import functools

import jax
import jax.numpy as jnp
from jax import lax
from jax.experimental import pallas as pl
from jax.experimental.pallas import tpu as pltpu
from jax.sharding import PartitionSpec as P

D = 1024
EMB = 512
HEADS = 8
QK = 64
PROJ = 3072
SEQ = 64
HIST = 8
ROWS_DEV = 2048
MOST = 8
N_DP = 8
N_TABLE = 32
PAIRS = HIST // 2
TOK = 2 * SEQ
SLOTS = 2 * N_TABLE * MOST
EPSILON = 1e-06
SCALE = float(2048 * 64) ** (-0.5)
MESH = pl.DeviceIdType.MESH
VMEM_LIMIT = 60 * 1024 * 1024
STREAMS = ((0, 96, True), (96, 96, True), (192, 64, False))
F32 = jnp.float32
BF16 = jnp.bfloat16


def mm(a, b):
    return lax.dot_general(a, b, (((1,), (0,)), ((), ())), preferred_element_type=F32)


def mm_nt(a, b):
    return lax.dot_general(a, b, (((1,), (1,)), ((), ())), preferred_element_type=F32)


def mm_tn(a, b):
    return lax.dot_general(a, b, (((0,), (0,)), ((), ())), preferred_element_type=F32)


def sigmoid(x):
    return 0.5 * jnp.tanh(0.5 * x) + 0.5


class Ring:
    def __init__(self, place, to_right, to_left, chunk, half, far, near, send, recv):
        self.place, self.right, self.left = place, to_right, to_left
        self.chunk, self.half, self.far, self.near = chunk, half, far, near
        self.send, self.recv = send, recv

    def copy(self, number, src, dst, device):
        return pltpu.make_async_remote_copy(
            src_ref=src, dst_ref=dst, send_sem=self.send.at[number], recv_sem=self.recv.at[number],
            device_id=device, device_id_type=MESH,
        )

    def make(self):
        across, after, ahead = (lax.rem(self.place + k, 4) for k in (2, 1, 3))
        self.after, self.ahead = after, ahead
        part, half, far, near = self.chunk, self.half, self.far, self.near
        self.copies = [
            self.copy(0, half(part(across), 0), far.at[0], self.right),
            self.copy(1, half(part(across), 1), far.at[1], self.left),
            self.copy(2, half(part(after), 1), half(near.at[0], 1), self.right),
            self.copy(3, half(part(ahead), 0), half(near.at[1], 0), self.left),
            self.copy(4, half(part(after), 0), half(near.at[0], 0), self.right),
            self.copy(5, half(part(ahead), 1), half(near.at[1], 1), self.left),
        ]

    def start_half(self, number):
        for k in ((0, 3), (1, 2))[number]:
            self.copies[k].start()

    def start(self):
        self.start_half(0)
        self.start_half(1)

    def forward(self, add):
        self.copies[0].wait_recv()
        add(self.half(self.chunk(self.after), 0), self.far.at[0])
        self.copies[4].start()
        self.copies[1].wait_recv()
        add(self.half(self.chunk(self.ahead), 1), self.far.at[1])
        self.copies[5].start()

    def arrive(self):
        for k in range(2, 6):
            self.copies[k].wait_recv()

    def end(self):
        for k in range(6):
            self.copies[k].wait_send()


def add_into(target, other):
    for n in range(target.shape[0]):
        target[n] = (target[n].astype(F32) + other[n].astype(F32)).astype(BF16)


def layer_pair(replies, cols, rows, upstream, wp, wo):
    item_at, action_at, length = cols[:, 0:1], cols[:, 1:2], cols[:, 2:3]
    places = lax.broadcasted_iota(jnp.int32, (TOK, SLOTS), 1)
    left = mm((places == item_at).astype(BF16), replies)
    right = mm((places == action_at).astype(BF16), replies)
    fetched = jnp.concatenate([left, right], axis=1)
    average = jnp.mean(fetched, axis=1, keepdims=True)
    centred = fetched - average
    rstd = lax.rsqrt(jnp.mean(centred * centred, axis=1, keepdims=True) + EPSILON)
    normed_full = centred * rstd
    normed = normed_full.astype(BF16)

    before = mm(normed, wp[...])
    gate = sigmoid(before)
    slope = gate * (1.0 + before * (1.0 - gate))
    projected = (before * gate).astype(BF16)
    u = projected[:, :D].astype(F32)
    values = projected[:, D : 2 * D]
    queries = projected[:, 2 * D : 2 * D + HEADS * QK]
    keys = projected[:, 2 * D + HEADS * QK :]

    at = lax.broadcasted_iota(jnp.int32, (TOK, TOK), 0)
    source = lax.broadcasted_iota(jnp.int32, (TOK, TOK), 1)
    seen = (source <= at) & ((at // SEQ) == (source // SEQ))
    share = jnp.where(seen, 1.0 / length.astype(F32), 0.0)
    parts = (source < QK, source >= QK)
    zero = jnp.zeros((TOK, TOK), BF16)

    weights, factors, attended = [], [], []
    for h in range(HEADS):
        two = slice((h // 2) * TOK, (h // 2 + 1) * TOK)
        key = jnp.where(parts[h % 2], keys[:, two], zero)
        score = mm_nt(queries[:, two], key)
        open_ = sigmoid(score)
        weight = (score * open_ * share).astype(BF16)
        weights.append(weight)
        factors.append(open_ * (1.0 + score * (1.0 - open_)) * share)
        attended.append(mm(weight, values[:, h * TOK : (h + 1) * TOK]))
    attended = jnp.concatenate(attended, axis=1)
    average = jnp.mean(attended, axis=1, keepdims=True)
    centred = attended - average
    spread = lax.rsqrt(jnp.mean(centred * centred, axis=1, keepdims=True) + EPSILON)
    inner = centred * spread
    mixed = inner * u

    place = lax.broadcasted_iota(jnp.int32, (TOK, D), 0) % SEQ
    top = jnp.where(place < length, upstream.astype(F32), 0.0)
    top_low = top.astype(BF16)
    grad_mixed = mm_nt(top_low, wo[...]).astype(BF16).astype(F32)
    grad_u = (grad_mixed * inner).astype(BF16)
    grad_inner = grad_mixed * u
    first = jnp.mean(grad_inner, axis=1, keepdims=True)
    second = jnp.mean(grad_inner * inner, axis=1, keepdims=True)
    grad_att = (spread * (grad_inner - first - inner * second)).astype(BF16)

    grad_v, grad_q, grad_k = [], [], []
    for h in range(HEADS):
        own = slice(h * TOK, (h + 1) * TOK)
        two = slice((h // 2) * TOK, (h // 2 + 1) * TOK)
        grad_weight = mm_nt(grad_att[:, own], values[:, own]).astype(BF16).astype(F32)
        grad_v.append(mm_tn(weights[h], grad_att[:, own]).astype(BF16))
        grad_score = (grad_weight * factors[h]).astype(BF16)
        key = jnp.where(parts[h % 2], keys[:, two], zero)
        query = jnp.where(parts[h % 2], queries[:, two], zero)
        gq = mm(grad_score, key)
        gk = mm_tn(grad_score, query)
        if h % 2:
            grad_q[-1] = (grad_q[-1] + gq).astype(BF16)
            grad_k[-1] = (grad_k[-1] + gk).astype(BF16)
        else:
            grad_q.append(gq)
            grad_k.append(gk)
    grad_projected = jnp.concatenate([grad_u] + grad_v + grad_q + grad_k, axis=1)
    grad_before = (grad_projected.astype(F32) * slope).astype(BF16)
    grad_normed = mm_nt(grad_before, wp[...])
    first = jnp.mean(grad_normed, axis=1, keepdims=True)
    second = jnp.mean(grad_normed * normed_full, axis=1, keepdims=True)
    grad_rows = (top + rstd * (grad_normed - first - normed_full * second)).astype(BF16)

    slots = lax.broadcasted_iota(jnp.int32, (SLOTS, TOK), 0)
    back = mm((slots == rows[0:1, :]).astype(BF16), grad_rows[:, :EMB])
    back = back + mm((slots == rows[1:2, :]).astype(BF16), grad_rows[:, EMB:])
    return normed_full.T.astype(BF16), mixed.T.astype(BF16), top_low, grad_before, back.astype(BF16)


def split_number(numbers):
    high = numbers // 256
    return (numbers - 256 * high).astype(BF16), high.astype(BF16)


def program_kernel(
    owner_ref, slot_ref, length_ref, order_ref, table_hbm, up_hbm, wp_hbm, wo_hbm,
    dense_ref, table_ref,
    table, up, wp, wo, msg_out, msg_in, req_out, req_in, wanted, req_rows, rows_s, cols_s,
    picked, replies, incoming, normed_t, mixed_t, gbs,
    g, core_buf, sums, far_1, far_2, far_3, near_1, near_2, near_3, sum_1, sum_2, sum_3,
    last_far_1, last_far_2, last_far_3, last_near_1, last_near_2, last_near_3,
    s4, zbuf, t_core, t_far, t_near,
    load_sem, m_send, m_recv, r_send, r_recv, f_send, f_recv, a_send, a_recv,
    core_send, core_recv, ring_send, ring_recv, z_send, z_recv,
):
    dp = lax.axis_index("dp")
    tab = lax.axis_index("table")
    y, c = dp // 2, dp % 2
    x, z = tab // 8, tab % 8
    other = (2 * y + 1 - c, tab)
    y_right = (2 * lax.rem(y + 1, 4) + c, tab)
    y_left = (2 * lax.rem(y + 3, 4) + c, tab)
    x_right = (dp, lax.rem(tab + 8, 32))
    x_left = (dp, lax.rem(tab + 24, 32))

    loads = [
        pltpu.make_async_copy(src, dst, load_sem.at[n])
        for n, (src, dst) in enumerate(
            ((table_hbm, table), (up_hbm, up), (wp_hbm, wp), (wo_hbm, wo))
        )
    ]
    for load in loads:
        load.start()

    barrier = pltpu.get_barrier_semaphore()

    def greet_dp(k, carry):
        pl.semaphore_signal(
            barrier, inc=1, device_id=(lax.rem(dp + k, 8), tab), device_id_type=MESH
        )
        return carry

    def greet_table(k, carry):
        pl.semaphore_signal(
            barrier, inc=1, device_id=(dp, lax.rem(tab + k, 32)), device_id_type=MESH
        )
        return carry

    lax.fori_loop(1, 8, greet_dp, 0)
    lax.fori_loop(1, 32, greet_table, 0)

    order = order_ref[...]
    rows_of_table = [owner_ref[m] * ROWS_DEV + slot_ref[m] for m in range(HIST)]
    for k in range(HIST):
        at = order[:, k : k + 1]
        lookups = jnp.zeros((2, SEQ), jnp.int32)
        length = jnp.zeros((1, 1), jnp.int32)
        for m in range(HIST):
            lookups = jnp.where(jnp.broadcast_to(at, (2, SEQ)) == m, rows_of_table[m], lookups)
            length = jnp.where(at == m, length_ref[:, m : m + 1], length)
        msg_out[k, 0:2, 0:SEQ] = lookups
        msg_out[k, 2:3, 0:SEQ] = jnp.broadcast_to(length, (1, SEQ))
    pl.semaphore_wait(barrier, 38)

    def msg_copy(k):
        peer = lax.rem(dp + k, 8)
        return pltpu.make_async_remote_copy(
            src_ref=msg_out.at[peer], dst_ref=msg_in.at[dp],
            send_sem=m_send.at[k], recv_sem=m_recv.at[k],
            device_id=(peer, tab), device_id_type=MESH,
        )

    for k in range(1, 8):
        msg_copy(k).start()
    msg_in[dp] = msg_out[dp]
    for k in range(1, 8):
        msg_copy(k).wait_recv()

    items = jnp.concatenate([msg_in[k, 0:1, :] for k in range(HIST)], axis=0)
    actions = jnp.concatenate([msg_in[k, 1:2, :] for k in range(HIST)], axis=0)
    lengths = jnp.concatenate([msg_in[k, 2:3, :] for k in range(HIST)], axis=0)[:, 0:1]
    is_item = lax.broadcasted_iota(jnp.int32, (HIST, TOK), 1) < SEQ
    ids = jnp.where(is_item, items, pltpu.roll(actions, SEQ, 1))
    owner = ids // ROWS_DEV
    ids_col = ids.astype(F32).T.astype(jnp.int32)
    owner_col, row_col = ids_col // ROWS_DEV, ids_col % ROWS_DEV
    sub = lax.broadcasted_iota(jnp.int32, (TOK, TOK), 0)
    lane = lax.broadcasted_iota(jnp.int32, (TOK, TOK), 1)
    ranks = []
    for m in range(HIST):
        same = (owner_col[:, m : m + 1] == owner[m : m + 1, :]) & (sub < lane)
        ranks.append(jnp.sum(jnp.where(same, 1.0, 0.0), axis=0, keepdims=True))
    rank = jnp.concatenate(ranks, axis=0)
    rank_col = rank.T.astype(jnp.int32)
    request = jnp.zeros((N_TABLE, TOK), F32)
    owners = lax.broadcasted_iota(jnp.int32, (N_TABLE, TOK), 0)
    for m in range(HIST):
        low, high = split_number(row_col[:, m : m + 1] + 1)
        spot = m * MOST + rank_col[:, m : m + 1]
        put = jnp.where(lane == spot, low.astype(F32), 0.0)
        put = jnp.where(lane == spot + 64, high.astype(F32), put)
        request = request + mm((owners == owner[m : m + 1, :]).astype(BF16), put.astype(BF16))
    request = request + 256.0 * pltpu.roll(request, 64, 1)
    request = jnp.where(owners >= 0, request, 0.0)
    request = jnp.where(lax.broadcasted_iota(jnp.int32, (N_TABLE, TOK), 1) < 64, request, 0.0)
    request = request.astype(jnp.int32)
    for o in range(N_TABLE):
        req_out[o] = request[o : o + 1, :]

    def req_copy(k):
        peer = lax.rem(tab + k, 32)
        return pltpu.make_async_remote_copy(
            src_ref=req_out.at[peer], dst_ref=req_in.at[tab],
            send_sem=r_send.at[k], recv_sem=r_recv.at[k],
            device_id=(dp, peer), device_id_type=MESH,
        )

    def ask(k, carry):
        req_copy(k).start()
        return carry

    lax.fori_loop(1, 32, ask, 0)
    req_in[tab] = req_out[tab]

    slot = owner * 16 + rank.astype(jnp.int32)
    first_half = lax.broadcasted_iota(jnp.int32, (1, TOK), 1) < SEQ
    for p in range(PAIRS):
        a = slot[2 * p : 2 * p + 1, :]
        b = slot[2 * p + 1 : 2 * p + 2, :] + MOST
        item = jnp.where(first_half, a, pltpu.roll(b, SEQ, 1))
        action = jnp.where(first_half, pltpu.roll(a, SEQ, 1), b)
        length = jnp.where(first_half, lengths[2 * p : 2 * p + 1], lengths[2 * p + 1 : 2 * p + 2])
        block = jnp.concatenate([item, action, length, length] * 2, axis=0)
        rows_s[p] = block
        cols_s[p] = block.astype(F32).T.astype(jnp.int32)

    def asked(k, carry):
        req_copy(k).wait_recv()
        return carry

    lax.fori_loop(1, 32, asked, 0)
    asks = jnp.concatenate([req_in[k] for k in range(N_TABLE)], axis=0)
    low, high = split_number(asks)
    tall = lax.broadcasted_iota(jnp.int32, (SLOTS, N_TABLE), 0) // 16
    tall = (tall == lax.broadcasted_iota(jnp.int32, (SLOTS, N_TABLE), 1)).astype(BF16)
    wanted[...] = mm(tall, low) + 256.0 * mm(tall, high) - 1.0
    wide = lax.broadcasted_iota(jnp.int32, (N_TABLE, SLOTS), 1) // 16
    wide = (wide == lax.broadcasted_iota(jnp.int32, (N_TABLE, SLOTS), 0)).astype(BF16)
    across = mm_tn(low, wide) + 256.0 * mm_tn(high, wide) - 1.0
    at = lax.broadcasted_iota(jnp.int32, (TOK, SLOTS), 0)
    in_owner = lax.broadcasted_iota(jnp.int32, (TOK, SLOTS), 1) % 16
    for p in range(PAIRS):
        line = jnp.sum(jnp.where(at == in_owner + 16 * p, across, 0.0), axis=0, keepdims=True)
        req_rows[:, p * SLOTS : (p + 1) * SLOTS] = line.astype(jnp.int32)

    def fetch_copy(p, k):
        peer = lax.rem(tab + k, 32)
        return pltpu.make_async_remote_copy(
            src_ref=picked.at[p, peer], dst_ref=replies.at[p, tab],
            send_sem=f_send.at[p, k], recv_sem=f_recv.at[p, k],
            device_id=(dp, peer), device_id_type=MESH,
        )

    loads[0].wait()

    def serve(p, carry):
        at = lax.broadcasted_iota(jnp.int32, (SLOTS, TOK), 0) % 16 + 16 * p
        seen = lax.broadcasted_iota(jnp.int32, (SLOTS, TOK), 1) == at
        line = jnp.sum(jnp.where(seen, wanted[...], 0.0), axis=1, keepdims=True)
        line = line.astype(jnp.int32)
        places = lax.broadcasted_iota(jnp.int32, (SLOTS, ROWS_DEV), 1)
        chosen = (places == line).astype(BF16)
        picked[p] = mm(chosen, table[...]).astype(BF16).reshape(N_TABLE, 16, EMB)

        def start(k, inner):
            fetch_copy(p, k).start()
            return inner

        lax.fori_loop(1, 32, start, 0)
        replies[p, tab] = picked[p, tab]
        return carry

    lax.fori_loop(0, PAIRS, serve, 0)

    outgoing = picked

    def give_copy(p, k):
        peer = lax.rem(tab + k, 32)
        return pltpu.make_async_remote_copy(
            src_ref=outgoing.at[p, peer], dst_ref=incoming.at[p, tab],
            send_sem=a_send.at[p, k], recv_sem=a_recv.at[p, k],
            device_id=(dp, peer), device_id_type=MESH,
        )

    for load in loads[1:]:
        load.wait()

    def give(n, carry):
        give_copy(n // 31, n % 31 + 1).start()
        return carry

    def fetched(p):
        def landed(k, carry):
            fetch_copy(p, k).wait_recv()
            fetch_copy(p, k).wait_send()
            return carry

        lax.fori_loop(1, 32, landed, 0)

    def pair(p, carry):
        fetched(p)

        @pl.when(p == PAIRS - 1)
        def _():
            lax.fori_loop(0, (PAIRS - 1) * 31, give, 0)

        tokens = pl.ds(pl.multiple_of(p * TOK, TOK), TOK)
        normed_p, mixed_p, top_p, before_p, back = layer_pair(
            replies[p].reshape(SLOTS, EMB), cols_s[p], rows_s[p], up[tokens, :], wp, wo
        )
        outgoing[p] = back.reshape(N_TABLE, 16, EMB)
        incoming[p, tab] = outgoing[p, tab]
        normed_t[:, tokens] = normed_p
        mixed_t[:, tokens] = mixed_p
        up[tokens, :] = top_p
        gbs[tokens, :] = before_p
        return carry

    lax.fori_loop(0, PAIRS, pair, 0)
    lax.fori_loop((PAIRS - 1) * 31, PAIRS * 31, give, 0)

    def core_copy(k):
        return pltpu.make_async_remote_copy(
            src_ref=g.at[0, k], dst_ref=core_buf.at[k],
            send_sem=core_send.at[k], recv_sem=core_recv.at[k],
            device_id=other, device_id_type=MESH,
        )

    s1 = g.at[1]
    t2 = g.at[0]

    def merge(k):
        core_copy(k).wait_recv()
        core_copy(k).wait_send()

        def step(n, inner):
            s1[k, n] = (s1[k, n].astype(F32) + core_buf[k, n].astype(F32)).astype(BF16)
            return inner

        lax.fori_loop(0, 4, step, 0)

    def two(ref, n):
        return ref.at[pl.ds(2 * n, 2)]

    def add_flat(target, other_ref):
        target[...] = (target[...].astype(F32) + other_ref[...].astype(F32)).astype(BF16)

    def chosen_rows(p, first, count):
        places = lax.broadcasted_iota(jnp.int32, (count, SLOTS), 0) + first
        return (places == req_rows[:, p * SLOTS : (p + 1) * SLOTS]).astype(BF16)

    def take_in(p):
        def given(k, carry):
            give_copy(p, k).wait_recv()
            return carry

        lax.fori_loop(1, 32, given, 0)

    def add_rows(p):
        take_in(p)

        def block(b, carry):
            first = b * 512
            part = mm(chosen_rows(p, first, 512), incoming[p].reshape(SLOTS, EMB))
            rows = pl.ds(pl.multiple_of(first, 512), 512)
            sums[rows, :] = part if p == 0 else sums[rows, :] + part
            return carry

        lax.fori_loop(0, 4, block, 0)

    fars, nears, partials = (far_1, far_2, far_3), (near_1, near_2, near_3), (sum_1, sum_2, sum_3)
    last_fars = (last_far_1, last_far_2, last_far_3)
    last_nears = (last_near_1, last_near_2, last_near_3)

    def ring_on(over_y, chunk, half, far, near, number):
        place, right, left = (y, y_right, y_left) if over_y else (x, x_right, x_left)
        ring = Ring(place, right, left, chunk, half, far, near,
                    ring_send.at[number], ring_recv.at[number])
        ring.make()
        return ring

    def first_chunk(n):
        first, count, over_y = STREAMS[n]
        if over_y:
            return lambda k: s1.at[k, :, pl.ds(first, count), :]
        return lambda k: s1.at[:, k, pl.ds(first, count), :]

    def half_rows(count):
        return lambda ref, n: ref.at[pl.ds(count // 2 * n, count // 2), :]

    firsts = [
        ring_on(STREAMS[n][2], first_chunk(n), two, fars[n], nears[n], n) for n in range(3)
    ]
    seconds = [
        ring_on(not STREAMS[n][2], lambda k, n=n: partials[n].at[k], half_rows(STREAMS[n][1]),
                last_fars[n], last_nears[n], 3 + n)
        for n in range(3)
    ]

    def turn(n):
        first, count, over_y = STREAMS[n]
        firsts[n].arrive()
        for m in range(4):
            own = s1[y, m, first : first + count, :] if over_y else s1[m, x, first : first + count, :]
            total = own.astype(F32) + nears[n][0, m].astype(F32) + nears[n][1, m].astype(F32)
            partials[n][m] = total.astype(BF16)
        seconds[n].start()

    def z_copy(target, source):
        return pltpu.make_async_remote_copy(
            src_ref=s4.at[target], dst_ref=zbuf.at[source],
            send_sem=z_send.at[target], recv_sem=z_recv.at[source],
            device_id=(dp, 8 * x + target), device_id_type=MESH,
        )

    def leave(n):
        first, count, over_y = STREAMS[n]
        seconds[n].arrive()
        place = x if over_y else y
        total = partials[n][place].astype(F32) + last_nears[n][0].astype(F32)
        total = (total + last_nears[n][1].astype(F32)).astype(BF16)
        s4[first // 32 : (first + count) // 32] = total.reshape(count // 32, 32, 512)
        for target in range(first // 32, (first + count) // 32):

            @pl.when(z != target)
            def _():
                z_copy(target, z).start()

    def chunk_at(n):
        return lax.rem(y + 2 + n + (n // 2) * (1 - 2 * (n % 2)), 4)

    def terms(n, carry):
        k = chunk_at(n)
        first = mm(normed_t[...], gbs[:, pl.ds(pl.multiple_of(k * 768, 768), 768)]) * SCALE
        second = mm(mixed_t[...], up[:, pl.ds(pl.multiple_of(k * 256, 256), 256)]) * SCALE
        for which, kept in ((0, 1 - c), (1, c)):
            one = first[:, which * 384 : (which + 1) * 384].astype(BF16)
            two_ = second[:, which * 128 : (which + 1) * 128].astype(BF16)
            g[kept, k, :, :, 0:384] = one.reshape(4, 256, 384)
            g[kept, k, :, :, 384:512] = two_.reshape(4, 256, 128)
        core_copy(k).start()

        @pl.when(n > 0)
        def _():
            merge(chunk_at(n - 1))

        @pl.when(n == 1)
        def _():
            firsts[0].copies[0].start()
            firsts[0].copies[1].start()

        @pl.when(n == 2)
        def _():
            firsts[0].copies[3].start()

        @pl.when(n == 3)
        def _():
            firsts[0].copies[2].start()

        return carry

    lax.fori_loop(0, 4, terms, 0)
    merge(y)
    firsts[2].start()
    firsts[1].copies[0].start()
    firsts[1].copies[1].start()
    add_rows(0)
    firsts[0].forward(add_into)
    firsts[1].copies[2].start()
    firsts[1].copies[3].start()
    turn(0)
    firsts[1].forward(add_into)
    add_rows(1)
    firsts[2].forward(add_into)
    seconds[0].forward(add_flat)
    turn(1)
    turn(2)
    leave(0)
    add_rows(2)
    seconds[1].forward(add_flat)
    seconds[2].forward(add_flat)
    leave(1)
    leave(2)

    take_in(PAIRS - 1)

    def rows_of(first):
        part = mm(chosen_rows(PAIRS - 1, first, 256), incoming[PAIRS - 1].reshape(SLOTS, EMB))
        rows = pl.ds(pl.multiple_of(first, 256), 256)
        return (sums[rows, :] + part).astype(BF16).astype(F32)

    def t_copy(b):
        lanes = pl.ds(pl.multiple_of(b * 128, 128), 128)
        return pltpu.make_async_remote_copy(
            src_ref=t2.at[1 - c, :, :, lanes], dst_ref=t_core.at[:, :, lanes],
            send_sem=core_send.at[4 + b], recv_sem=core_recv.at[4 + b],
            device_id=other, device_id_type=MESH,
        )

    def table_block(b, carry):
        upper = rows_of(b * 256)
        lower = rows_of(b * 256 + 1024)
        lanes = pl.ds(pl.multiple_of(b * 128, 128), 128)
        is_left = lax.broadcasted_iota(jnp.int32, (256, 128), 1) < 64
        for k in range(4):
            up_k, low_k = upper[:, k * 128 : (k + 1) * 128], lower[:, k * 128 : (k + 1) * 128]
            t2[0, k, :, lanes] = jnp.where(is_left, up_k, pltpu.roll(low_k, 64, 1)).astype(BF16)
            t2[1, k, :, lanes] = jnp.where(is_left, pltpu.roll(up_k, 64, 1), low_k).astype(BF16)
        t_copy(b).start()
        return carry

    def table_merge(b, carry):
        t_copy(b).wait_recv()
        lanes = pl.ds(pl.multiple_of(b * 128, 128), 128)
        for k in range(4):
            mine = t2[c, k, :, lanes].astype(F32) + t_core[k, :, lanes].astype(F32)
            t2[c, k, :, lanes] = mine.astype(BF16)
        return carry

    ring_t = Ring(y, y_right, y_left, lambda k: t2.at[c, k],
                  lambda ref, n: ref.at[:, pl.ds(256 * n, 256)], t_far, t_near,
                  ring_send.at[6], ring_recv.at[6])
    ring_t.make()
    lax.fori_loop(0, 3, table_block, 0)
    lax.fori_loop(0, 2, table_merge, 0)
    ring_t.start_half(0)
    lax.fori_loop(3, 4, table_block, 0)
    lax.fori_loop(2, 4, table_merge, 0)
    ring_t.start_half(1)

    ring_t.forward(add_flat)
    total = s4[z].astype(F32)
    for k in range(1, 8):
        source = lax.rem(z + k, 8)
        z_copy(z, source).wait_recv()
        total = total + zbuf[source].astype(F32)
    dense_ref[...] = total.astype(BF16)
    ring_t.arrive()
    total = t2[c, y].astype(F32) + t_near[0].astype(F32) + t_near[1].astype(F32)
    table_ref[...] = total.astype(BF16)

    def sent(k, carry):
        req_copy(k).wait_send()
        for p in range(PAIRS):
            give_copy(p, k).wait_send()
        return carry

    lax.fori_loop(1, 32, sent, 0)
    for k in range(4):
        t_copy(k).wait_send()
    for k in range(1, 8):
        msg_copy(k).wait_send()
        z_copy(lax.rem(z + k, 8), z).wait_send()
    for ring in (*firsts, *seconds, ring_t):
        ring.end()


def output_kernel(dense_ref, sums_ref, proj_ref, outw_ref, table_ref):
    proj_ref[...] = dense_ref[:, :384]
    outw_ref[...] = dense_ref[:, 384:]
    across = sums_ref[...].astype(F32).T.astype(BF16)
    for b in range(4):
        for half in range(2):
            part = across[b * 128 + half * 64 : b * 128 + half * 64 + 64]
            table_ref[:, half * 1024 + b * 256 : half * 1024 + (b + 1) * 256] = part


def run(*arrays):
    whole = pl.BlockSpec(memory_space=pltpu.VMEM)
    anywhere = pl.BlockSpec(memory_space=pl.ANY)
    dma = pltpu.SemaphoreType.DMA
    tokens = HIST * SEQ

    def buf(*shape):
        return pltpu.VMEM(shape, BF16)

    parts = pl.pallas_call(
        program_kernel,
        out_shape=(
            jax.ShapeDtypeStruct((32, 512), BF16),
            jax.ShapeDtypeStruct((256, 512), BF16),
        ),
        in_specs=[whole] * 4 + [anywhere] * 4,
        out_specs=(whole,) * 2,
        scratch_shapes=[
            buf(ROWS_DEV, EMB), buf(tokens, D), buf(D, PROJ), buf(D, D),
            pltpu.VMEM((HIST, 8, TOK), jnp.int32),
            pltpu.VMEM((HIST, 8, TOK), jnp.int32),
            pltpu.VMEM((N_TABLE, 1, TOK), jnp.int32),
            pltpu.VMEM((N_TABLE, 1, TOK), jnp.int32),
            pltpu.VMEM((SLOTS, TOK), F32),
            pltpu.VMEM((1, PAIRS * SLOTS), jnp.int32),
            pltpu.VMEM((PAIRS, 8, TOK), jnp.int32),
            pltpu.VMEM((PAIRS, TOK, 8), jnp.int32),
            buf(PAIRS, N_TABLE, 16, EMB), buf(PAIRS, N_TABLE, 16, EMB),
            buf(PAIRS, N_TABLE, 16, EMB),
            buf(D, tokens), buf(D, tokens), buf(tokens, PROJ),
            buf(2, 4, 4, 256, 512), buf(4, 4, 256, 512), pltpu.VMEM((ROWS_DEV, EMB), F32),
            *[buf(2, 2, n, 512) for _, n, _ in STREAMS],
            *[buf(2, 4, n, 512) for _, n, _ in STREAMS],
            *[buf(4, n, 512) for _, n, _ in STREAMS],
            *[buf(2, n // 2, 512) for _, n, _ in STREAMS],
            *[buf(2, n, 512) for _, n, _ in STREAMS],
            buf(8, 32, 512), buf(8, 32, 512),
            buf(4, 256, 512), buf(2, 256, 256), buf(2, 256, 512),
            dma((4,)), dma((8,)), dma((8,)), dma((32,)), dma((32,)),
            dma((PAIRS, 32)), dma((PAIRS, 32)), dma((PAIRS, 32)), dma((PAIRS, 32)),
            dma((8,)), dma((8,)), dma((7, 6)), dma((7, 6)), dma((8,)), dma((8,)),
        ],
        compiler_params=pltpu.CompilerParams(
            vmem_limit_bytes=VMEM_LIMIT, collective_id=0, has_side_effects=True
        ),
        name="whole_program",
    )(*arrays)
    return pl.pallas_call(
        output_kernel,
        out_shape=(
            jax.ShapeDtypeStruct((32, 384), BF16),
            jax.ShapeDtypeStruct((32, 128), BF16),
            jax.ShapeDtypeStruct((64, 2048), BF16),
        ),
        in_specs=[whole] * 2,
        out_specs=(whole,) * 3,
        name="outputs",
    )(*parts)


def body(
    embed_table, owner_shard, slot_row, lengths, send_order, proj_weight, out_weight, upstream
):
    proj, outw, table = run(
        jnp.swapaxes(owner_shard[..., 0], 1, 2), jnp.swapaxes(slot_row, 1, 2),
        lengths.reshape(1, HIST), send_order, embed_table, upstream.reshape(HIST * SEQ, D),
        proj_weight, out_weight,
    )
    return table.T, proj, outw


def solution(mesh):
    in_specs = (
        P("table", None),
        P(("dp", "table"), None, None, None),
        P(("dp", "table"), None, None),
        P(("dp", "table")),
        P(("dp", "table"), None),
        P(),
        P(),
        P(("dp", "table"), None, None),
    )
    out_specs = (P("table", "dp"), P("table", "dp"), P("table", "dp"))
    return jax.shard_map(body, mesh=mesh, in_specs=in_specs, out_specs=out_specs, check_vma=False)
```

```python
import functools

import jax
import jax.numpy as jnp
from jax import lax
from jax.experimental import pallas as pl
from jax.experimental.pallas import tpu as pltpu
from jax.sharding import PartitionSpec as P

D = 1024
EMB = 512
HEADS = 8
QK = 64
PROJ = 3072
SEQ = 64
HIST = 8
ROWS_DEV = 2048
MOST = 8
N_DP = 8
N_TABLE = 32
PAIRS = HIST // 2
TOK = 2 * SEQ
SLOTS = 2 * N_TABLE * MOST
EPSILON = 1e-06
SCALE = float(2048 * 64) ** (-0.5)
MESH = pl.DeviceIdType.MESH
VMEM_LIMIT = 60 * 1024 * 1024
STREAMS = ((0, 96, True), (96, 96, True), (192, 64, False))
F32 = jnp.float32
BF16 = jnp.bfloat16


def mm(a, b):
    return lax.dot_general(a, b, (((1,), (0,)), ((), ())), preferred_element_type=F32)


def mm_nt(a, b):
    return lax.dot_general(a, b, (((1,), (1,)), ((), ())), preferred_element_type=F32)


def mm_tn(a, b):
    return lax.dot_general(a, b, (((0,), (0,)), ((), ())), preferred_element_type=F32)


def sigmoid(x):
    return 0.5 * jnp.tanh(0.5 * x) + 0.5


class Ring:
    def __init__(self, place, to_right, to_left, chunk, half, far, near, send, recv):
        self.place, self.right, self.left = place, to_right, to_left
        self.chunk, self.half, self.far, self.near = chunk, half, far, near
        self.send, self.recv = send, recv

    def copy(self, number, src, dst, device):
        return pltpu.make_async_remote_copy(
            src_ref=src, dst_ref=dst, send_sem=self.send.at[number], recv_sem=self.recv.at[number],
            device_id=device, device_id_type=MESH,
        )

    def make(self):
        across, after, ahead = (lax.rem(self.place + k, 4) for k in (2, 1, 3))
        self.after, self.ahead = after, ahead
        part, half, far, near = self.chunk, self.half, self.far, self.near
        self.copies = [
            self.copy(0, half(part(across), 0), far.at[0], self.right),
            self.copy(1, half(part(across), 1), far.at[1], self.left),
            self.copy(2, half(part(after), 1), half(near.at[0], 1), self.right),
            self.copy(3, half(part(ahead), 0), half(near.at[1], 0), self.left),
            self.copy(4, half(part(after), 0), half(near.at[0], 0), self.right),
            self.copy(5, half(part(ahead), 1), half(near.at[1], 1), self.left),
        ]

    def start_half(self, number):
        for k in ((0, 3), (1, 2))[number]:
            self.copies[k].start()

    def start(self):
        self.start_half(0)
        self.start_half(1)

    def forward(self, add):
        self.copies[0].wait_recv()
        add(self.half(self.chunk(self.after), 0), self.far.at[0])
        self.copies[4].start()
        self.copies[1].wait_recv()
        add(self.half(self.chunk(self.ahead), 1), self.far.at[1])
        self.copies[5].start()

    def arrive(self):
        for k in range(2, 6):
            self.copies[k].wait_recv()

    def end(self):
        for k in range(6):
            self.copies[k].wait_send()


def add_into(target, other):
    for n in range(target.shape[0]):
        target[n] = (target[n].astype(F32) + other[n].astype(F32)).astype(BF16)


def layer_pair(replies, cols, rows, upstream, wp, wo):
    item_at, action_at, length = cols[:, 0:1], cols[:, 1:2], cols[:, 2:3]
    places = lax.broadcasted_iota(jnp.int32, (TOK, SLOTS), 1)
    left = mm((places == item_at).astype(BF16), replies)
    right = mm((places == action_at).astype(BF16), replies)
    fetched = jnp.concatenate([left, right], axis=1)
    average = jnp.mean(fetched, axis=1, keepdims=True)
    centred = fetched - average
    rstd = lax.rsqrt(jnp.mean(centred * centred, axis=1, keepdims=True) + EPSILON)
    normed_full = centred * rstd
    normed = normed_full.astype(BF16)

    before = mm(normed, wp[...])
    gate = sigmoid(before)
    slope = gate * (1.0 + before * (1.0 - gate))
    projected = (before * gate).astype(BF16)
    u = projected[:, :D].astype(F32)
    values = projected[:, D : 2 * D]
    queries = projected[:, 2 * D : 2 * D + HEADS * QK]
    keys = projected[:, 2 * D + HEADS * QK :]

    at = lax.broadcasted_iota(jnp.int32, (TOK, TOK), 0)
    source = lax.broadcasted_iota(jnp.int32, (TOK, TOK), 1)
    seen = (source <= at) & ((at // SEQ) == (source // SEQ))
    share = jnp.where(seen, 1.0 / length.astype(F32), 0.0)
    parts = (source < QK, source >= QK)
    zero = jnp.zeros((TOK, TOK), BF16)

    weights, factors, attended = [], [], []
    for h in range(HEADS):
        two = slice((h // 2) * TOK, (h // 2 + 1) * TOK)
        key = jnp.where(parts[h % 2], keys[:, two], zero)
        score = mm_nt(queries[:, two], key)
        open_ = sigmoid(score)
        weight = (score * open_ * share).astype(BF16)
        weights.append(weight)
        factors.append(open_ * (1.0 + score * (1.0 - open_)) * share)
        attended.append(mm(weight, values[:, h * TOK : (h + 1) * TOK]))
    attended = jnp.concatenate(attended, axis=1)
    average = jnp.mean(attended, axis=1, keepdims=True)
    centred = attended - average
    spread = lax.rsqrt(jnp.mean(centred * centred, axis=1, keepdims=True) + EPSILON)
    inner = centred * spread
    mixed = inner * u

    place = lax.broadcasted_iota(jnp.int32, (TOK, D), 0) % SEQ
    top = jnp.where(place < length, upstream.astype(F32), 0.0)
    top_low = top.astype(BF16)
    grad_mixed = mm_nt(top_low, wo[...]).astype(BF16).astype(F32)
    grad_u = (grad_mixed * inner).astype(BF16)
    grad_inner = grad_mixed * u
    first = jnp.mean(grad_inner, axis=1, keepdims=True)
    second = jnp.mean(grad_inner * inner, axis=1, keepdims=True)
    grad_att = (spread * (grad_inner - first - inner * second)).astype(BF16)

    grad_v, grad_q, grad_k = [], [], []
    for h in range(HEADS):
        own = slice(h * TOK, (h + 1) * TOK)
        two = slice((h // 2) * TOK, (h // 2 + 1) * TOK)
        grad_weight = mm_nt(grad_att[:, own], values[:, own]).astype(BF16).astype(F32)
        grad_v.append(mm_tn(weights[h], grad_att[:, own]).astype(BF16))
        grad_score = (grad_weight * factors[h]).astype(BF16)
        key = jnp.where(parts[h % 2], keys[:, two], zero)
        query = jnp.where(parts[h % 2], queries[:, two], zero)
        gq = mm(grad_score, key)
        gk = mm_tn(grad_score, query)
        if h % 2:
            grad_q[-1] = (grad_q[-1] + gq).astype(BF16)
            grad_k[-1] = (grad_k[-1] + gk).astype(BF16)
        else:
            grad_q.append(gq)
            grad_k.append(gk)
    grad_projected = jnp.concatenate([grad_u] + grad_v + grad_q + grad_k, axis=1)
    grad_before = (grad_projected.astype(F32) * slope).astype(BF16)
    grad_normed = mm_nt(grad_before, wp[...])
    first = jnp.mean(grad_normed, axis=1, keepdims=True)
    second = jnp.mean(grad_normed * normed_full, axis=1, keepdims=True)
    grad_rows = (top + rstd * (grad_normed - first - normed_full * second)).astype(BF16)

    slots = lax.broadcasted_iota(jnp.int32, (SLOTS, TOK), 0)
    back = mm((slots == rows[0:1, :]).astype(BF16), grad_rows[:, :EMB])
    back = back + mm((slots == rows[1:2, :]).astype(BF16), grad_rows[:, EMB:])
    return normed_full.T.astype(BF16), mixed.T.astype(BF16), top_low, grad_before, back.astype(BF16)


def split_number(numbers):
    high = numbers // 256
    return (numbers - 256 * high).astype(BF16), high.astype(BF16)


def program_kernel(
    owner_ref, slot_ref, length_ref, order_ref, table_hbm, up_hbm, wp_hbm, wo_hbm,
    dense_ref, table_ref,
    table, up, wp, wo, msg_out, msg_in, req_out, req_in, wanted, req_rows, rows_s, cols_s,
    picked, replies, incoming, normed_t, mixed_t, gbs,
    g, core_buf, sums, far_1, far_2, far_3, near_1, near_2, near_3, sum_1, sum_2, sum_3,
    last_far_1, last_far_2, last_far_3, last_near_1, last_near_2, last_near_3,
    s4, zbuf, t_core, t_far, t_near,
    load_sem, m_send, m_recv, r_send, r_recv, f_send, f_recv, a_send, a_recv,
    core_send, core_recv, ring_send, ring_recv, z_send, z_recv,
):
    dp = lax.axis_index("dp")
    tab = lax.axis_index("table")
    y, c = dp // 2, dp % 2
    x, z = tab // 8, tab % 8
    other = (2 * y + 1 - c, tab)
    y_right = (2 * lax.rem(y + 1, 4) + c, tab)
    y_left = (2 * lax.rem(y + 3, 4) + c, tab)
    x_right = (dp, lax.rem(tab + 8, 32))
    x_left = (dp, lax.rem(tab + 24, 32))

    loads = [
        pltpu.make_async_copy(src, dst, load_sem.at[n])
        for n, (src, dst) in enumerate(
            ((table_hbm, table), (up_hbm, up), (wp_hbm, wp), (wo_hbm, wo))
        )
    ]
    for load in loads:
        load.start()

    barrier = pltpu.get_barrier_semaphore()

    def greet_dp(k, carry):
        pl.semaphore_signal(
            barrier, inc=1, device_id=(lax.rem(dp + k, 8), tab), device_id_type=MESH
        )
        return carry

    def greet_table(k, carry):
        pl.semaphore_signal(
            barrier, inc=1, device_id=(dp, lax.rem(tab + k, 32)), device_id_type=MESH
        )
        return carry

    lax.fori_loop(1, 8, greet_dp, 0)
    lax.fori_loop(1, 32, greet_table, 0)

    order = order_ref[...]
    rows_of_table = [owner_ref[m] * ROWS_DEV + slot_ref[m] for m in range(HIST)]
    for k in range(HIST):
        at = order[:, k : k + 1]
        lookups = jnp.zeros((2, SEQ), jnp.int32)
        length = jnp.zeros((1, 1), jnp.int32)
        for m in range(HIST):
            lookups = jnp.where(jnp.broadcast_to(at, (2, SEQ)) == m, rows_of_table[m], lookups)
            length = jnp.where(at == m, length_ref[:, m : m + 1], length)
        msg_out[k, 0:2, 0:SEQ] = lookups
        msg_out[k, 2:3, 0:SEQ] = jnp.broadcast_to(length, (1, SEQ))
    pl.semaphore_wait(barrier, 38)

    def msg_copy(k):
        peer = lax.rem(dp + k, 8)
        return pltpu.make_async_remote_copy(
            src_ref=msg_out.at[peer], dst_ref=msg_in.at[dp],
            send_sem=m_send.at[k], recv_sem=m_recv.at[k],
            device_id=(peer, tab), device_id_type=MESH,
        )

    for k in range(1, 8):
        msg_copy(k).start()
    msg_in[dp] = msg_out[dp]
    for k in range(1, 8):
        msg_copy(k).wait_recv()

    items = jnp.concatenate([msg_in[k, 0:1, :] for k in range(HIST)], axis=0)
    actions = jnp.concatenate([msg_in[k, 1:2, :] for k in range(HIST)], axis=0)
    lengths = jnp.concatenate([msg_in[k, 2:3, :] for k in range(HIST)], axis=0)[:, 0:1]
    is_item = lax.broadcasted_iota(jnp.int32, (HIST, TOK), 1) < SEQ
    ids = jnp.where(is_item, items, pltpu.roll(actions, SEQ, 1))
    owner = ids // ROWS_DEV
    ids_col = ids.astype(F32).T.astype(jnp.int32)
    owner_col, row_col = ids_col // ROWS_DEV, ids_col % ROWS_DEV
    sub = lax.broadcasted_iota(jnp.int32, (TOK, TOK), 0)
    lane = lax.broadcasted_iota(jnp.int32, (TOK, TOK), 1)
    ranks = []
    for m in range(HIST):
        same = (owner_col[:, m : m + 1] == owner[m : m + 1, :]) & (sub < lane)
        ranks.append(jnp.sum(jnp.where(same, 1.0, 0.0), axis=0, keepdims=True))
    rank = jnp.concatenate(ranks, axis=0)
    rank_col = rank.T.astype(jnp.int32)
    request = jnp.zeros((N_TABLE, TOK), F32)
    owners = lax.broadcasted_iota(jnp.int32, (N_TABLE, TOK), 0)
    for m in range(HIST):
        low, high = split_number(row_col[:, m : m + 1] + 1)
        spot = m * MOST + rank_col[:, m : m + 1]
        put = jnp.where(lane == spot, low.astype(F32), 0.0)
        put = jnp.where(lane == spot + 64, high.astype(F32), put)
        request = request + mm((owners == owner[m : m + 1, :]).astype(BF16), put.astype(BF16))
    request = request + 256.0 * pltpu.roll(request, 64, 1)
    request = jnp.where(owners >= 0, request, 0.0)
    request = jnp.where(lax.broadcasted_iota(jnp.int32, (N_TABLE, TOK), 1) < 64, request, 0.0)
    request = request.astype(jnp.int32)
    for o in range(N_TABLE):
        req_out[o] = request[o : o + 1, :]

    def req_copy(k):
        peer = lax.rem(tab + k, 32)
        return pltpu.make_async_remote_copy(
            src_ref=req_out.at[peer], dst_ref=req_in.at[tab],
            send_sem=r_send.at[k], recv_sem=r_recv.at[k],
            device_id=(dp, peer), device_id_type=MESH,
        )

    def ask(k, carry):
        req_copy(k).start()
        return carry

    lax.fori_loop(1, 32, ask, 0)
    req_in[tab] = req_out[tab]

    slot = owner * 16 + rank.astype(jnp.int32)
    first_half = lax.broadcasted_iota(jnp.int32, (1, TOK), 1) < SEQ
    for p in range(PAIRS):
        a = slot[2 * p : 2 * p + 1, :]
        b = slot[2 * p + 1 : 2 * p + 2, :] + MOST
        item = jnp.where(first_half, a, pltpu.roll(b, SEQ, 1))
        action = jnp.where(first_half, pltpu.roll(a, SEQ, 1), b)
        length = jnp.where(first_half, lengths[2 * p : 2 * p + 1], lengths[2 * p + 1 : 2 * p + 2])
        block = jnp.concatenate([item, action, length, length] * 2, axis=0)
        rows_s[p] = block
        cols_s[p] = block.astype(F32).T.astype(jnp.int32)

    def asked(k, carry):
        req_copy(k).wait_recv()
        return carry

    lax.fori_loop(1, 32, asked, 0)
    asks = jnp.concatenate([req_in[k] for k in range(N_TABLE)], axis=0)
    low, high = split_number(asks)
    tall = lax.broadcasted_iota(jnp.int32, (SLOTS, N_TABLE), 0) // 16
    tall = (tall == lax.broadcasted_iota(jnp.int32, (SLOTS, N_TABLE), 1)).astype(BF16)
    wanted[...] = mm(tall, low) + 256.0 * mm(tall, high) - 1.0
    wide = lax.broadcasted_iota(jnp.int32, (N_TABLE, SLOTS), 1) // 16
    wide = (wide == lax.broadcasted_iota(jnp.int32, (N_TABLE, SLOTS), 0)).astype(BF16)
    across = mm_tn(low, wide) + 256.0 * mm_tn(high, wide) - 1.0
    at = lax.broadcasted_iota(jnp.int32, (TOK, SLOTS), 0)
    in_owner = lax.broadcasted_iota(jnp.int32, (TOK, SLOTS), 1) % 16
    for p in range(PAIRS):
        line = jnp.sum(jnp.where(at == in_owner + 16 * p, across, 0.0), axis=0, keepdims=True)
        req_rows[:, p * SLOTS : (p + 1) * SLOTS] = line.astype(jnp.int32)

    def fetch_copy(p, k):
        peer = lax.rem(tab + k, 32)
        return pltpu.make_async_remote_copy(
            src_ref=picked.at[p, peer], dst_ref=replies.at[p, tab],
            send_sem=f_send.at[p, k], recv_sem=f_recv.at[p, k],
            device_id=(dp, peer), device_id_type=MESH,
        )

    loads[0].wait()

    def serve(p, carry):
        at = lax.broadcasted_iota(jnp.int32, (SLOTS, TOK), 0) % 16 + 16 * p
        seen = lax.broadcasted_iota(jnp.int32, (SLOTS, TOK), 1) == at
        line = jnp.sum(jnp.where(seen, wanted[...], 0.0), axis=1, keepdims=True)
        line = line.astype(jnp.int32)
        places = lax.broadcasted_iota(jnp.int32, (SLOTS, ROWS_DEV), 1)
        chosen = (places == line).astype(BF16)
        picked[p] = mm(chosen, table[...]).astype(BF16).reshape(N_TABLE, 16, EMB)

        def start(k, inner):
            fetch_copy(p, k).start()
            return inner

        lax.fori_loop(1, 32, start, 0)
        replies[p, tab] = picked[p, tab]
        return carry

    lax.fori_loop(0, PAIRS, serve, 0)

    outgoing = picked

    def give_copy(last, k):
        peer = lax.rem(tab + k, 32)
        pairs = pl.ds(PAIRS - 1, 1) if last else pl.ds(0, PAIRS - 1)
        return pltpu.make_async_remote_copy(
            src_ref=outgoing.at[pairs, peer], dst_ref=incoming.at[pairs, tab],
            send_sem=a_send.at[last, k], recv_sem=a_recv.at[last, k],
            device_id=(dp, peer), device_id_type=MESH,
        )

    for load in loads[1:]:
        load.wait()

    def give(last):
        def start(k, carry):
            give_copy(last, k).start()
            return carry

        lax.fori_loop(1, 32, start, 0)

    def fetched(p):
        def landed(k, carry):
            fetch_copy(p, k).wait_recv()
            fetch_copy(p, k).wait_send()
            return carry

        lax.fori_loop(1, 32, landed, 0)

    def pair(p, carry):
        fetched(p)

        @pl.when(p == PAIRS - 1)
        def _():
            give(0)

        tokens = pl.ds(pl.multiple_of(p * TOK, TOK), TOK)
        normed_p, mixed_p, top_p, before_p, back = layer_pair(
            replies[p].reshape(SLOTS, EMB), cols_s[p], rows_s[p], up[tokens, :], wp, wo
        )
        outgoing[p] = back.reshape(N_TABLE, 16, EMB)
        incoming[p, tab] = outgoing[p, tab]
        normed_t[:, tokens] = normed_p
        mixed_t[:, tokens] = mixed_p
        up[tokens, :] = top_p
        gbs[tokens, :] = before_p
        return carry

    lax.fori_loop(0, PAIRS, pair, 0)

    def core_copy(k):
        return pltpu.make_async_remote_copy(
            src_ref=g.at[0, k], dst_ref=core_buf.at[k],
            send_sem=core_send.at[k], recv_sem=core_recv.at[k],
            device_id=other, device_id_type=MESH,
        )

    s1 = g.at[1]
    t2 = g.at[0]

    def merge(k):
        core_copy(k).wait_recv()
        core_copy(k).wait_send()

        def step(n, inner):
            s1[k, n] = (s1[k, n].astype(F32) + core_buf[k, n].astype(F32)).astype(BF16)
            return inner

        lax.fori_loop(0, 4, step, 0)

    def two(ref, n):
        return ref.at[pl.ds(2 * n, 2)]

    def add_flat(target, other_ref):
        target[...] = (target[...].astype(F32) + other_ref[...].astype(F32)).astype(BF16)

    def chosen_rows(slots, first, count):
        asked_row = req_rows[:, slots]
        places = lax.broadcasted_iota(jnp.int32, (count, asked_row.shape[1]), 0) + first
        return (places == asked_row).astype(BF16)

    def take_in(last):
        def given(k, carry):
            give_copy(last, k).wait_recv()
            return carry

        lax.fori_loop(1, 32, given, 0)

    early = (PAIRS - 1) * SLOTS

    def add_rows():
        take_in(0)

        def block(b, carry):
            rows = pl.ds(pl.multiple_of(b * 256, 256), 256)
            rows_in = incoming[0 : PAIRS - 1].reshape(early, EMB)
            sums[rows, :] = mm(chosen_rows(slice(0, early), b * 256, 256), rows_in)
            return carry

        lax.fori_loop(0, 8, block, 0)

    fars, nears, partials = (far_1, far_2, far_3), (near_1, near_2, near_3), (sum_1, sum_2, sum_3)
    last_fars = (last_far_1, last_far_2, last_far_3)
    last_nears = (last_near_1, last_near_2, last_near_3)

    def ring_on(over_y, chunk, half, far, near, number):
        place, right, left = (y, y_right, y_left) if over_y else (x, x_right, x_left)
        ring = Ring(place, right, left, chunk, half, far, near,
                    ring_send.at[number], ring_recv.at[number])
        ring.make()
        return ring

    def first_chunk(n):
        first, count, over_y = STREAMS[n]
        if over_y:
            return lambda k: s1.at[k, :, pl.ds(first, count), :]
        return lambda k: s1.at[:, k, pl.ds(first, count), :]

    def half_rows(count):
        return lambda ref, n: ref.at[pl.ds(count // 2 * n, count // 2), :]

    firsts = [
        ring_on(STREAMS[n][2], first_chunk(n), two, fars[n], nears[n], n) for n in range(3)
    ]
    seconds = [
        ring_on(not STREAMS[n][2], lambda k, n=n: partials[n].at[k], half_rows(STREAMS[n][1]),
                last_fars[n], last_nears[n], 3 + n)
        for n in range(3)
    ]

    def turn(n):
        first, count, over_y = STREAMS[n]
        firsts[n].arrive()
        for m in range(4):
            own = s1[y, m, first : first + count, :] if over_y else s1[m, x, first : first + count, :]
            total = own.astype(F32) + nears[n][0, m].astype(F32) + nears[n][1, m].astype(F32)
            partials[n][m] = total.astype(BF16)
        seconds[n].start()

    def z_copy(target, source):
        return pltpu.make_async_remote_copy(
            src_ref=s4.at[target], dst_ref=zbuf.at[source],
            send_sem=z_send.at[target], recv_sem=z_recv.at[source],
            device_id=(dp, 8 * x + target), device_id_type=MESH,
        )

    def leave(n):
        first, count, over_y = STREAMS[n]
        seconds[n].arrive()
        place = x if over_y else y
        total = partials[n][place].astype(F32) + last_nears[n][0].astype(F32)
        total = (total + last_nears[n][1].astype(F32)).astype(BF16)
        s4[first // 32 : (first + count) // 32] = total.reshape(count // 32, 32, 512)
        for target in range(first // 32, (first + count) // 32):

            @pl.when(z != target)
            def _():
                z_copy(target, z).start()

    def chunk_at(n):
        return lax.rem(y + 2 + n + (n // 2) * (1 - 2 * (n % 2)), 4)

    def terms(n, carry):
        k = chunk_at(n)
        first = mm(normed_t[...], gbs[:, pl.ds(pl.multiple_of(k * 768, 768), 768)]) * SCALE
        second = mm(mixed_t[...], up[:, pl.ds(pl.multiple_of(k * 256, 256), 256)]) * SCALE
        for which, kept in ((0, 1 - c), (1, c)):
            one = first[:, which * 384 : (which + 1) * 384].astype(BF16)
            two_ = second[:, which * 128 : (which + 1) * 128].astype(BF16)
            g[kept, k, :, :, 0:384] = one.reshape(4, 256, 384)
            g[kept, k, :, :, 384:512] = two_.reshape(4, 256, 128)
        core_copy(k).start()

        @pl.when(n > 0)
        def _():
            merge(chunk_at(n - 1))

        @pl.when(n == 1)
        def _():
            firsts[0].copies[0].start()
            firsts[0].copies[1].start()

        @pl.when(n == 2)
        def _():
            firsts[0].copies[3].start()

        @pl.when(n == 3)
        def _():
            firsts[0].copies[2].start()

        return carry

    lax.fori_loop(0, 4, terms, 0)
    merge(y)
    firsts[2].start()
    firsts[1].copies[0].start()
    firsts[1].copies[1].start()
    give(1)
    firsts[0].forward(add_into)
    firsts[1].copies[2].start()
    firsts[1].copies[3].start()
    turn(0)
    firsts[1].forward(add_into)
    firsts[2].forward(add_into)
    seconds[0].forward(add_flat)
    add_rows()
    turn(1)
    turn(2)
    leave(0)
    seconds[1].forward(add_flat)
    seconds[2].forward(add_flat)
    leave(1)
    leave(2)

    take_in(1)

    def rows_of(first):
        part = mm(chosen_rows(slice(early, early + SLOTS), first, 256), incoming[PAIRS - 1].reshape(SLOTS, EMB))
        rows = pl.ds(pl.multiple_of(first, 256), 256)
        return (sums[rows, :] + part).astype(BF16).astype(F32)

    def t_copy(b):
        lanes = pl.ds(pl.multiple_of(b * 128, 128), 128)
        return pltpu.make_async_remote_copy(
            src_ref=t2.at[1 - c, :, :, lanes], dst_ref=t_core.at[:, :, lanes],
            send_sem=core_send.at[4 + b], recv_sem=core_recv.at[4 + b],
            device_id=other, device_id_type=MESH,
        )

    def table_block(b, carry):
        upper = rows_of(b * 256)
        lower = rows_of(b * 256 + 1024)
        lanes = pl.ds(pl.multiple_of(b * 128, 128), 128)
        is_left = lax.broadcasted_iota(jnp.int32, (256, 128), 1) < 64
        for k in range(4):
            up_k, low_k = upper[:, k * 128 : (k + 1) * 128], lower[:, k * 128 : (k + 1) * 128]
            t2[0, k, :, lanes] = jnp.where(is_left, up_k, pltpu.roll(low_k, 64, 1)).astype(BF16)
            t2[1, k, :, lanes] = jnp.where(is_left, pltpu.roll(up_k, 64, 1), low_k).astype(BF16)
        t_copy(b).start()
        return carry

    def table_merge(b, carry):
        t_copy(b).wait_recv()
        lanes = pl.ds(pl.multiple_of(b * 128, 128), 128)
        for k in range(4):
            mine = t2[c, k, :, lanes].astype(F32) + t_core[k, :, lanes].astype(F32)
            t2[c, k, :, lanes] = mine.astype(BF16)
        return carry

    ring_t = Ring(y, y_right, y_left, lambda k: t2.at[c, k],
                  lambda ref, n: ref.at[:, pl.ds(256 * n, 256)], t_far, t_near,
                  ring_send.at[6], ring_recv.at[6])
    ring_t.make()
    lax.fori_loop(0, 3, table_block, 0)
    lax.fori_loop(0, 2, table_merge, 0)
    ring_t.start_half(0)
    lax.fori_loop(3, 4, table_block, 0)
    lax.fori_loop(2, 4, table_merge, 0)
    ring_t.start_half(1)

    ring_t.forward(add_flat)
    total = s4[z].astype(F32)
    for k in range(1, 8):
        source = lax.rem(z + k, 8)
        z_copy(z, source).wait_recv()
        total = total + zbuf[source].astype(F32)
    dense_ref[...] = total.astype(BF16)
    ring_t.arrive()
    total = t2[c, y].astype(F32) + t_near[0].astype(F32) + t_near[1].astype(F32)
    table_ref[...] = total.astype(BF16)

    def sent(k, carry):
        req_copy(k).wait_send()
        give_copy(0, k).wait_send()
        give_copy(1, k).wait_send()
        return carry

    lax.fori_loop(1, 32, sent, 0)
    for k in range(4):
        t_copy(k).wait_send()
    for k in range(1, 8):
        msg_copy(k).wait_send()
        z_copy(lax.rem(z + k, 8), z).wait_send()
    for ring in (*firsts, *seconds, ring_t):
        ring.end()


def output_kernel(dense_ref, sums_ref, proj_ref, outw_ref, table_ref):
    proj_ref[...] = dense_ref[:, :384]
    outw_ref[...] = dense_ref[:, 384:]
    across = sums_ref[...].astype(F32).T.astype(BF16)
    for b in range(4):
        for half in range(2):
            part = across[b * 128 + half * 64 : b * 128 + half * 64 + 64]
            table_ref[:, half * 1024 + b * 256 : half * 1024 + (b + 1) * 256] = part


def run(*arrays):
    whole = pl.BlockSpec(memory_space=pltpu.VMEM)
    anywhere = pl.BlockSpec(memory_space=pl.ANY)
    dma = pltpu.SemaphoreType.DMA
    tokens = HIST * SEQ

    def buf(*shape):
        return pltpu.VMEM(shape, BF16)

    parts = pl.pallas_call(
        program_kernel,
        out_shape=(
            jax.ShapeDtypeStruct((32, 512), BF16),
            jax.ShapeDtypeStruct((256, 512), BF16),
        ),
        in_specs=[whole] * 4 + [anywhere] * 4,
        out_specs=(whole,) * 2,
        scratch_shapes=[
            buf(ROWS_DEV, EMB), buf(tokens, D), buf(D, PROJ), buf(D, D),
            pltpu.VMEM((HIST, 8, TOK), jnp.int32),
            pltpu.VMEM((HIST, 8, TOK), jnp.int32),
            pltpu.VMEM((N_TABLE, 1, TOK), jnp.int32),
            pltpu.VMEM((N_TABLE, 1, TOK), jnp.int32),
            pltpu.VMEM((SLOTS, TOK), F32),
            pltpu.VMEM((1, PAIRS * SLOTS), jnp.int32),
            pltpu.VMEM((PAIRS, 8, TOK), jnp.int32),
            pltpu.VMEM((PAIRS, TOK, 8), jnp.int32),
            buf(PAIRS, N_TABLE, 16, EMB), buf(PAIRS, N_TABLE, 16, EMB),
            buf(PAIRS, N_TABLE, 16, EMB),
            buf(D, tokens), buf(D, tokens), buf(tokens, PROJ),
            buf(2, 4, 4, 256, 512), buf(4, 4, 256, 512), pltpu.VMEM((ROWS_DEV, EMB), F32),
            *[buf(2, 2, n, 512) for _, n, _ in STREAMS],
            *[buf(2, 4, n, 512) for _, n, _ in STREAMS],
            *[buf(4, n, 512) for _, n, _ in STREAMS],
            *[buf(2, n // 2, 512) for _, n, _ in STREAMS],
            *[buf(2, n, 512) for _, n, _ in STREAMS],
            buf(8, 32, 512), buf(8, 32, 512),
            buf(4, 256, 512), buf(2, 256, 256), buf(2, 256, 512),
            dma((4,)), dma((8,)), dma((8,)), dma((32,)), dma((32,)),
            dma((PAIRS, 32)), dma((PAIRS, 32)), dma((2, 32)), dma((2, 32)),
            dma((8,)), dma((8,)), dma((7, 6)), dma((7, 6)), dma((8,)), dma((8,)),
        ],
        compiler_params=pltpu.CompilerParams(
            vmem_limit_bytes=VMEM_LIMIT, collective_id=0, has_side_effects=True
        ),
        name="whole_program",
    )(*arrays)
    return pl.pallas_call(
        output_kernel,
        out_shape=(
            jax.ShapeDtypeStruct((32, 384), BF16),
            jax.ShapeDtypeStruct((32, 128), BF16),
            jax.ShapeDtypeStruct((64, 2048), BF16),
        ),
        in_specs=[whole] * 2,
        out_specs=(whole,) * 3,
        name="outputs",
    )(*parts)


def body(
    embed_table, owner_shard, slot_row, lengths, send_order, proj_weight, out_weight, upstream
):
    proj, outw, table = run(
        jnp.swapaxes(owner_shard[..., 0], 1, 2), jnp.swapaxes(slot_row, 1, 2),
        lengths.reshape(1, HIST), send_order, embed_table, upstream.reshape(HIST * SEQ, D),
        proj_weight, out_weight,
    )
    return table.T, proj, outw


def solution(mesh):
    in_specs = (
        P("table", None),
        P(("dp", "table"), None, None, None),
        P(("dp", "table"), None, None),
        P(("dp", "table")),
        P(("dp", "table"), None),
        P(),
        P(),
        P(("dp", "table"), None, None),
    )
    out_specs = (P("table", "dp"), P("table", "dp"), P("table", "dp"))
    return jax.shard_map(body, mesh=mesh, in_specs=in_specs, out_specs=out_specs, check_vma=False)
```

```python
import functools

import jax
import jax.numpy as jnp
from jax import lax
from jax.experimental import pallas as pl
from jax.experimental.pallas import tpu as pltpu
from jax.sharding import PartitionSpec as P

D = 1024
EMB = 512
HEADS = 8
QK = 64
PROJ = 3072
SEQ = 64
HIST = 8
ROWS_DEV = 2048
MOST = 8
N_DP = 8
N_TABLE = 32
PAIRS = HIST // 2
TOK = 2 * SEQ
SLOTS = 2 * N_TABLE * MOST
EPSILON = 1e-06
SCALE = float(2048 * 64) ** (-0.5)
MESH = pl.DeviceIdType.MESH
VMEM_LIMIT = 60 * 1024 * 1024
STREAMS = ((0, 96, True), (96, 96, True), (192, 64, False))
F32 = jnp.float32
BF16 = jnp.bfloat16


def mm(a, b):
    return lax.dot_general(a, b, (((1,), (0,)), ((), ())), preferred_element_type=F32)


def mm_nt(a, b):
    return lax.dot_general(a, b, (((1,), (1,)), ((), ())), preferred_element_type=F32)


def mm_tn(a, b):
    return lax.dot_general(a, b, (((0,), (0,)), ((), ())), preferred_element_type=F32)


def sigmoid(x):
    return 0.5 * jnp.tanh(0.5 * x) + 0.5


class Ring:
    def __init__(self, place, to_right, to_left, chunk, half, far, near, send, recv):
        self.place, self.right, self.left = place, to_right, to_left
        self.chunk, self.half, self.far, self.near = chunk, half, far, near
        self.send, self.recv = send, recv

    def copy(self, number, src, dst, device):
        return pltpu.make_async_remote_copy(
            src_ref=src, dst_ref=dst, send_sem=self.send.at[number], recv_sem=self.recv.at[number],
            device_id=device, device_id_type=MESH,
        )

    def make(self):
        across, after, ahead = (lax.rem(self.place + k, 4) for k in (2, 1, 3))
        self.after, self.ahead = after, ahead
        part, half, far, near = self.chunk, self.half, self.far, self.near
        self.copies = [
            self.copy(0, half(part(across), 0), far.at[0], self.right),
            self.copy(1, half(part(across), 1), far.at[1], self.left),
            self.copy(2, half(part(after), 1), half(near.at[0], 1), self.right),
            self.copy(3, half(part(ahead), 0), half(near.at[1], 0), self.left),
            self.copy(4, half(part(after), 0), half(near.at[0], 0), self.right),
            self.copy(5, half(part(ahead), 1), half(near.at[1], 1), self.left),
        ]

    def start_half(self, number):
        for k in ((0, 3), (1, 2))[number]:
            self.copies[k].start()

    def start(self):
        self.start_half(0)
        self.start_half(1)

    def forward(self, add):
        self.copies[0].wait_recv()
        add(self.half(self.chunk(self.after), 0), self.far.at[0])
        self.copies[4].start()
        self.copies[1].wait_recv()
        add(self.half(self.chunk(self.ahead), 1), self.far.at[1])
        self.copies[5].start()

    def arrive(self):
        for k in range(2, 6):
            self.copies[k].wait_recv()

    def end(self):
        for k in range(6):
            self.copies[k].wait_send()


def add_into(target, other):
    for n in range(target.shape[0]):
        target[n] = (target[n].astype(F32) + other[n].astype(F32)).astype(BF16)


def layer_pair(replies, cols, rows, upstream, wp, wo):
    item_at, action_at, length = cols[:, 0:1], cols[:, 1:2], cols[:, 2:3]
    places = lax.broadcasted_iota(jnp.int32, (TOK, SLOTS), 1)
    left = mm((places == item_at).astype(BF16), replies)
    right = mm((places == action_at).astype(BF16), replies)
    fetched = jnp.concatenate([left, right], axis=1)
    average = jnp.mean(fetched, axis=1, keepdims=True)
    centred = fetched - average
    rstd = lax.rsqrt(jnp.mean(centred * centred, axis=1, keepdims=True) + EPSILON)
    normed_full = centred * rstd
    normed = normed_full.astype(BF16)

    before = mm(normed, wp[...])
    gate = sigmoid(before)
    slope = gate * (1.0 + before * (1.0 - gate))
    projected = (before * gate).astype(BF16)
    u = projected[:, :D].astype(F32)
    values = projected[:, D : 2 * D]
    queries = projected[:, 2 * D : 2 * D + HEADS * QK]
    keys = projected[:, 2 * D + HEADS * QK :]

    at = lax.broadcasted_iota(jnp.int32, (TOK, TOK), 0)
    source = lax.broadcasted_iota(jnp.int32, (TOK, TOK), 1)
    seen = (source <= at) & ((at // SEQ) == (source // SEQ))
    share = jnp.where(seen, 1.0 / length.astype(F32), 0.0)
    parts = (source < QK, source >= QK)
    zero = jnp.zeros((TOK, TOK), BF16)

    weights, factors, attended = [], [], []
    for h in range(HEADS):
        two = slice((h // 2) * TOK, (h // 2 + 1) * TOK)
        key = jnp.where(parts[h % 2], keys[:, two], zero)
        score = mm_nt(queries[:, two], key)
        open_ = sigmoid(score)
        weight = (score * open_ * share).astype(BF16)
        weights.append(weight)
        factors.append(open_ * (1.0 + score * (1.0 - open_)) * share)
        attended.append(mm(weight, values[:, h * TOK : (h + 1) * TOK]))
    attended = jnp.concatenate(attended, axis=1)
    average = jnp.mean(attended, axis=1, keepdims=True)
    centred = attended - average
    spread = lax.rsqrt(jnp.mean(centred * centred, axis=1, keepdims=True) + EPSILON)
    inner = centred * spread
    mixed = inner * u

    place = lax.broadcasted_iota(jnp.int32, (TOK, D), 0) % SEQ
    top = jnp.where(place < length, upstream.astype(F32), 0.0)
    top_low = top.astype(BF16)
    grad_mixed = mm_nt(top_low, wo[...]).astype(BF16).astype(F32)
    grad_u = (grad_mixed * inner).astype(BF16)
    grad_inner = grad_mixed * u
    first = jnp.mean(grad_inner, axis=1, keepdims=True)
    second = jnp.mean(grad_inner * inner, axis=1, keepdims=True)
    grad_att = (spread * (grad_inner - first - inner * second)).astype(BF16)

    grad_v, grad_q, grad_k = [], [], []
    for h in range(HEADS):
        own = slice(h * TOK, (h + 1) * TOK)
        two = slice((h // 2) * TOK, (h // 2 + 1) * TOK)
        grad_weight = mm_nt(grad_att[:, own], values[:, own]).astype(BF16).astype(F32)
        grad_v.append(mm_tn(weights[h], grad_att[:, own]).astype(BF16))
        grad_score = (grad_weight * factors[h]).astype(BF16)
        key = jnp.where(parts[h % 2], keys[:, two], zero)
        query = jnp.where(parts[h % 2], queries[:, two], zero)
        gq = mm(grad_score, key)
        gk = mm_tn(grad_score, query)
        if h % 2:
            grad_q[-1] = (grad_q[-1] + gq).astype(BF16)
            grad_k[-1] = (grad_k[-1] + gk).astype(BF16)
        else:
            grad_q.append(gq)
            grad_k.append(gk)
    grad_projected = jnp.concatenate([grad_u] + grad_v + grad_q + grad_k, axis=1)
    grad_before = (grad_projected.astype(F32) * slope).astype(BF16)
    grad_normed = mm_nt(grad_before, wp[...])
    first = jnp.mean(grad_normed, axis=1, keepdims=True)
    second = jnp.mean(grad_normed * normed_full, axis=1, keepdims=True)
    grad_rows = (top + rstd * (grad_normed - first - normed_full * second)).astype(BF16)

    slots = lax.broadcasted_iota(jnp.int32, (SLOTS, TOK), 0)
    back = mm((slots == rows[0:1, :]).astype(BF16), grad_rows[:, :EMB])
    back = back + mm((slots == rows[1:2, :]).astype(BF16), grad_rows[:, EMB:])
    return normed_full.T.astype(BF16), mixed.T.astype(BF16), top_low, grad_before, back.astype(BF16)


def split_number(numbers):
    high = numbers // 256
    return (numbers - 256 * high).astype(BF16), high.astype(BF16)


def program_kernel(
    owner_ref, slot_ref, length_ref, order_ref, table_hbm, up_hbm, wp_hbm, wo_hbm,
    dense_ref, table_ref,
    table, up, wp, wo, msg_out, msg_in, req_out, req_in, wanted, req_rows, rows_s, cols_s,
    picked, replies, incoming, normed_t, mixed_t, gbs,
    g, core_buf, sums, far_1, far_2, far_3, near_1, near_2, near_3, sum_1, sum_2, sum_3,
    last_far_1, last_far_2, last_far_3, last_near_1, last_near_2, last_near_3,
    s4, zbuf, t_core, t_far, t_near,
    load_sem, m_send, m_recv, r_send, r_recv, f_send, f_recv, a_send, a_recv,
    core_send, core_recv, ring_send, ring_recv, z_send, z_recv,
):
    dp = lax.axis_index("dp")
    tab = lax.axis_index("table")
    y, c = dp // 2, dp % 2
    x, z = tab // 8, tab % 8
    other = (2 * y + 1 - c, tab)
    y_right = (2 * lax.rem(y + 1, 4) + c, tab)
    y_left = (2 * lax.rem(y + 3, 4) + c, tab)
    x_right = (dp, lax.rem(tab + 8, 32))
    x_left = (dp, lax.rem(tab + 24, 32))

    loads = [
        pltpu.make_async_copy(src, dst, load_sem.at[n])
        for n, (src, dst) in enumerate(
            ((table_hbm, table), (up_hbm, up), (wp_hbm, wp), (wo_hbm, wo))
        )
    ]
    for load in loads:
        load.start()

    barrier = pltpu.get_barrier_semaphore()

    def greet_dp(k, carry):
        pl.semaphore_signal(
            barrier, inc=1, device_id=(lax.rem(dp + k, 8), tab), device_id_type=MESH
        )
        return carry

    def greet_table(k, carry):
        pl.semaphore_signal(
            barrier, inc=1, device_id=(dp, lax.rem(tab + k, 32)), device_id_type=MESH
        )
        return carry

    lax.fori_loop(1, 8, greet_dp, 0)
    lax.fori_loop(1, 32, greet_table, 0)

    order = order_ref[...]
    rows_of_table = [owner_ref[m] * ROWS_DEV + slot_ref[m] for m in range(HIST)]
    for k in range(HIST):
        at = order[:, k : k + 1]
        lookups = jnp.zeros((2, SEQ), jnp.int32)
        length = jnp.zeros((1, 1), jnp.int32)
        for m in range(HIST):
            lookups = jnp.where(jnp.broadcast_to(at, (2, SEQ)) == m, rows_of_table[m], lookups)
            length = jnp.where(at == m, length_ref[:, m : m + 1], length)
        msg_out[k, 0:2, 0:SEQ] = lookups
        msg_out[k, 2:3, 0:SEQ] = jnp.broadcast_to(length, (1, SEQ))
    pl.semaphore_wait(barrier, 38)

    def msg_copy(k):
        peer = lax.rem(dp + k, 8)
        return pltpu.make_async_remote_copy(
            src_ref=msg_out.at[peer], dst_ref=msg_in.at[dp],
            send_sem=m_send.at[k], recv_sem=m_recv.at[k],
            device_id=(peer, tab), device_id_type=MESH,
        )

    for k in range(1, 8):
        msg_copy(k).start()
    msg_in[dp] = msg_out[dp]
    for k in range(1, 8):
        msg_copy(k).wait_recv()

    items = jnp.concatenate([msg_in[k, 0:1, :] for k in range(HIST)], axis=0)
    actions = jnp.concatenate([msg_in[k, 1:2, :] for k in range(HIST)], axis=0)
    lengths = jnp.concatenate([msg_in[k, 2:3, :] for k in range(HIST)], axis=0)[:, 0:1]
    is_item = lax.broadcasted_iota(jnp.int32, (HIST, TOK), 1) < SEQ
    ids = jnp.where(is_item, items, pltpu.roll(actions, SEQ, 1))
    owner = ids // ROWS_DEV
    ids_col = ids.astype(F32).T.astype(jnp.int32)
    owner_col, row_col = ids_col // ROWS_DEV, ids_col % ROWS_DEV
    sub = lax.broadcasted_iota(jnp.int32, (TOK, TOK), 0)
    lane = lax.broadcasted_iota(jnp.int32, (TOK, TOK), 1)
    ranks = []
    for m in range(HIST):
        same = (owner_col[:, m : m + 1] == owner[m : m + 1, :]) & (sub < lane)
        ranks.append(jnp.sum(jnp.where(same, 1.0, 0.0), axis=0, keepdims=True))
    rank = jnp.concatenate(ranks, axis=0)
    rank_col = rank.T.astype(jnp.int32)
    request = jnp.zeros((N_TABLE, TOK), F32)
    owners = lax.broadcasted_iota(jnp.int32, (N_TABLE, TOK), 0)
    for m in range(HIST):
        low, high = split_number(row_col[:, m : m + 1] + 1)
        spot = m * MOST + rank_col[:, m : m + 1]
        put = jnp.where(lane == spot, low.astype(F32), 0.0)
        put = jnp.where(lane == spot + 64, high.astype(F32), put)
        request = request + mm((owners == owner[m : m + 1, :]).astype(BF16), put.astype(BF16))
    request = request + 256.0 * pltpu.roll(request, 64, 1)
    request = jnp.where(owners >= 0, request, 0.0)
    request = jnp.where(lax.broadcasted_iota(jnp.int32, (N_TABLE, TOK), 1) < 64, request, 0.0)
    request = request.astype(jnp.int32)
    for o in range(N_TABLE):
        req_out[o] = request[o : o + 1, :]

    def req_copy(k):
        peer = lax.rem(tab + k, 32)
        return pltpu.make_async_remote_copy(
            src_ref=req_out.at[peer], dst_ref=req_in.at[tab],
            send_sem=r_send.at[k], recv_sem=r_recv.at[k],
            device_id=(dp, peer), device_id_type=MESH,
        )

    def ask(k, carry):
        req_copy(k).start()
        return carry

    lax.fori_loop(1, 32, ask, 0)
    req_in[tab] = req_out[tab]

    slot = owner * 16 + rank.astype(jnp.int32)
    first_half = lax.broadcasted_iota(jnp.int32, (1, TOK), 1) < SEQ
    for p in range(PAIRS):
        a = slot[2 * p : 2 * p + 1, :]
        b = slot[2 * p + 1 : 2 * p + 2, :] + MOST
        item = jnp.where(first_half, a, pltpu.roll(b, SEQ, 1))
        action = jnp.where(first_half, pltpu.roll(a, SEQ, 1), b)
        length = jnp.where(first_half, lengths[2 * p : 2 * p + 1], lengths[2 * p + 1 : 2 * p + 2])
        block = jnp.concatenate([item, action, length, length] * 2, axis=0)
        rows_s[p] = block
        cols_s[p] = block.astype(F32).T.astype(jnp.int32)

    def asked(k, carry):
        req_copy(k).wait_recv()
        return carry

    lax.fori_loop(1, 32, asked, 0)
    asks = jnp.concatenate([req_in[k] for k in range(N_TABLE)], axis=0)
    low, high = split_number(asks)
    tall = lax.broadcasted_iota(jnp.int32, (SLOTS, N_TABLE), 0) // 16
    tall = (tall == lax.broadcasted_iota(jnp.int32, (SLOTS, N_TABLE), 1)).astype(BF16)
    wanted[...] = mm(tall, low) + 256.0 * mm(tall, high) - 1.0
    wide = lax.broadcasted_iota(jnp.int32, (N_TABLE, SLOTS), 1) // 16
    wide = (wide == lax.broadcasted_iota(jnp.int32, (N_TABLE, SLOTS), 0)).astype(BF16)
    across = mm_tn(low, wide) + 256.0 * mm_tn(high, wide) - 1.0
    at = lax.broadcasted_iota(jnp.int32, (TOK, SLOTS), 0)
    in_owner = lax.broadcasted_iota(jnp.int32, (TOK, SLOTS), 1) % 16
    for p in range(PAIRS):
        line = jnp.sum(jnp.where(at == in_owner + 16 * p, across, 0.0), axis=0, keepdims=True)
        req_rows[:, p * SLOTS : (p + 1) * SLOTS] = line.astype(jnp.int32)

    def fetch_copy(p, k):
        peer = lax.rem(tab + k, 32)
        return pltpu.make_async_remote_copy(
            src_ref=picked.at[p, peer], dst_ref=replies.at[p, tab],
            send_sem=f_send.at[p, k], recv_sem=f_recv.at[p, k],
            device_id=(dp, peer), device_id_type=MESH,
        )

    loads[0].wait()

    def serve(p, carry):
        at = lax.broadcasted_iota(jnp.int32, (SLOTS, TOK), 0) % 16 + 16 * p
        seen = lax.broadcasted_iota(jnp.int32, (SLOTS, TOK), 1) == at
        line = jnp.sum(jnp.where(seen, wanted[...], 0.0), axis=1, keepdims=True)
        line = line.astype(jnp.int32)
        places = lax.broadcasted_iota(jnp.int32, (SLOTS, ROWS_DEV), 1)
        chosen = (places == line).astype(BF16)
        picked[p] = mm(chosen, table[...]).astype(BF16).reshape(N_TABLE, 16, EMB)

        def start(k, inner):
            fetch_copy(p, k).start()
            return inner

        lax.fori_loop(1, 32, start, 0)
        replies[p, tab] = picked[p, tab]
        return carry

    lax.fori_loop(0, PAIRS, serve, 0)

    outgoing = picked

    def give_copy(last, k):
        peer = lax.rem(tab + k, 32)
        pairs = pl.ds(PAIRS - 1, 1) if last else pl.ds(0, PAIRS - 1)
        return pltpu.make_async_remote_copy(
            src_ref=outgoing.at[pairs, peer], dst_ref=incoming.at[pairs, tab],
            send_sem=a_send.at[last, k], recv_sem=a_recv.at[last, k],
            device_id=(dp, peer), device_id_type=MESH,
        )

    for load in loads[1:]:
        load.wait()

    def give(last):
        def start(k, carry):
            give_copy(last, k).start()
            return carry

        lax.fori_loop(1, 32, start, 0)

    def fetched(p):
        def landed(k, carry):
            fetch_copy(p, k).wait_recv()
            fetch_copy(p, k).wait_send()
            return carry

        lax.fori_loop(1, 32, landed, 0)

    def pair(p, carry):
        fetched(p)

        @pl.when(p == PAIRS - 1)
        def _():
            give(0)

        tokens = pl.ds(pl.multiple_of(p * TOK, TOK), TOK)
        normed_p, mixed_p, top_p, before_p, back = layer_pair(
            replies[p].reshape(SLOTS, EMB), cols_s[p], rows_s[p], up[tokens, :], wp, wo
        )
        outgoing[p] = back.reshape(N_TABLE, 16, EMB)
        incoming[p, tab] = outgoing[p, tab]
        normed_t[:, tokens] = normed_p
        mixed_t[:, tokens] = mixed_p
        up[tokens, :] = top_p
        gbs[tokens, :] = before_p
        return carry

    lax.fori_loop(0, PAIRS, pair, 0)

    def core_copy(k):
        return pltpu.make_async_remote_copy(
            src_ref=g.at[0, k], dst_ref=core_buf.at[k],
            send_sem=core_send.at[k], recv_sem=core_recv.at[k],
            device_id=other, device_id_type=MESH,
        )

    s1 = g.at[1]
    t2 = g.at[0]

    def merge(k):
        core_copy(k).wait_recv()
        core_copy(k).wait_send()

        def step(n, inner):
            s1[k, n] = (s1[k, n].astype(F32) + core_buf[k, n].astype(F32)).astype(BF16)
            return inner

        lax.fori_loop(0, 4, step, 0)

    def two(ref, n):
        return ref.at[pl.ds(2 * n, 2)]

    def add_flat(target, other_ref):
        target[...] = (target[...].astype(F32) + other_ref[...].astype(F32)).astype(BF16)

    def chosen_rows(slots, first, count):
        asked_row = req_rows[:, slots]
        places = lax.broadcasted_iota(jnp.int32, (count, asked_row.shape[1]), 0) + first
        return (places == asked_row).astype(BF16)

    def take_in(last):
        def given(k, carry):
            give_copy(last, k).wait_recv()
            return carry

        lax.fori_loop(1, 32, given, 0)

    early = (PAIRS - 1) * SLOTS

    def add_rows():
        take_in(0)

        def block(b, carry):
            rows = pl.ds(pl.multiple_of(b * 256, 256), 256)
            rows_in = incoming[0 : PAIRS - 1].reshape(early, EMB)
            sums[rows, :] = mm(chosen_rows(slice(0, early), b * 256, 256), rows_in)
            return carry

        lax.fori_loop(0, 8, block, 0)

    fars, nears, partials = (far_1, far_2, far_3), (near_1, near_2, near_3), (sum_1, sum_2, sum_3)
    last_fars = (last_far_1, last_far_2, last_far_3)
    last_nears = (last_near_1, last_near_2, last_near_3)

    def ring_on(over_y, chunk, half, far, near, number):
        place, right, left = (y, y_right, y_left) if over_y else (x, x_right, x_left)
        ring = Ring(place, right, left, chunk, half, far, near,
                    ring_send.at[number], ring_recv.at[number])
        ring.make()
        return ring

    def first_chunk(n):
        first, count, over_y = STREAMS[n]
        if over_y:
            return lambda k: s1.at[k, :, pl.ds(first, count), :]
        return lambda k: s1.at[:, k, pl.ds(first, count), :]

    def half_rows(count):
        return lambda ref, n: ref.at[pl.ds(count // 2 * n, count // 2), :]

    firsts = [
        ring_on(STREAMS[n][2], first_chunk(n), two, fars[n], nears[n], n) for n in range(3)
    ]
    seconds = [
        ring_on(not STREAMS[n][2], lambda k, n=n: partials[n].at[k], half_rows(STREAMS[n][1]),
                last_fars[n], last_nears[n], 3 + n)
        for n in range(3)
    ]

    def turn(n):
        first, count, over_y = STREAMS[n]
        firsts[n].arrive()
        for m in range(4):
            own = s1[y, m, first : first + count, :] if over_y else s1[m, x, first : first + count, :]
            total = own.astype(F32) + nears[n][0, m].astype(F32) + nears[n][1, m].astype(F32)
            partials[n][m] = total.astype(BF16)
        seconds[n].start()

    def z_copy(target, source):
        return pltpu.make_async_remote_copy(
            src_ref=s4.at[target], dst_ref=zbuf.at[source],
            send_sem=z_send.at[target], recv_sem=z_recv.at[source],
            device_id=(dp, 8 * x + target), device_id_type=MESH,
        )

    def leave(n):
        first, count, over_y = STREAMS[n]
        seconds[n].arrive()
        place = x if over_y else y
        total = partials[n][place].astype(F32) + last_nears[n][0].astype(F32)
        total = (total + last_nears[n][1].astype(F32)).astype(BF16)
        s4[first // 32 : (first + count) // 32] = total.reshape(count // 32, 32, 512)
        for target in range(first // 32, (first + count) // 32):

            @pl.when(z != target)
            def _():
                z_copy(target, z).start()

    def chunk_at(n):
        return lax.rem(y + 2 + n + (n // 2) * (1 - 2 * (n % 2)), 4)

    def terms(n, carry):
        k = chunk_at(n)
        first = mm(normed_t[...], gbs[:, pl.ds(pl.multiple_of(k * 768, 768), 768)]) * SCALE
        second = mm(mixed_t[...], up[:, pl.ds(pl.multiple_of(k * 256, 256), 256)]) * SCALE
        for which, kept in ((0, 1 - c), (1, c)):
            one = first[:, which * 384 : (which + 1) * 384].astype(BF16)
            two_ = second[:, which * 128 : (which + 1) * 128].astype(BF16)
            g[kept, k, :, :, 0:384] = one.reshape(4, 256, 384)
            g[kept, k, :, :, 384:512] = two_.reshape(4, 256, 128)
        core_copy(k).start()

        @pl.when(n > 0)
        def _():
            merge(chunk_at(n - 1))

        @pl.when(n == 1)
        def _():
            firsts[0].copies[0].start()
            firsts[0].copies[1].start()

        @pl.when(n == 2)
        def _():
            firsts[0].copies[3].start()

        @pl.when(n == 3)
        def _():
            firsts[0].copies[2].start()

        return carry

    lax.fori_loop(0, 4, terms, 0)
    merge(y)
    firsts[2].start()
    firsts[1].copies[0].start()
    firsts[1].copies[1].start()
    give(1)
    firsts[0].forward(add_into)
    firsts[1].copies[2].start()
    firsts[1].copies[3].start()
    turn(0)
    firsts[1].forward(add_into)
    firsts[2].forward(add_into)
    seconds[0].forward(add_flat)
    add_rows()
    turn(1)
    turn(2)
    leave(0)
    seconds[1].forward(add_flat)
    seconds[2].forward(add_flat)

    take_in(1)

    def rows_of(first):
        part = mm(chosen_rows(slice(early, early + SLOTS), first, 256), incoming[PAIRS - 1].reshape(SLOTS, EMB))
        rows = pl.ds(pl.multiple_of(first, 256), 256)
        return (sums[rows, :] + part).astype(BF16).astype(F32)

    def t_copy(b):
        lanes = pl.ds(pl.multiple_of(b * 128, 128), 128)
        return pltpu.make_async_remote_copy(
            src_ref=t2.at[1 - c, :, :, lanes], dst_ref=t_core.at[:, :, lanes],
            send_sem=core_send.at[4 + b], recv_sem=core_recv.at[4 + b],
            device_id=other, device_id_type=MESH,
        )

    def table_block(b, carry):
        upper = rows_of(b * 256)
        lower = rows_of(b * 256 + 1024)
        lanes = pl.ds(pl.multiple_of(b * 128, 128), 128)
        is_left = lax.broadcasted_iota(jnp.int32, (256, 128), 1) < 64
        for k in range(4):
            up_k, low_k = upper[:, k * 128 : (k + 1) * 128], lower[:, k * 128 : (k + 1) * 128]
            t2[0, k, :, lanes] = jnp.where(is_left, up_k, pltpu.roll(low_k, 64, 1)).astype(BF16)
            t2[1, k, :, lanes] = jnp.where(is_left, pltpu.roll(up_k, 64, 1), low_k).astype(BF16)
        t_copy(b).start()
        return carry

    def table_merge(b, carry):
        t_copy(b).wait_recv()
        lanes = pl.ds(pl.multiple_of(b * 128, 128), 128)
        for k in range(4):
            mine = t2[c, k, :, lanes].astype(F32) + t_core[k, :, lanes].astype(F32)
            t2[c, k, :, lanes] = mine.astype(BF16)
        return carry

    ring_t = Ring(y, y_right, y_left, lambda k: t2.at[c, k],
                  lambda ref, n: ref.at[:, pl.ds(256 * n, 256)], t_far, t_near,
                  ring_send.at[6], ring_recv.at[6])
    ring_t.make()
    lax.fori_loop(0, 3, table_block, 0)
    lax.fori_loop(0, 2, table_merge, 0)
    ring_t.start_half(0)
    lax.fori_loop(3, 4, table_block, 0)
    lax.fori_loop(2, 4, table_merge, 0)
    ring_t.start_half(1)
    leave(1)
    leave(2)

    ring_t.forward(add_flat)

    def sent(k, carry):
        req_copy(k).wait_send()
        give_copy(0, k).wait_send()
        give_copy(1, k).wait_send()
        return carry

    lax.fori_loop(1, 32, sent, 0)
    total = s4[z].astype(F32)
    for k in range(1, 8):
        source = lax.rem(z + k, 8)
        z_copy(z, source).wait_recv()
        total = total + zbuf[source].astype(F32)
    dense_ref[...] = total.astype(BF16)
    ring_t.arrive()
    total = t2[c, y].astype(F32) + t_near[0].astype(F32) + t_near[1].astype(F32)
    table_ref[...] = total.astype(BF16)

    for k in range(4):
        t_copy(k).wait_send()
    for k in range(1, 8):
        msg_copy(k).wait_send()
        z_copy(lax.rem(z + k, 8), z).wait_send()
    for ring in (*firsts, *seconds, ring_t):
        ring.end()


def output_kernel(dense_ref, sums_ref, proj_ref, outw_ref, table_ref):
    proj_ref[...] = dense_ref[:, :384]
    outw_ref[...] = dense_ref[:, 384:]
    across = sums_ref[...].astype(F32).T.astype(BF16)
    for b in range(4):
        for half in range(2):
            part = across[b * 128 + half * 64 : b * 128 + half * 64 + 64]
            table_ref[:, half * 1024 + b * 256 : half * 1024 + (b + 1) * 256] = part


def run(*arrays):
    whole = pl.BlockSpec(memory_space=pltpu.VMEM)
    anywhere = pl.BlockSpec(memory_space=pl.ANY)
    dma = pltpu.SemaphoreType.DMA
    tokens = HIST * SEQ

    def buf(*shape):
        return pltpu.VMEM(shape, BF16)

    parts = pl.pallas_call(
        program_kernel,
        out_shape=(
            jax.ShapeDtypeStruct((32, 512), BF16),
            jax.ShapeDtypeStruct((256, 512), BF16),
        ),
        in_specs=[whole] * 4 + [anywhere] * 4,
        out_specs=(whole,) * 2,
        scratch_shapes=[
            buf(ROWS_DEV, EMB), buf(tokens, D), buf(D, PROJ), buf(D, D),
            pltpu.VMEM((HIST, 8, TOK), jnp.int32),
            pltpu.VMEM((HIST, 8, TOK), jnp.int32),
            pltpu.VMEM((N_TABLE, 1, TOK), jnp.int32),
            pltpu.VMEM((N_TABLE, 1, TOK), jnp.int32),
            pltpu.VMEM((SLOTS, TOK), F32),
            pltpu.VMEM((1, PAIRS * SLOTS), jnp.int32),
            pltpu.VMEM((PAIRS, 8, TOK), jnp.int32),
            pltpu.VMEM((PAIRS, TOK, 8), jnp.int32),
            buf(PAIRS, N_TABLE, 16, EMB), buf(PAIRS, N_TABLE, 16, EMB),
            buf(PAIRS, N_TABLE, 16, EMB),
            buf(D, tokens), buf(D, tokens), buf(tokens, PROJ),
            buf(2, 4, 4, 256, 512), buf(4, 4, 256, 512), pltpu.VMEM((ROWS_DEV, EMB), F32),
            *[buf(2, 2, n, 512) for _, n, _ in STREAMS],
            *[buf(2, 4, n, 512) for _, n, _ in STREAMS],
            *[buf(4, n, 512) for _, n, _ in STREAMS],
            *[buf(2, n // 2, 512) for _, n, _ in STREAMS],
            *[buf(2, n, 512) for _, n, _ in STREAMS],
            buf(8, 32, 512), buf(8, 32, 512),
            buf(4, 256, 512), buf(2, 256, 256), buf(2, 256, 512),
            dma((4,)), dma((8,)), dma((8,)), dma((32,)), dma((32,)),
            dma((PAIRS, 32)), dma((PAIRS, 32)), dma((2, 32)), dma((2, 32)),
            dma((8,)), dma((8,)), dma((7, 6)), dma((7, 6)), dma((8,)), dma((8,)),
        ],
        compiler_params=pltpu.CompilerParams(
            vmem_limit_bytes=VMEM_LIMIT, collective_id=0, has_side_effects=True
        ),
        name="whole_program",
    )(*arrays)
    return pl.pallas_call(
        output_kernel,
        out_shape=(
            jax.ShapeDtypeStruct((32, 384), BF16),
            jax.ShapeDtypeStruct((32, 128), BF16),
            jax.ShapeDtypeStruct((64, 2048), BF16),
        ),
        in_specs=[whole] * 2,
        out_specs=(whole,) * 3,
        name="outputs",
    )(*parts)


def body(
    embed_table, owner_shard, slot_row, lengths, send_order, proj_weight, out_weight, upstream
):
    proj, outw, table = run(
        jnp.swapaxes(owner_shard[..., 0], 1, 2), jnp.swapaxes(slot_row, 1, 2),
        lengths.reshape(1, HIST), send_order, embed_table, upstream.reshape(HIST * SEQ, D),
        proj_weight, out_weight,
    )
    return table.T, proj, outw


def solution(mesh):
    in_specs = (
        P("table", None),
        P(("dp", "table"), None, None, None),
        P(("dp", "table"), None, None),
        P(("dp", "table")),
        P(("dp", "table"), None),
        P(),
        P(),
        P(("dp", "table"), None, None),
    )
    out_specs = (P("table", "dp"), P("table", "dp"), P("table", "dp"))
    return jax.shard_map(body, mesh=mesh, in_specs=in_specs, out_specs=out_specs, check_vma=False)
```

```python
import functools

import jax
import jax.numpy as jnp
from jax import lax
from jax.experimental import pallas as pl
from jax.experimental.pallas import tpu as pltpu
from jax.sharding import PartitionSpec as P

D = 1024
EMB = 512
HEADS = 8
QK = 64
PROJ = 3072
SEQ = 64
HIST = 8
ROWS_DEV = 2048
MOST = 8
N_DP = 8
N_TABLE = 32
PAIRS = HIST // 2
TOK = 2 * SEQ
SLOTS = 2 * N_TABLE * MOST
EPSILON = 1e-06
SCALE = float(2048 * 64) ** (-0.5)
MESH = pl.DeviceIdType.MESH
VMEM_LIMIT = 60 * 1024 * 1024
STREAMS = ((0, 96, True), (96, 96, True), (192, 64, False))
F32 = jnp.float32
BF16 = jnp.bfloat16


def mm(a, b):
    return lax.dot_general(a, b, (((1,), (0,)), ((), ())), preferred_element_type=F32)


def mm_nt(a, b):
    return lax.dot_general(a, b, (((1,), (1,)), ((), ())), preferred_element_type=F32)


def mm_tn(a, b):
    return lax.dot_general(a, b, (((0,), (0,)), ((), ())), preferred_element_type=F32)


def sigmoid(x):
    return 0.5 * jnp.tanh(0.5 * x) + 0.5


class Ring:
    def __init__(self, place, to_right, to_left, chunk, half, far, near, send, recv):
        self.place, self.right, self.left = place, to_right, to_left
        self.chunk, self.half, self.far, self.near = chunk, half, far, near
        self.send, self.recv = send, recv

    def copy(self, number, src, dst, device):
        return pltpu.make_async_remote_copy(
            src_ref=src, dst_ref=dst, send_sem=self.send.at[number], recv_sem=self.recv.at[number],
            device_id=device, device_id_type=MESH,
        )

    def make(self):
        across, after, ahead = (lax.rem(self.place + k, 4) for k in (2, 1, 3))
        self.after, self.ahead = after, ahead
        part, half, far, near = self.chunk, self.half, self.far, self.near
        self.copies = [
            self.copy(0, half(part(across), 0), far.at[0], self.right),
            self.copy(1, half(part(across), 1), far.at[1], self.left),
            self.copy(2, half(part(after), 1), half(near.at[0], 1), self.right),
            self.copy(3, half(part(ahead), 0), half(near.at[1], 0), self.left),
            self.copy(4, half(part(after), 0), half(near.at[0], 0), self.right),
            self.copy(5, half(part(ahead), 1), half(near.at[1], 1), self.left),
        ]

    def start_half(self, number):
        for k in ((0, 3), (1, 2))[number]:
            self.copies[k].start()

    def start(self):
        self.start_half(0)
        self.start_half(1)

    def forward(self, add):
        self.copies[0].wait_recv()
        add(self.half(self.chunk(self.after), 0), self.far.at[0])
        self.copies[4].start()
        self.copies[1].wait_recv()
        add(self.half(self.chunk(self.ahead), 1), self.far.at[1])
        self.copies[5].start()

    def arrive(self):
        for k in range(2, 6):
            self.copies[k].wait_recv()

    def end(self):
        for k in range(6):
            self.copies[k].wait_send()


def add_into(target, other):
    for n in range(target.shape[0]):
        target[n] = (target[n].astype(F32) + other[n].astype(F32)).astype(BF16)


def layer_pair(replies, cols, rows, upstream, wp, wo):
    item_at, action_at, length = cols[:, 0:1], cols[:, 1:2], cols[:, 2:3]
    places = lax.broadcasted_iota(jnp.int32, (TOK, SLOTS), 1)
    left = mm((places == item_at).astype(BF16), replies)
    right = mm((places == action_at).astype(BF16), replies)
    fetched = jnp.concatenate([left, right], axis=1)
    average = jnp.mean(fetched, axis=1, keepdims=True)
    centred = fetched - average
    rstd = lax.rsqrt(jnp.mean(centred * centred, axis=1, keepdims=True) + EPSILON)
    normed_full = centred * rstd
    normed = normed_full.astype(BF16)

    before = mm(normed, wp[...])
    gate = sigmoid(before)
    slope = gate * (1.0 + before * (1.0 - gate))
    projected = (before * gate).astype(BF16)
    u = projected[:, :D].astype(F32)
    values = projected[:, D : 2 * D]
    queries = projected[:, 2 * D : 2 * D + HEADS * QK]
    keys = projected[:, 2 * D + HEADS * QK :]

    at = lax.broadcasted_iota(jnp.int32, (TOK, TOK), 0)
    source = lax.broadcasted_iota(jnp.int32, (TOK, TOK), 1)
    seen = (source <= at) & ((at // SEQ) == (source // SEQ))
    share = jnp.where(seen, 1.0 / length.astype(F32), 0.0)
    parts = (source < QK, source >= QK)
    zero = jnp.zeros((TOK, TOK), BF16)

    weights, factors, attended = [], [], []
    for h in range(HEADS):
        two = slice((h // 2) * TOK, (h // 2 + 1) * TOK)
        key = jnp.where(parts[h % 2], keys[:, two], zero)
        score = mm_nt(queries[:, two], key)
        open_ = sigmoid(score)
        weight = (score * open_ * share).astype(BF16)
        weights.append(weight)
        factors.append(open_ * (1.0 + score * (1.0 - open_)) * share)
        attended.append(mm(weight, values[:, h * TOK : (h + 1) * TOK]))
    attended = jnp.concatenate(attended, axis=1)
    average = jnp.mean(attended, axis=1, keepdims=True)
    centred = attended - average
    spread = lax.rsqrt(jnp.mean(centred * centred, axis=1, keepdims=True) + EPSILON)
    inner = centred * spread
    mixed = inner * u

    place = lax.broadcasted_iota(jnp.int32, (TOK, D), 0) % SEQ
    top = jnp.where(place < length, upstream.astype(F32), 0.0)
    top_low = top.astype(BF16)
    grad_mixed = mm_nt(top_low, wo[...]).astype(BF16).astype(F32)
    grad_u = (grad_mixed * inner).astype(BF16)
    grad_inner = grad_mixed * u
    first = jnp.mean(grad_inner, axis=1, keepdims=True)
    second = jnp.mean(grad_inner * inner, axis=1, keepdims=True)
    grad_att = (spread * (grad_inner - first - inner * second)).astype(BF16)

    grad_v, grad_q, grad_k = [], [], []
    for h in range(HEADS):
        own = slice(h * TOK, (h + 1) * TOK)
        two = slice((h // 2) * TOK, (h // 2 + 1) * TOK)
        grad_weight = mm_nt(grad_att[:, own], values[:, own]).astype(BF16).astype(F32)
        grad_v.append(mm_tn(weights[h], grad_att[:, own]).astype(BF16))
        grad_score = (grad_weight * factors[h]).astype(BF16)
        key = jnp.where(parts[h % 2], keys[:, two], zero)
        query = jnp.where(parts[h % 2], queries[:, two], zero)
        gq = mm(grad_score, key)
        gk = mm_tn(grad_score, query)
        if h % 2:
            grad_q[-1] = (grad_q[-1] + gq).astype(BF16)
            grad_k[-1] = (grad_k[-1] + gk).astype(BF16)
        else:
            grad_q.append(gq)
            grad_k.append(gk)
    grad_projected = jnp.concatenate([grad_u] + grad_v + grad_q + grad_k, axis=1)
    grad_before = (grad_projected.astype(F32) * slope).astype(BF16)
    grad_normed = mm_nt(grad_before, wp[...])
    first = jnp.mean(grad_normed, axis=1, keepdims=True)
    second = jnp.mean(grad_normed * normed_full, axis=1, keepdims=True)
    grad_rows = (top + rstd * (grad_normed - first - normed_full * second)).astype(BF16)

    slots = lax.broadcasted_iota(jnp.int32, (SLOTS, TOK), 0)
    back = mm((slots == rows[0:1, :]).astype(BF16), grad_rows[:, :EMB])
    back = back + mm((slots == rows[1:2, :]).astype(BF16), grad_rows[:, EMB:])
    return normed_full.T.astype(BF16), mixed.T.astype(BF16), top_low, grad_before, back.astype(BF16)


def split_number(numbers):
    high = numbers // 256
    return (numbers - 256 * high).astype(BF16), high.astype(BF16)


def program_kernel(
    owner_ref, slot_ref, length_ref, order_ref, table_hbm, up_hbm, wp_hbm, wo_hbm,
    dense_ref, table_ref,
    table, up, wp, wo, msg_out, msg_in, req_out, req_in, wanted, req_rows, rows_s, cols_s,
    picked, replies, incoming, normed_t, mixed_t, gbs,
    g, core_buf, sums, far_1, far_2, far_3, near_1, near_2, near_3, sum_1, sum_2, sum_3,
    last_far_1, last_far_2, last_far_3, last_near_1, last_near_2, last_near_3,
    s4, zbuf, t_core, t_far, t_near,
    load_sem, m_send, m_recv, r_send, r_recv, f_send, f_recv, a_send, a_recv,
    core_send, core_recv, ring_send, ring_recv, z_send, z_recv,
):
    dp = lax.axis_index("dp")
    tab = lax.axis_index("table")
    y, c = dp // 2, dp % 2
    x, z = tab // 8, tab % 8
    other = (2 * y + 1 - c, tab)
    y_right = (2 * lax.rem(y + 1, 4) + c, tab)
    y_left = (2 * lax.rem(y + 3, 4) + c, tab)
    x_right = (dp, lax.rem(tab + 8, 32))
    x_left = (dp, lax.rem(tab + 24, 32))

    loads = [
        pltpu.make_async_copy(src, dst, load_sem.at[n])
        for n, (src, dst) in enumerate(
            ((table_hbm, table), (up_hbm, up), (wp_hbm, wp), (wo_hbm, wo))
        )
    ]
    for load in loads:
        load.start()

    barrier = pltpu.get_barrier_semaphore()

    def greet_dp(k, carry):
        pl.semaphore_signal(
            barrier, inc=1, device_id=(lax.rem(dp + k, 8), tab), device_id_type=MESH
        )
        return carry

    def greet_table(k, carry):
        pl.semaphore_signal(
            barrier, inc=1, device_id=(dp, lax.rem(tab + k, 32)), device_id_type=MESH
        )
        return carry

    lax.fori_loop(1, 8, greet_dp, 0)
    lax.fori_loop(1, 32, greet_table, 0)

    order = order_ref[...]
    rows_of_table = [owner_ref[m] * ROWS_DEV + slot_ref[m] for m in range(HIST)]
    for k in range(HIST):
        at = order[:, k : k + 1]
        lookups = jnp.zeros((2, SEQ), jnp.int32)
        length = jnp.zeros((1, 1), jnp.int32)
        for m in range(HIST):
            lookups = jnp.where(jnp.broadcast_to(at, (2, SEQ)) == m, rows_of_table[m], lookups)
            length = jnp.where(at == m, length_ref[:, m : m + 1], length)
        msg_out[k, 0:2, 0:SEQ] = lookups
        msg_out[k, 2:3, 0:SEQ] = jnp.broadcast_to(length, (1, SEQ))
    pl.semaphore_wait(barrier, 38)

    def msg_copy(k):
        peer = lax.rem(dp + k, 8)
        return pltpu.make_async_remote_copy(
            src_ref=msg_out.at[peer], dst_ref=msg_in.at[dp],
            send_sem=m_send.at[k], recv_sem=m_recv.at[k],
            device_id=(peer, tab), device_id_type=MESH,
        )

    for k in range(1, 8):
        msg_copy(k).start()
    msg_in[dp] = msg_out[dp]
    for k in range(1, 8):
        msg_copy(k).wait_recv()

    items = jnp.concatenate([msg_in[k, 0:1, :] for k in range(HIST)], axis=0)
    actions = jnp.concatenate([msg_in[k, 1:2, :] for k in range(HIST)], axis=0)
    lengths = jnp.concatenate([msg_in[k, 2:3, :] for k in range(HIST)], axis=0)[:, 0:1]
    is_item = lax.broadcasted_iota(jnp.int32, (HIST, TOK), 1) < SEQ
    ids = jnp.where(is_item, items, pltpu.roll(actions, SEQ, 1))
    owner = ids // ROWS_DEV
    ids_col = ids.astype(F32).T.astype(jnp.int32)
    owner_col, row_col = ids_col // ROWS_DEV, ids_col % ROWS_DEV
    sub = lax.broadcasted_iota(jnp.int32, (TOK, TOK), 0)
    lane = lax.broadcasted_iota(jnp.int32, (TOK, TOK), 1)
    ranks = []
    for m in range(HIST):
        same = (owner_col[:, m : m + 1] == owner[m : m + 1, :]) & (sub < lane)
        ranks.append(jnp.sum(jnp.where(same, 1.0, 0.0), axis=0, keepdims=True))
    rank = jnp.concatenate(ranks, axis=0)
    rank_col = rank.T.astype(jnp.int32)
    request = jnp.zeros((N_TABLE, TOK), F32)
    owners = lax.broadcasted_iota(jnp.int32, (N_TABLE, TOK), 0)
    for m in range(HIST):
        low, high = split_number(row_col[:, m : m + 1] + 1)
        spot = m * MOST + rank_col[:, m : m + 1]
        put = jnp.where(lane == spot, low.astype(F32), 0.0)
        put = jnp.where(lane == spot + 64, high.astype(F32), put)
        request = request + mm((owners == owner[m : m + 1, :]).astype(BF16), put.astype(BF16))
    request = request + 256.0 * pltpu.roll(request, 64, 1)
    request = jnp.where(owners >= 0, request, 0.0)
    request = jnp.where(lax.broadcasted_iota(jnp.int32, (N_TABLE, TOK), 1) < 64, request, 0.0)
    request = request.astype(jnp.int32)
    for o in range(N_TABLE):
        req_out[o] = request[o : o + 1, :]

    def req_copy(k):
        peer = lax.rem(tab + k, 32)
        return pltpu.make_async_remote_copy(
            src_ref=req_out.at[peer], dst_ref=req_in.at[tab],
            send_sem=r_send.at[k], recv_sem=r_recv.at[k],
            device_id=(dp, peer), device_id_type=MESH,
        )

    def zigzag(n):
        return (1 - n % 2) * (n // 2 + 1) + n % 2 * (31 - n // 2)

    def ask(n, carry):
        req_copy(zigzag(n)).start()
        return carry

    lax.fori_loop(0, 31, ask, 0)
    req_in[tab] = req_out[tab]

    slot = owner * 16 + rank.astype(jnp.int32)
    first_half = lax.broadcasted_iota(jnp.int32, (1, TOK), 1) < SEQ
    for p in range(PAIRS):
        a = slot[2 * p : 2 * p + 1, :]
        b = slot[2 * p + 1 : 2 * p + 2, :] + MOST
        item = jnp.where(first_half, a, pltpu.roll(b, SEQ, 1))
        action = jnp.where(first_half, pltpu.roll(a, SEQ, 1), b)
        length = jnp.where(first_half, lengths[2 * p : 2 * p + 1], lengths[2 * p + 1 : 2 * p + 2])
        block = jnp.concatenate([item, action, length, length] * 2, axis=0)
        rows_s[p] = block
        cols_s[p] = block.astype(F32).T.astype(jnp.int32)

    def asked(k, carry):
        req_copy(k).wait_recv()
        return carry

    lax.fori_loop(1, 32, asked, 0)
    asks = jnp.concatenate([req_in[k] for k in range(N_TABLE)], axis=0)
    low, high = split_number(asks)
    tall = lax.broadcasted_iota(jnp.int32, (SLOTS, N_TABLE), 0) // 16
    tall = (tall == lax.broadcasted_iota(jnp.int32, (SLOTS, N_TABLE), 1)).astype(BF16)
    wanted[...] = mm(tall, low) + 256.0 * mm(tall, high) - 1.0
    wide = lax.broadcasted_iota(jnp.int32, (N_TABLE, SLOTS), 1) // 16
    wide = (wide == lax.broadcasted_iota(jnp.int32, (N_TABLE, SLOTS), 0)).astype(BF16)
    across = mm_tn(low, wide) + 256.0 * mm_tn(high, wide) - 1.0
    at = lax.broadcasted_iota(jnp.int32, (TOK, SLOTS), 0)
    in_owner = lax.broadcasted_iota(jnp.int32, (TOK, SLOTS), 1) % 16
    for p in range(PAIRS):
        line = jnp.sum(jnp.where(at == in_owner + 16 * p, across, 0.0), axis=0, keepdims=True)
        req_rows[:, p * SLOTS : (p + 1) * SLOTS] = line.astype(jnp.int32)

    def fetch_copy(p, k):
        peer = lax.rem(tab + k, 32)
        return pltpu.make_async_remote_copy(
            src_ref=picked.at[p, peer], dst_ref=replies.at[p, tab],
            send_sem=f_send.at[p, k], recv_sem=f_recv.at[p, k],
            device_id=(dp, peer), device_id_type=MESH,
        )

    loads[0].wait()

    def serve(p, carry):
        at = lax.broadcasted_iota(jnp.int32, (SLOTS, TOK), 0) % 16 + 16 * p
        seen = lax.broadcasted_iota(jnp.int32, (SLOTS, TOK), 1) == at
        line = jnp.sum(jnp.where(seen, wanted[...], 0.0), axis=1, keepdims=True)
        line = line.astype(jnp.int32)
        places = lax.broadcasted_iota(jnp.int32, (SLOTS, ROWS_DEV), 1)
        chosen = (places == line).astype(BF16)
        picked[p] = mm(chosen, table[...]).astype(BF16).reshape(N_TABLE, 16, EMB)

        def start(n, inner):
            fetch_copy(p, zigzag(n)).start()
            return inner

        lax.fori_loop(0, 31, start, 0)
        replies[p, tab] = picked[p, tab]
        return carry

    lax.fori_loop(0, PAIRS, serve, 0)

    outgoing = picked

    def give_copy(last, k):
        peer = lax.rem(tab + k, 32)
        pairs = pl.ds(PAIRS - 1, 1) if last else pl.ds(0, PAIRS - 1)
        return pltpu.make_async_remote_copy(
            src_ref=outgoing.at[pairs, peer], dst_ref=incoming.at[pairs, tab],
            send_sem=a_send.at[last, k], recv_sem=a_recv.at[last, k],
            device_id=(dp, peer), device_id_type=MESH,
        )

    for load in loads[1:]:
        load.wait()

    def give(last):
        def start(n, carry):
            give_copy(last, zigzag(n)).start()
            return carry

        lax.fori_loop(0, 31, start, 0)

    def fetched(p):
        def landed(k, carry):
            fetch_copy(p, k).wait_recv()
            fetch_copy(p, k).wait_send()
            return carry

        lax.fori_loop(1, 32, landed, 0)

    def pair(p, carry):
        fetched(p)

        @pl.when(p == PAIRS - 1)
        def _():
            give(0)

        tokens = pl.ds(pl.multiple_of(p * TOK, TOK), TOK)
        normed_p, mixed_p, top_p, before_p, back = layer_pair(
            replies[p].reshape(SLOTS, EMB), cols_s[p], rows_s[p], up[tokens, :], wp, wo
        )
        outgoing[p] = back.reshape(N_TABLE, 16, EMB)
        incoming[p, tab] = outgoing[p, tab]
        normed_t[:, tokens] = normed_p
        mixed_t[:, tokens] = mixed_p
        up[tokens, :] = top_p
        gbs[tokens, :] = before_p
        return carry

    lax.fori_loop(0, PAIRS, pair, 0)

    def core_copy(k):
        return pltpu.make_async_remote_copy(
            src_ref=g.at[0, k], dst_ref=core_buf.at[k],
            send_sem=core_send.at[k], recv_sem=core_recv.at[k],
            device_id=other, device_id_type=MESH,
        )

    s1 = g.at[1]
    t2 = g.at[0]

    def merge(k):
        core_copy(k).wait_recv()
        core_copy(k).wait_send()

        def step(n, inner):
            s1[k, n] = (s1[k, n].astype(F32) + core_buf[k, n].astype(F32)).astype(BF16)
            return inner

        lax.fori_loop(0, 4, step, 0)

    def two(ref, n):
        return ref.at[pl.ds(2 * n, 2)]

    def add_flat(target, other_ref):
        target[...] = (target[...].astype(F32) + other_ref[...].astype(F32)).astype(BF16)

    def chosen_rows(slots, first, count):
        asked_row = req_rows[:, slots]
        places = lax.broadcasted_iota(jnp.int32, (count, asked_row.shape[1]), 0) + first
        return (places == asked_row).astype(BF16)

    def take_in(last):
        def given(k, carry):
            give_copy(last, k).wait_recv()
            return carry

        lax.fori_loop(1, 32, given, 0)

    early = (PAIRS - 1) * SLOTS

    def add_rows():
        take_in(0)

        def block(b, carry):
            rows = pl.ds(pl.multiple_of(b * 256, 256), 256)
            rows_in = incoming[0 : PAIRS - 1].reshape(early, EMB)
            sums[rows, :] = mm(chosen_rows(slice(0, early), b * 256, 256), rows_in)
            return carry

        lax.fori_loop(0, 8, block, 0)

    fars, nears, partials = (far_1, far_2, far_3), (near_1, near_2, near_3), (sum_1, sum_2, sum_3)
    last_fars = (last_far_1, last_far_2, last_far_3)
    last_nears = (last_near_1, last_near_2, last_near_3)

    def ring_on(over_y, chunk, half, far, near, number):
        place, right, left = (y, y_right, y_left) if over_y else (x, x_right, x_left)
        ring = Ring(place, right, left, chunk, half, far, near,
                    ring_send.at[number], ring_recv.at[number])
        ring.make()
        return ring

    def first_chunk(n):
        first, count, over_y = STREAMS[n]
        if over_y:
            return lambda k: s1.at[k, :, pl.ds(first, count), :]
        return lambda k: s1.at[:, k, pl.ds(first, count), :]

    def half_rows(count):
        return lambda ref, n: ref.at[pl.ds(count // 2 * n, count // 2), :]

    firsts = [
        ring_on(STREAMS[n][2], first_chunk(n), two, fars[n], nears[n], n) for n in range(3)
    ]
    seconds = [
        ring_on(not STREAMS[n][2], lambda k, n=n: partials[n].at[k], half_rows(STREAMS[n][1]),
                last_fars[n], last_nears[n], 3 + n)
        for n in range(3)
    ]

    def turn(n):
        first, count, over_y = STREAMS[n]
        firsts[n].arrive()
        for m in range(4):
            own = s1[y, m, first : first + count, :] if over_y else s1[m, x, first : first + count, :]
            total = own.astype(F32) + nears[n][0, m].astype(F32) + nears[n][1, m].astype(F32)
            partials[n][m] = total.astype(BF16)
        seconds[n].start()

    def z_copy(target, source):
        return pltpu.make_async_remote_copy(
            src_ref=s4.at[target], dst_ref=zbuf.at[source],
            send_sem=z_send.at[target], recv_sem=z_recv.at[source],
            device_id=(dp, 8 * x + target), device_id_type=MESH,
        )

    def leave(n):
        first, count, over_y = STREAMS[n]
        seconds[n].arrive()
        place = x if over_y else y
        total = partials[n][place].astype(F32) + last_nears[n][0].astype(F32)
        total = (total + last_nears[n][1].astype(F32)).astype(BF16)
        s4[first // 32 : (first + count) // 32] = total.reshape(count // 32, 32, 512)
        for target in range(first // 32, (first + count) // 32):

            @pl.when(z != target)
            def _():
                z_copy(target, z).start()

    def chunk_at(n):
        return lax.rem(y + 2 + n + (n // 2) * (1 - 2 * (n % 2)), 4)

    def terms(n, carry):
        k = chunk_at(n)
        first = mm(normed_t[...], gbs[:, pl.ds(pl.multiple_of(k * 768, 768), 768)]) * SCALE
        second = mm(mixed_t[...], up[:, pl.ds(pl.multiple_of(k * 256, 256), 256)]) * SCALE
        for which, kept in ((0, 1 - c), (1, c)):
            one = first[:, which * 384 : (which + 1) * 384].astype(BF16)
            two_ = second[:, which * 128 : (which + 1) * 128].astype(BF16)
            g[kept, k, :, :, 0:384] = one.reshape(4, 256, 384)
            g[kept, k, :, :, 384:512] = two_.reshape(4, 256, 128)
        core_copy(k).start()

        @pl.when(n > 0)
        def _():
            merge(chunk_at(n - 1))

        @pl.when(n == 1)
        def _():
            firsts[0].copies[0].start()
            firsts[0].copies[1].start()

        @pl.when(n == 2)
        def _():
            firsts[0].copies[3].start()

        @pl.when(n == 3)
        def _():
            firsts[0].copies[2].start()

        return carry

    lax.fori_loop(0, 4, terms, 0)
    merge(y)
    firsts[2].start()
    firsts[1].copies[0].start()
    firsts[1].copies[1].start()
    give(1)
    firsts[0].forward(add_into)
    firsts[1].copies[2].start()
    firsts[1].copies[3].start()
    turn(0)
    firsts[1].forward(add_into)
    firsts[2].forward(add_into)
    seconds[0].forward(add_flat)
    add_rows()
    turn(1)
    turn(2)
    leave(0)
    seconds[1].forward(add_flat)
    seconds[2].forward(add_flat)

    take_in(1)

    def rows_of(first):
        part = mm(chosen_rows(slice(early, early + SLOTS), first, 256), incoming[PAIRS - 1].reshape(SLOTS, EMB))
        rows = pl.ds(pl.multiple_of(first, 256), 256)
        return (sums[rows, :] + part).astype(BF16).astype(F32)

    def t_copy(b):
        lanes = pl.ds(pl.multiple_of(b * 128, 128), 128)
        return pltpu.make_async_remote_copy(
            src_ref=t2.at[1 - c, :, :, lanes], dst_ref=t_core.at[:, :, lanes],
            send_sem=core_send.at[4 + b], recv_sem=core_recv.at[4 + b],
            device_id=other, device_id_type=MESH,
        )

    def table_block(b, carry):
        upper = rows_of(b * 256)
        lower = rows_of(b * 256 + 1024)
        lanes = pl.ds(pl.multiple_of(b * 128, 128), 128)
        is_left = lax.broadcasted_iota(jnp.int32, (256, 128), 1) < 64
        for k in range(4):
            up_k, low_k = upper[:, k * 128 : (k + 1) * 128], lower[:, k * 128 : (k + 1) * 128]
            t2[0, k, :, lanes] = jnp.where(is_left, up_k, pltpu.roll(low_k, 64, 1)).astype(BF16)
            t2[1, k, :, lanes] = jnp.where(is_left, pltpu.roll(up_k, 64, 1), low_k).astype(BF16)
        t_copy(b).start()
        return carry

    def table_merge(b, carry):
        t_copy(b).wait_recv()
        lanes = pl.ds(pl.multiple_of(b * 128, 128), 128)
        for k in range(4):
            mine = t2[c, k, :, lanes].astype(F32) + t_core[k, :, lanes].astype(F32)
            t2[c, k, :, lanes] = mine.astype(BF16)
        return carry

    ring_t = Ring(y, y_right, y_left, lambda k: t2.at[c, k],
                  lambda ref, n: ref.at[:, pl.ds(256 * n, 256)], t_far, t_near,
                  ring_send.at[6], ring_recv.at[6])
    ring_t.make()
    lax.fori_loop(0, 3, table_block, 0)
    lax.fori_loop(0, 2, table_merge, 0)
    ring_t.start_half(0)
    lax.fori_loop(3, 4, table_block, 0)
    lax.fori_loop(2, 4, table_merge, 0)
    ring_t.start_half(1)
    leave(1)
    leave(2)

    ring_t.forward(add_flat)

    def sent(k, carry):
        req_copy(k).wait_send()
        give_copy(0, k).wait_send()
        give_copy(1, k).wait_send()
        return carry

    lax.fori_loop(1, 32, sent, 0)
    total = s4[z].astype(F32)
    for k in range(1, 8):
        source = lax.rem(z + k, 8)
        z_copy(z, source).wait_recv()
        total = total + zbuf[source].astype(F32)
    dense_ref[...] = total.astype(BF16)
    ring_t.arrive()
    total = t2[c, y].astype(F32) + t_near[0].astype(F32) + t_near[1].astype(F32)
    table_ref[...] = total.astype(BF16)

    for k in range(4):
        t_copy(k).wait_send()
    for k in range(1, 8):
        msg_copy(k).wait_send()
        z_copy(lax.rem(z + k, 8), z).wait_send()
    for ring in (*firsts, *seconds, ring_t):
        ring.end()


def output_kernel(dense_ref, sums_ref, proj_ref, outw_ref, table_ref):
    proj_ref[...] = dense_ref[:, :384]
    outw_ref[...] = dense_ref[:, 384:]
    across = sums_ref[...].astype(F32).T.astype(BF16)
    for b in range(4):
        for half in range(2):
            part = across[b * 128 + half * 64 : b * 128 + half * 64 + 64]
            table_ref[:, half * 1024 + b * 256 : half * 1024 + (b + 1) * 256] = part


def run(*arrays):
    whole = pl.BlockSpec(memory_space=pltpu.VMEM)
    anywhere = pl.BlockSpec(memory_space=pl.ANY)
    dma = pltpu.SemaphoreType.DMA
    tokens = HIST * SEQ

    def buf(*shape):
        return pltpu.VMEM(shape, BF16)

    parts = pl.pallas_call(
        program_kernel,
        out_shape=(
            jax.ShapeDtypeStruct((32, 512), BF16),
            jax.ShapeDtypeStruct((256, 512), BF16),
        ),
        in_specs=[whole] * 4 + [anywhere] * 4,
        out_specs=(whole,) * 2,
        scratch_shapes=[
            buf(ROWS_DEV, EMB), buf(tokens, D), buf(D, PROJ), buf(D, D),
            pltpu.VMEM((HIST, 8, TOK), jnp.int32),
            pltpu.VMEM((HIST, 8, TOK), jnp.int32),
            pltpu.VMEM((N_TABLE, 1, TOK), jnp.int32),
            pltpu.VMEM((N_TABLE, 1, TOK), jnp.int32),
            pltpu.VMEM((SLOTS, TOK), F32),
            pltpu.VMEM((1, PAIRS * SLOTS), jnp.int32),
            pltpu.VMEM((PAIRS, 8, TOK), jnp.int32),
            pltpu.VMEM((PAIRS, TOK, 8), jnp.int32),
            buf(PAIRS, N_TABLE, 16, EMB), buf(PAIRS, N_TABLE, 16, EMB),
            buf(PAIRS, N_TABLE, 16, EMB),
            buf(D, tokens), buf(D, tokens), buf(tokens, PROJ),
            buf(2, 4, 4, 256, 512), buf(4, 4, 256, 512), pltpu.VMEM((ROWS_DEV, EMB), F32),
            *[buf(2, 2, n, 512) for _, n, _ in STREAMS],
            *[buf(2, 4, n, 512) for _, n, _ in STREAMS],
            *[buf(4, n, 512) for _, n, _ in STREAMS],
            *[buf(2, n // 2, 512) for _, n, _ in STREAMS],
            *[buf(2, n, 512) for _, n, _ in STREAMS],
            buf(8, 32, 512), buf(8, 32, 512),
            buf(4, 256, 512), buf(2, 256, 256), buf(2, 256, 512),
            dma((4,)), dma((8,)), dma((8,)), dma((32,)), dma((32,)),
            dma((PAIRS, 32)), dma((PAIRS, 32)), dma((2, 32)), dma((2, 32)),
            dma((8,)), dma((8,)), dma((7, 6)), dma((7, 6)), dma((8,)), dma((8,)),
        ],
        compiler_params=pltpu.CompilerParams(
            vmem_limit_bytes=VMEM_LIMIT, collective_id=0, has_side_effects=True
        ),
        name="whole_program",
    )(*arrays)
    return pl.pallas_call(
        output_kernel,
        out_shape=(
            jax.ShapeDtypeStruct((32, 384), BF16),
            jax.ShapeDtypeStruct((32, 128), BF16),
            jax.ShapeDtypeStruct((64, 2048), BF16),
        ),
        in_specs=[whole] * 2,
        out_specs=(whole,) * 3,
        name="outputs",
    )(*parts)


def body(
    embed_table, owner_shard, slot_row, lengths, send_order, proj_weight, out_weight, upstream
):
    proj, outw, table = run(
        jnp.swapaxes(owner_shard[..., 0], 1, 2), jnp.swapaxes(slot_row, 1, 2),
        lengths.reshape(1, HIST), send_order, embed_table, upstream.reshape(HIST * SEQ, D),
        proj_weight, out_weight,
    )
    return table.T, proj, outw


def solution(mesh):
    in_specs = (
        P("table", None),
        P(("dp", "table"), None, None, None),
        P(("dp", "table"), None, None),
        P(("dp", "table")),
        P(("dp", "table"), None),
        P(),
        P(),
        P(("dp", "table"), None, None),
    )
    out_specs = (P("table", "dp"), P("table", "dp"), P("table", "dp"))
    return jax.shard_map(body, mesh=mesh, in_specs=in_specs, out_specs=out_specs, check_vma=False)
```

```python
import functools

import jax
import jax.numpy as jnp
from jax import lax
from jax.experimental import pallas as pl
from jax.experimental.pallas import tpu as pltpu
from jax.sharding import PartitionSpec as P

D = 1024
EMB = 512
HEADS = 8
QK = 64
PROJ = 3072
SEQ = 64
HIST = 8
ROWS_DEV = 2048
MOST = 8
N_DP = 8
N_TABLE = 32
PAIRS = HIST // 2
TOK = 2 * SEQ
SLOTS = 2 * N_TABLE * MOST
EPSILON = 1e-06
SCALE = float(2048 * 64) ** (-0.5)
MESH = pl.DeviceIdType.MESH
VMEM_LIMIT = 60 * 1024 * 1024
STREAMS = ((0, 96, True), (96, 96, True), (192, 64, False))
F32 = jnp.float32
BF16 = jnp.bfloat16


def mm(a, b):
    return lax.dot_general(a, b, (((1,), (0,)), ((), ())), preferred_element_type=F32)


def mm_nt(a, b):
    return lax.dot_general(a, b, (((1,), (1,)), ((), ())), preferred_element_type=F32)


def mm_tn(a, b):
    return lax.dot_general(a, b, (((0,), (0,)), ((), ())), preferred_element_type=F32)


def sigmoid(x):
    return 0.5 * jnp.tanh(0.5 * x) + 0.5


class Ring:
    def __init__(self, place, to_right, to_left, chunk, half, far, near, send, recv):
        self.place, self.right, self.left = place, to_right, to_left
        self.chunk, self.half, self.far, self.near = chunk, half, far, near
        self.send, self.recv = send, recv

    def copy(self, number, src, dst, device):
        return pltpu.make_async_remote_copy(
            src_ref=src, dst_ref=dst, send_sem=self.send.at[number], recv_sem=self.recv.at[number],
            device_id=device, device_id_type=MESH,
        )

    def make(self):
        across, after, ahead = (lax.rem(self.place + k, 4) for k in (2, 1, 3))
        self.after, self.ahead = after, ahead
        part, half, far, near = self.chunk, self.half, self.far, self.near
        self.copies = [
            self.copy(0, half(part(across), 0), far.at[0], self.right),
            self.copy(1, half(part(across), 1), far.at[1], self.left),
            self.copy(2, half(part(after), 1), half(near.at[0], 1), self.right),
            self.copy(3, half(part(ahead), 0), half(near.at[1], 0), self.left),
            self.copy(4, half(part(after), 0), half(near.at[0], 0), self.right),
            self.copy(5, half(part(ahead), 1), half(near.at[1], 1), self.left),
        ]

    def start_half(self, number):
        for k in ((0, 3), (1, 2))[number]:
            self.copies[k].start()

    def start(self):
        self.start_half(0)
        self.start_half(1)

    def forward(self, add):
        self.copies[0].wait_recv()
        add(self.half(self.chunk(self.after), 0), self.far.at[0])
        self.copies[4].start()
        self.copies[1].wait_recv()
        add(self.half(self.chunk(self.ahead), 1), self.far.at[1])
        self.copies[5].start()

    def arrive(self):
        for k in range(2, 6):
            self.copies[k].wait_recv()

    def end(self):
        for k in range(6):
            self.copies[k].wait_send()


def add_into(target, other):
    for n in range(target.shape[0]):
        target[n] = (target[n].astype(F32) + other[n].astype(F32)).astype(BF16)


def layer_pair(replies, cols, rows, upstream, wp, wo):
    item_at, action_at, length = cols[:, 0:1], cols[:, 1:2], cols[:, 2:3]
    places = lax.broadcasted_iota(jnp.int32, (TOK, SLOTS), 1)
    left = mm((places == item_at).astype(BF16), replies)
    right = mm((places == action_at).astype(BF16), replies)
    fetched = jnp.concatenate([left, right], axis=1)
    average = jnp.mean(fetched, axis=1, keepdims=True)
    centred = fetched - average
    rstd = lax.rsqrt(jnp.mean(centred * centred, axis=1, keepdims=True) + EPSILON)
    normed_full = centred * rstd
    normed = normed_full.astype(BF16)

    before = mm(normed, wp[...])
    gate = sigmoid(before)
    slope = gate * (1.0 + before * (1.0 - gate))
    projected = (before * gate).astype(BF16)
    u = projected[:, :D].astype(F32)
    values = projected[:, D : 2 * D]
    queries = projected[:, 2 * D : 2 * D + HEADS * QK]
    keys = projected[:, 2 * D + HEADS * QK :]

    at = lax.broadcasted_iota(jnp.int32, (TOK, TOK), 0)
    source = lax.broadcasted_iota(jnp.int32, (TOK, TOK), 1)
    seen = (source <= at) & ((at // SEQ) == (source // SEQ))
    share = jnp.where(seen, 1.0 / length.astype(F32), 0.0)
    parts = (source < QK, source >= QK)
    zero = jnp.zeros((TOK, TOK), BF16)

    weights, factors, attended = [], [], []
    for h in range(HEADS):
        two = slice((h // 2) * TOK, (h // 2 + 1) * TOK)
        key = jnp.where(parts[h % 2], keys[:, two], zero)
        score = mm_nt(queries[:, two], key)
        open_ = sigmoid(score)
        weight = (score * open_ * share).astype(BF16)
        weights.append(weight)
        factors.append(open_ * (1.0 + score * (1.0 - open_)) * share)
        attended.append(mm(weight, values[:, h * TOK : (h + 1) * TOK]))
    attended = jnp.concatenate(attended, axis=1)
    average = jnp.mean(attended, axis=1, keepdims=True)
    centred = attended - average
    spread = lax.rsqrt(jnp.mean(centred * centred, axis=1, keepdims=True) + EPSILON)
    inner = centred * spread
    mixed = inner * u

    place = lax.broadcasted_iota(jnp.int32, (TOK, D), 0) % SEQ
    top = jnp.where(place < length, upstream.astype(F32), 0.0)
    top_low = top.astype(BF16)
    grad_mixed = mm_nt(top_low, wo[...]).astype(BF16).astype(F32)
    grad_u = (grad_mixed * inner).astype(BF16)
    grad_inner = grad_mixed * u
    first = jnp.mean(grad_inner, axis=1, keepdims=True)
    second = jnp.mean(grad_inner * inner, axis=1, keepdims=True)
    grad_att = (spread * (grad_inner - first - inner * second)).astype(BF16)

    grad_v, grad_q, grad_k = [], [], []
    for h in range(HEADS):
        own = slice(h * TOK, (h + 1) * TOK)
        two = slice((h // 2) * TOK, (h // 2 + 1) * TOK)
        grad_weight = mm_nt(grad_att[:, own], values[:, own]).astype(BF16).astype(F32)
        grad_v.append(mm_tn(weights[h], grad_att[:, own]).astype(BF16))
        grad_score = (grad_weight * factors[h]).astype(BF16)
        key = jnp.where(parts[h % 2], keys[:, two], zero)
        query = jnp.where(parts[h % 2], queries[:, two], zero)
        gq = mm(grad_score, key)
        gk = mm_tn(grad_score, query)
        if h % 2:
            grad_q[-1] = (grad_q[-1] + gq).astype(BF16)
            grad_k[-1] = (grad_k[-1] + gk).astype(BF16)
        else:
            grad_q.append(gq)
            grad_k.append(gk)
    grad_projected = jnp.concatenate([grad_u] + grad_v + grad_q + grad_k, axis=1)
    grad_before = (grad_projected.astype(F32) * slope).astype(BF16)
    grad_normed = mm_nt(grad_before, wp[...])
    first = jnp.mean(grad_normed, axis=1, keepdims=True)
    second = jnp.mean(grad_normed * normed_full, axis=1, keepdims=True)
    grad_rows = (top + rstd * (grad_normed - first - normed_full * second)).astype(BF16)

    slots = lax.broadcasted_iota(jnp.int32, (SLOTS, TOK), 0)
    back = mm((slots == rows[0:1, :]).astype(BF16), grad_rows[:, :EMB])
    back = back + mm((slots == rows[1:2, :]).astype(BF16), grad_rows[:, EMB:])
    return normed_full.T.astype(BF16), mixed.T.astype(BF16), top_low, grad_before, back.astype(BF16)


def split_number(numbers):
    high = numbers // 256
    return (numbers - 256 * high).astype(BF16), high.astype(BF16)


def program_kernel(
    owner_ref, slot_ref, length_ref, order_ref, table_hbm, up_hbm, wp_hbm, wo_hbm,
    dense_ref, table_ref,
    table, up, wp, wo, msg_out, msg_in, req_out, req_in, wanted, req_rows, rows_s, cols_s,
    picked, replies, incoming, normed_t, mixed_t, gbs,
    g, core_buf, sums, far_1, far_2, far_3, near_1, near_2, near_3, sum_1, sum_2, sum_3,
    last_far_1, last_far_2, last_far_3, last_near_1, last_near_2, last_near_3,
    s4, zbuf, t_core, t_far, t_near,
    load_sem, m_send, m_recv, r_send, r_recv, f_send, f_recv, a_send, a_recv,
    core_send, core_recv, ring_send, ring_recv, z_send, z_recv,
):
    dp = lax.axis_index("dp")
    tab = lax.axis_index("table")
    y, c = dp // 2, dp % 2
    x, z = tab // 8, tab % 8
    other = (2 * y + 1 - c, tab)
    y_right = (2 * lax.rem(y + 1, 4) + c, tab)
    y_left = (2 * lax.rem(y + 3, 4) + c, tab)
    x_right = (dp, lax.rem(tab + 8, 32))
    x_left = (dp, lax.rem(tab + 24, 32))

    loads = [
        pltpu.make_async_copy(src, dst, load_sem.at[n])
        for n, (src, dst) in enumerate(
            ((table_hbm, table), (up_hbm, up), (wp_hbm, wp), (wo_hbm, wo))
        )
    ]
    for load in loads:
        load.start()

    barrier = pltpu.get_barrier_semaphore()

    def greet_dp(k, carry):
        pl.semaphore_signal(
            barrier, inc=1, device_id=(lax.rem(dp + k, 8), tab), device_id_type=MESH
        )
        return carry

    def greet_table(k, carry):
        pl.semaphore_signal(
            barrier, inc=1, device_id=(dp, lax.rem(tab + k, 32)), device_id_type=MESH
        )
        return carry

    lax.fori_loop(1, 8, greet_dp, 0)
    lax.fori_loop(1, 32, greet_table, 0)

    order = order_ref[...]
    rows_of_table = [owner_ref[m] * ROWS_DEV + slot_ref[m] for m in range(HIST)]
    for k in range(HIST):
        at = order[:, k : k + 1]
        lookups = jnp.zeros((2, SEQ), jnp.int32)
        length = jnp.zeros((1, 1), jnp.int32)
        for m in range(HIST):
            lookups = jnp.where(jnp.broadcast_to(at, (2, SEQ)) == m, rows_of_table[m], lookups)
            length = jnp.where(at == m, length_ref[:, m : m + 1], length)
        msg_out[k, 0:2, 0:SEQ] = lookups
        msg_out[k, 2:3, 0:SEQ] = jnp.broadcast_to(length, (1, SEQ))
    pl.semaphore_wait(barrier, 38)

    def msg_copy(k):
        peer = lax.rem(dp + k, 8)
        return pltpu.make_async_remote_copy(
            src_ref=msg_out.at[peer], dst_ref=msg_in.at[dp],
            send_sem=m_send.at[k], recv_sem=m_recv.at[k],
            device_id=(peer, tab), device_id_type=MESH,
        )

    for k in range(1, 8):
        msg_copy(k).start()
    msg_in[dp] = msg_out[dp]
    for k in range(1, 8):
        msg_copy(k).wait_recv()

    items = jnp.concatenate([msg_in[k, 0:1, :] for k in range(HIST)], axis=0)
    actions = jnp.concatenate([msg_in[k, 1:2, :] for k in range(HIST)], axis=0)
    lengths = jnp.concatenate([msg_in[k, 2:3, :] for k in range(HIST)], axis=0)[:, 0:1]
    is_item = lax.broadcasted_iota(jnp.int32, (HIST, TOK), 1) < SEQ
    ids = jnp.where(is_item, items, pltpu.roll(actions, SEQ, 1))
    owner = ids // ROWS_DEV
    ids_col = ids.astype(F32).T.astype(jnp.int32)
    owner_col, row_col = ids_col // ROWS_DEV, ids_col % ROWS_DEV
    sub = lax.broadcasted_iota(jnp.int32, (TOK, TOK), 0)
    lane = lax.broadcasted_iota(jnp.int32, (TOK, TOK), 1)
    ranks = []
    for m in range(HIST):
        same = (owner_col[:, m : m + 1] == owner[m : m + 1, :]) & (sub < lane)
        ranks.append(jnp.sum(jnp.where(same, 1.0, 0.0), axis=0, keepdims=True))
    rank = jnp.concatenate(ranks, axis=0)
    rank_col = rank.T.astype(jnp.int32)
    request = jnp.zeros((N_TABLE, TOK), F32)
    owners = lax.broadcasted_iota(jnp.int32, (N_TABLE, TOK), 0)
    for m in range(HIST):
        low, high = split_number(row_col[:, m : m + 1] + 1)
        spot = m * MOST + rank_col[:, m : m + 1]
        put = jnp.where(lane == spot, low.astype(F32), 0.0)
        put = jnp.where(lane == spot + 64, high.astype(F32), put)
        request = request + mm((owners == owner[m : m + 1, :]).astype(BF16), put.astype(BF16))
    request = request + 256.0 * pltpu.roll(request, 64, 1)
    request = jnp.where(owners >= 0, request, 0.0)
    request = jnp.where(lax.broadcasted_iota(jnp.int32, (N_TABLE, TOK), 1) < 64, request, 0.0)
    request = request.astype(jnp.int32)
    for o in range(N_TABLE):
        req_out[o] = request[o : o + 1, :]

    def req_copy(k):
        peer = lax.rem(tab + k, 32)
        return pltpu.make_async_remote_copy(
            src_ref=req_out.at[peer], dst_ref=req_in.at[tab],
            send_sem=r_send.at[k], recv_sem=r_recv.at[k],
            device_id=(dp, peer), device_id_type=MESH,
        )

    def ask(k, carry):
        req_copy(k).start()
        return carry

    lax.fori_loop(1, 32, ask, 0)
    req_in[tab] = req_out[tab]

    slot = owner * 16 + rank.astype(jnp.int32)
    first_half = lax.broadcasted_iota(jnp.int32, (1, TOK), 1) < SEQ
    for p in range(PAIRS):
        a = slot[2 * p : 2 * p + 1, :]
        b = slot[2 * p + 1 : 2 * p + 2, :] + MOST
        item = jnp.where(first_half, a, pltpu.roll(b, SEQ, 1))
        action = jnp.where(first_half, pltpu.roll(a, SEQ, 1), b)
        length = jnp.where(first_half, lengths[2 * p : 2 * p + 1], lengths[2 * p + 1 : 2 * p + 2])
        block = jnp.concatenate([item, action, length, length] * 2, axis=0)
        rows_s[p] = block
        cols_s[p] = block.astype(F32).T.astype(jnp.int32)

    def asked(k, carry):
        req_copy(k).wait_recv()
        return carry

    lax.fori_loop(1, 32, asked, 0)
    asks = jnp.concatenate([req_in[k] for k in range(N_TABLE)], axis=0)
    low, high = split_number(asks)
    tall = lax.broadcasted_iota(jnp.int32, (SLOTS, N_TABLE), 0) // 16
    tall = (tall == lax.broadcasted_iota(jnp.int32, (SLOTS, N_TABLE), 1)).astype(BF16)
    wanted[...] = mm(tall, low) + 256.0 * mm(tall, high) - 1.0
    wide = lax.broadcasted_iota(jnp.int32, (N_TABLE, SLOTS), 1) // 16
    wide = (wide == lax.broadcasted_iota(jnp.int32, (N_TABLE, SLOTS), 0)).astype(BF16)
    across = mm_tn(low, wide) + 256.0 * mm_tn(high, wide) - 1.0
    at = lax.broadcasted_iota(jnp.int32, (TOK, SLOTS), 0)
    in_owner = lax.broadcasted_iota(jnp.int32, (TOK, SLOTS), 1) % 16
    for p in range(PAIRS):
        line = jnp.sum(jnp.where(at == in_owner + 16 * p, across, 0.0), axis=0, keepdims=True)
        req_rows[:, p * SLOTS : (p + 1) * SLOTS] = line.astype(jnp.int32)

    def fetch_copy(p, k):
        peer = lax.rem(tab + k, 32)
        return pltpu.make_async_remote_copy(
            src_ref=picked.at[p, peer], dst_ref=replies.at[p, tab],
            send_sem=f_send.at[p, k], recv_sem=f_recv.at[p, k],
            device_id=(dp, peer), device_id_type=MESH,
        )

    loads[0].wait()

    def serve(p, carry):
        at = lax.broadcasted_iota(jnp.int32, (SLOTS, TOK), 0) % 16 + 16 * p
        seen = lax.broadcasted_iota(jnp.int32, (SLOTS, TOK), 1) == at
        line = jnp.sum(jnp.where(seen, wanted[...], 0.0), axis=1, keepdims=True)
        line = line.astype(jnp.int32)
        places = lax.broadcasted_iota(jnp.int32, (SLOTS, ROWS_DEV), 1)
        chosen = (places == line).astype(BF16)
        picked[p] = mm(chosen, table[...]).astype(BF16).reshape(N_TABLE, 16, EMB)

        def start(k, inner):
            fetch_copy(p, k).start()
            return inner

        lax.fori_loop(1, 32, start, 0)
        replies[p, tab] = picked[p, tab]
        return carry

    lax.fori_loop(0, PAIRS, serve, 0)

    outgoing = picked

    def give_copy(last, k):
        peer = 8 * lax.rem(x + k // 8, 4) + lax.rem(z + k % 8, 8)
        pairs = pl.ds(PAIRS - 1, 1) if last else pl.ds(0, PAIRS - 1)
        return pltpu.make_async_remote_copy(
            src_ref=outgoing.at[pairs, peer], dst_ref=incoming.at[pairs, tab],
            send_sem=a_send.at[last, k], recv_sem=a_recv.at[last, k],
            device_id=(dp, peer), device_id_type=MESH,
        )

    for load in loads[1:]:
        load.wait()

    def give(last):
        def start(n, carry):
            give_copy(last, 31 - n).start()
            return carry

        lax.fori_loop(0, 31, start, 0)

    def fetched(p):
        def landed(k, carry):
            fetch_copy(p, k).wait_recv()
            fetch_copy(p, k).wait_send()
            return carry

        lax.fori_loop(1, 32, landed, 0)

    def pair(p, carry):
        fetched(p)

        @pl.when(p == PAIRS - 1)
        def _():
            give(0)

        tokens = pl.ds(pl.multiple_of(p * TOK, TOK), TOK)
        normed_p, mixed_p, top_p, before_p, back = layer_pair(
            replies[p].reshape(SLOTS, EMB), cols_s[p], rows_s[p], up[tokens, :], wp, wo
        )
        outgoing[p] = back.reshape(N_TABLE, 16, EMB)
        incoming[p, tab] = outgoing[p, tab]
        normed_t[:, tokens] = normed_p
        mixed_t[:, tokens] = mixed_p
        up[tokens, :] = top_p
        gbs[tokens, :] = before_p
        return carry

    lax.fori_loop(0, PAIRS, pair, 0)

    def core_copy(k):
        return pltpu.make_async_remote_copy(
            src_ref=g.at[0, k], dst_ref=core_buf.at[k],
            send_sem=core_send.at[k], recv_sem=core_recv.at[k],
            device_id=other, device_id_type=MESH,
        )

    s1 = g.at[1]
    t2 = g.at[0]

    def merge(k):
        core_copy(k).wait_recv()
        core_copy(k).wait_send()

        def step(n, inner):
            s1[k, n] = (s1[k, n].astype(F32) + core_buf[k, n].astype(F32)).astype(BF16)
            return inner

        lax.fori_loop(0, 4, step, 0)

    def two(ref, n):
        return ref.at[pl.ds(2 * n, 2)]

    def add_flat(target, other_ref):
        target[...] = (target[...].astype(F32) + other_ref[...].astype(F32)).astype(BF16)

    def chosen_rows(slots, first, count):
        asked_row = req_rows[:, slots]
        places = lax.broadcasted_iota(jnp.int32, (count, asked_row.shape[1]), 0) + first
        return (places == asked_row).astype(BF16)

    def take_in(last):
        def given(k, carry):
            give_copy(last, k).wait_recv()
            return carry

        lax.fori_loop(1, 32, given, 0)

    early = (PAIRS - 1) * SLOTS

    def add_rows():
        take_in(0)

        def block(b, carry):
            rows = pl.ds(pl.multiple_of(b * 256, 256), 256)
            rows_in = incoming[0 : PAIRS - 1].reshape(early, EMB)
            sums[rows, :] = mm(chosen_rows(slice(0, early), b * 256, 256), rows_in)
            return carry

        lax.fori_loop(0, 8, block, 0)

    fars, nears, partials = (far_1, far_2, far_3), (near_1, near_2, near_3), (sum_1, sum_2, sum_3)
    last_fars = (last_far_1, last_far_2, last_far_3)
    last_nears = (last_near_1, last_near_2, last_near_3)

    def ring_on(over_y, chunk, half, far, near, number):
        place, right, left = (y, y_right, y_left) if over_y else (x, x_right, x_left)
        ring = Ring(place, right, left, chunk, half, far, near,
                    ring_send.at[number], ring_recv.at[number])
        ring.make()
        return ring

    def first_chunk(n):
        first, count, over_y = STREAMS[n]
        if over_y:
            return lambda k: s1.at[k, :, pl.ds(first, count), :]
        return lambda k: s1.at[:, k, pl.ds(first, count), :]

    def half_rows(count):
        return lambda ref, n: ref.at[pl.ds(count // 2 * n, count // 2), :]

    firsts = [
        ring_on(STREAMS[n][2], first_chunk(n), two, fars[n], nears[n], n) for n in range(3)
    ]
    seconds = [
        ring_on(not STREAMS[n][2], lambda k, n=n: partials[n].at[k], half_rows(STREAMS[n][1]),
                last_fars[n], last_nears[n], 3 + n)
        for n in range(3)
    ]

    def turn(n):
        first, count, over_y = STREAMS[n]
        firsts[n].arrive()
        for m in range(4):
            own = s1[y, m, first : first + count, :] if over_y else s1[m, x, first : first + count, :]
            total = own.astype(F32) + nears[n][0, m].astype(F32) + nears[n][1, m].astype(F32)
            partials[n][m] = total.astype(BF16)
        seconds[n].start()

    def z_copy(target, source):
        return pltpu.make_async_remote_copy(
            src_ref=s4.at[target], dst_ref=zbuf.at[source],
            send_sem=z_send.at[target], recv_sem=z_recv.at[source],
            device_id=(dp, 8 * x + target), device_id_type=MESH,
        )

    def leave(n):
        first, count, over_y = STREAMS[n]
        seconds[n].arrive()
        place = x if over_y else y
        total = partials[n][place].astype(F32) + last_nears[n][0].astype(F32)
        total = (total + last_nears[n][1].astype(F32)).astype(BF16)
        s4[first // 32 : (first + count) // 32] = total.reshape(count // 32, 32, 512)
        for target in range(first // 32, (first + count) // 32):

            @pl.when(z != target)
            def _():
                z_copy(target, z).start()

    def chunk_at(n):
        return lax.rem(y + 2 + n + (n // 2) * (1 - 2 * (n % 2)), 4)

    def terms(n, carry):
        k = chunk_at(n)
        first = mm(normed_t[...], gbs[:, pl.ds(pl.multiple_of(k * 768, 768), 768)]) * SCALE
        second = mm(mixed_t[...], up[:, pl.ds(pl.multiple_of(k * 256, 256), 256)]) * SCALE
        for which, kept in ((0, 1 - c), (1, c)):
            one = first[:, which * 384 : (which + 1) * 384].astype(BF16)
            two_ = second[:, which * 128 : (which + 1) * 128].astype(BF16)
            g[kept, k, :, :, 0:384] = one.reshape(4, 256, 384)
            g[kept, k, :, :, 384:512] = two_.reshape(4, 256, 128)
        core_copy(k).start()

        @pl.when(n > 0)
        def _():
            merge(chunk_at(n - 1))

        @pl.when(n == 1)
        def _():
            firsts[0].copies[0].start()
            firsts[0].copies[1].start()

        @pl.when(n == 2)
        def _():
            firsts[0].copies[3].start()

        @pl.when(n == 3)
        def _():
            firsts[0].copies[2].start()

        return carry

    lax.fori_loop(0, 4, terms, 0)
    merge(y)
    firsts[2].start()
    firsts[1].copies[0].start()
    firsts[1].copies[1].start()
    give(1)
    firsts[0].forward(add_into)
    firsts[1].copies[2].start()
    firsts[1].copies[3].start()
    turn(0)
    firsts[1].forward(add_into)
    firsts[2].forward(add_into)
    seconds[0].forward(add_flat)
    add_rows()
    turn(1)
    turn(2)
    leave(0)
    seconds[1].forward(add_flat)
    seconds[2].forward(add_flat)

    take_in(1)

    def rows_of(first):
        part = mm(chosen_rows(slice(early, early + SLOTS), first, 256), incoming[PAIRS - 1].reshape(SLOTS, EMB))
        rows = pl.ds(pl.multiple_of(first, 256), 256)
        return (sums[rows, :] + part).astype(BF16).astype(F32)

    def t_copy(b):
        lanes = pl.ds(pl.multiple_of(b * 128, 128), 128)
        return pltpu.make_async_remote_copy(
            src_ref=t2.at[1 - c, :, :, lanes], dst_ref=t_core.at[:, :, lanes],
            send_sem=core_send.at[4 + b], recv_sem=core_recv.at[4 + b],
            device_id=other, device_id_type=MESH,
        )

    def table_block(b, carry):
        upper = rows_of(b * 256)
        lower = rows_of(b * 256 + 1024)
        lanes = pl.ds(pl.multiple_of(b * 128, 128), 128)
        is_left = lax.broadcasted_iota(jnp.int32, (256, 128), 1) < 64
        for k in range(4):
            up_k, low_k = upper[:, k * 128 : (k + 1) * 128], lower[:, k * 128 : (k + 1) * 128]
            t2[0, k, :, lanes] = jnp.where(is_left, up_k, pltpu.roll(low_k, 64, 1)).astype(BF16)
            t2[1, k, :, lanes] = jnp.where(is_left, pltpu.roll(up_k, 64, 1), low_k).astype(BF16)
        t_copy(b).start()
        return carry

    def table_merge(b, carry):
        t_copy(b).wait_recv()
        lanes = pl.ds(pl.multiple_of(b * 128, 128), 128)
        for k in range(4):
            mine = t2[c, k, :, lanes].astype(F32) + t_core[k, :, lanes].astype(F32)
            t2[c, k, :, lanes] = mine.astype(BF16)
        return carry

    ring_t = Ring(y, y_right, y_left, lambda k: t2.at[c, k],
                  lambda ref, n: ref.at[:, pl.ds(256 * n, 256)], t_far, t_near,
                  ring_send.at[6], ring_recv.at[6])
    ring_t.make()
    lax.fori_loop(0, 3, table_block, 0)
    lax.fori_loop(0, 2, table_merge, 0)
    ring_t.start_half(0)
    lax.fori_loop(3, 4, table_block, 0)
    lax.fori_loop(2, 4, table_merge, 0)
    ring_t.start_half(1)
    leave(1)
    leave(2)

    ring_t.forward(add_flat)

    def sent(k, carry):
        req_copy(k).wait_send()
        give_copy(0, k).wait_send()
        give_copy(1, k).wait_send()
        return carry

    lax.fori_loop(1, 32, sent, 0)
    total = s4[z].astype(F32)
    for k in range(1, 8):
        source = lax.rem(z + k, 8)
        z_copy(z, source).wait_recv()
        total = total + zbuf[source].astype(F32)
    dense_ref[...] = total.astype(BF16)
    ring_t.arrive()
    total = t2[c, y].astype(F32) + t_near[0].astype(F32) + t_near[1].astype(F32)
    table_ref[...] = total.astype(BF16)

    for k in range(4):
        t_copy(k).wait_send()
    for k in range(1, 8):
        msg_copy(k).wait_send()
        z_copy(lax.rem(z + k, 8), z).wait_send()
    for ring in (*firsts, *seconds, ring_t):
        ring.end()


def output_kernel(dense_ref, sums_ref, proj_ref, outw_ref, table_ref):
    proj_ref[...] = dense_ref[:, :384]
    outw_ref[...] = dense_ref[:, 384:]
    across = sums_ref[...].astype(F32).T.astype(BF16)
    for b in range(4):
        for half in range(2):
            part = across[b * 128 + half * 64 : b * 128 + half * 64 + 64]
            table_ref[:, half * 1024 + b * 256 : half * 1024 + (b + 1) * 256] = part


def run(*arrays):
    whole = pl.BlockSpec(memory_space=pltpu.VMEM)
    anywhere = pl.BlockSpec(memory_space=pl.ANY)
    dma = pltpu.SemaphoreType.DMA
    tokens = HIST * SEQ

    def buf(*shape):
        return pltpu.VMEM(shape, BF16)

    parts = pl.pallas_call(
        program_kernel,
        out_shape=(
            jax.ShapeDtypeStruct((32, 512), BF16),
            jax.ShapeDtypeStruct((256, 512), BF16),
        ),
        in_specs=[whole] * 4 + [anywhere] * 4,
        out_specs=(whole,) * 2,
        scratch_shapes=[
            buf(ROWS_DEV, EMB), buf(tokens, D), buf(D, PROJ), buf(D, D),
            pltpu.VMEM((HIST, 8, TOK), jnp.int32),
            pltpu.VMEM((HIST, 8, TOK), jnp.int32),
            pltpu.VMEM((N_TABLE, 1, TOK), jnp.int32),
            pltpu.VMEM((N_TABLE, 1, TOK), jnp.int32),
            pltpu.VMEM((SLOTS, TOK), F32),
            pltpu.VMEM((1, PAIRS * SLOTS), jnp.int32),
            pltpu.VMEM((PAIRS, 8, TOK), jnp.int32),
            pltpu.VMEM((PAIRS, TOK, 8), jnp.int32),
            buf(PAIRS, N_TABLE, 16, EMB), buf(PAIRS, N_TABLE, 16, EMB),
            buf(PAIRS, N_TABLE, 16, EMB),
            buf(D, tokens), buf(D, tokens), buf(tokens, PROJ),
            buf(2, 4, 4, 256, 512), buf(4, 4, 256, 512), pltpu.VMEM((ROWS_DEV, EMB), F32),
            *[buf(2, 2, n, 512) for _, n, _ in STREAMS],
            *[buf(2, 4, n, 512) for _, n, _ in STREAMS],
            *[buf(4, n, 512) for _, n, _ in STREAMS],
            *[buf(2, n // 2, 512) for _, n, _ in STREAMS],
            *[buf(2, n, 512) for _, n, _ in STREAMS],
            buf(8, 32, 512), buf(8, 32, 512),
            buf(4, 256, 512), buf(2, 256, 256), buf(2, 256, 512),
            dma((4,)), dma((8,)), dma((8,)), dma((32,)), dma((32,)),
            dma((PAIRS, 32)), dma((PAIRS, 32)), dma((2, 32)), dma((2, 32)),
            dma((8,)), dma((8,)), dma((7, 6)), dma((7, 6)), dma((8,)), dma((8,)),
        ],
        compiler_params=pltpu.CompilerParams(
            vmem_limit_bytes=VMEM_LIMIT, collective_id=0, has_side_effects=True
        ),
        name="whole_program",
    )(*arrays)
    return pl.pallas_call(
        output_kernel,
        out_shape=(
            jax.ShapeDtypeStruct((32, 384), BF16),
            jax.ShapeDtypeStruct((32, 128), BF16),
            jax.ShapeDtypeStruct((64, 2048), BF16),
        ),
        in_specs=[whole] * 2,
        out_specs=(whole,) * 3,
        name="outputs",
    )(*parts)


def body(
    embed_table, owner_shard, slot_row, lengths, send_order, proj_weight, out_weight, upstream
):
    proj, outw, table = run(
        jnp.swapaxes(owner_shard[..., 0], 1, 2), jnp.swapaxes(slot_row, 1, 2),
        lengths.reshape(1, HIST), send_order, embed_table, upstream.reshape(HIST * SEQ, D),
        proj_weight, out_weight,
    )
    return table.T, proj, outw


def solution(mesh):
    in_specs = (
        P("table", None),
        P(("dp", "table"), None, None, None),
        P(("dp", "table"), None, None),
        P(("dp", "table")),
        P(("dp", "table"), None),
        P(),
        P(),
        P(("dp", "table"), None, None),
    )
    out_specs = (P("table", "dp"), P("table", "dp"), P("table", "dp"))
    return jax.shard_map(body, mesh=mesh, in_specs=in_specs, out_specs=out_specs, check_vma=False)
```
